128 devices in a mesh: wide: 32 (over z, x, y_hi), narrow: 4 (over y_lo, core).
Axes of the slice: x: 4, y: 4 (y_hi: 2, y_lo: 2; y = y_hi * 2 + y_lo), z: 4, core: 2. Of those that a mesh axis runs over, the one named last changes fastest.
Arguments:
- displacement: float32 [3, 3, 512, 128, 384], P(None, None, 'wide', 'narrow'), may hold values from -6 to 6
- material: int32 [512, 128, 24], P('wide', 'narrow'), may hold values 0 or 1
- level_set: float32 [384, 128, 512], P('wide', 'narrow'), may hold values from -6 to 6
Outputs:
- level_next: float32 [384, 128, 512], P('wide', 'narrow')
- speed: float32 [384, 128, 512], P('wide', 'narrow')
The draws below stay inside these ranges and needn't reach their ends.
All inputs are finite; a program needn't handle non-finite values. No bound on the sum of `material` on one device may be relied on, other than what follows from the above.
Results may differ from the reference program's by a relative error of at most 0.00002.
Values sent between devices are 32-bit elements; how exact they have to be, the bound alone decides.
No kernel may reach another device: no remote copies, remote signals or barrier semaphores. Data moves between devices by JAX's collectives and lax.ppermute only.
A program may use at most 192 MiB of HBM per device.

```python
import jax
import jax.numpy as jnp
from jax import lax

BZ = 16
EXT_PASSES = 4
HJ_STEPS = 3
NX = 512
NY = 128
NZ = 384


def set_ends(array, stream_key, smallest, high):
    extent = array.shape
    place = [jax.random.randint(jax.random.fold_in(stream_key, axis), (), 0, extent[axis]) for axis in range(len(extent))]
    array = array.at[tuple(place)].set(smallest)
    longest = extent.index(max(extent))
    place[longest] = (place[longest] + 1) % extent[longest]
    return array.at[tuple(place)].set(high)


def block_scale(rng, dims, cuts, least, high):
    loudness = 1.0
    for axis_at, blocks in cuts:
        heights = jax.random.uniform(jax.random.fold_in(jax.random.fold_in(rng, 6), axis_at), (blocks,), jnp.float32, least / len(cuts), high / len(cuts))
        loudness = loudness * jnp.repeat(jnp.exp(heights), dims[axis_at] // blocks).reshape((-1,) + (1,) * (len(dims) - 1 - axis_at))
    return loudness


def gaussian(stream_key, shape, scale, bound, cuts=(), held_as=jnp.bfloat16):
    array = jax.random.normal(stream_key, shape, jnp.float32) * scale
    if len(cuts) > 0:
        array = block_scale(stream_key, shape, cuts, -0.22, 0.18) * array
    return jnp.clip(array, min=-bound, max=bound).astype(held_as)


def setup_inputs(seed: int = 0) -> dict:
    streams_of = jax.random.split(jax.random.key(seed), 4)
    return {
        "displacement": gaussian(streams_of[0], (3, 3, NX, NY, NZ), 1.0, 6.0, ((2, 32), (3, 4)), jnp.float32),
        "material": set_ends((jax.random.randint(streams_of[1], (NX, NY, NZ // BZ), 0, 4) < 3).astype(jnp.int32), jax.random.fold_in(streams_of[1], 1), 0, 1),
        "level_set": gaussian(streams_of[2], (NZ, NY, NX), 1.0, 6.0, ((0, 32), (1, 4)), jnp.float32),
    }


SHEAR = 0.384615
LAME = 0.576923
WENO_EPS = 1e-06
TIME_STEP = 0.3
VAL_TAPS = (1.0 / 48.0, 23.0 / 48.0, 23.0 / 48.0, 1.0 / 48.0)
DER_TAPS = (-1.0 / 8.0, -5.0 / 8.0, 5.0 / 8.0, 1.0 / 8.0)

def apply_taps(padded, taps, axis, count):
    total = taps[0] * lax.slice_in_dim(padded, 1, 1 + count, axis=axis)
    for k in range(1, 4):
        total = total + taps[k] * lax.slice_in_dim(padded, 1 + k, 1 + k + count, axis=axis)
    return total

def strain_energy(grad_x, grad_y, grad_z, stiffness):
    exx = grad_x[:, 0]
    eyy = grad_y[:, 1]
    ezz = grad_z[:, 2]
    exy = 0.5 * (grad_y[:, 0] + grad_x[:, 1])
    exz = 0.5 * (grad_z[:, 0] + grad_x[:, 2])
    eyz = 0.5 * (grad_z[:, 1] + grad_y[:, 2])
    trace = exx + eyy + ezz
    square = exx * exx + eyy * eyy + ezz * ezz + 2.0 * (exy * exy + exz * exz + eyz * eyz)
    density = SHEAR * square + 0.5 * LAME * trace * trace
    return stiffness * lax.optimization_barrier(jnp.sum(density, axis=0))

def neighbour_mean(padded):
    wider = jnp.pad(padded, ((0, 0), (0, 0), (1, 1)))
    total = wider[2:, 1:-1, 1:-1] + wider[:-2, 1:-1, 1:-1]
    total = total + wider[1:-1, 2:, 1:-1] + wider[1:-1, :-2, 1:-1]
    total = total + wider[1:-1, 1:-1, 2:] + wider[1:-1, 1:-1, :-2]
    return total * (1.0 / 6.0)

def weno_side(v1, v2, v3, v4, v5):
    p_one = v1 / 3.0 - 7.0 * v2 / 6.0 + 11.0 * v3 / 6.0
    p_two = -v2 / 6.0 + 5.0 * v3 / 6.0 + v4 / 3.0
    p_three = v3 / 3.0 + 5.0 * v4 / 6.0 - v5 / 6.0
    b_one = 13.0 / 12.0 * (v1 - 2.0 * v2 + v3) ** 2 + 0.25 * (v1 - 4.0 * v2 + 3.0 * v3) ** 2
    b_two = 13.0 / 12.0 * (v2 - 2.0 * v3 + v4) ** 2 + 0.25 * (v2 - v4) ** 2
    b_three = 13.0 / 12.0 * (v3 - 2.0 * v4 + v5) ** 2 + 0.25 * (3.0 * v3 - 4.0 * v4 + v5) ** 2
    a_one = 0.1 / (WENO_EPS + b_one) ** 2
    a_two = 0.6 / (WENO_EPS + b_two) ** 2
    a_three = 0.3 / (WENO_EPS + b_three) ** 2
    return (a_one * p_one + a_two * p_two + a_three * p_three) / (a_one + a_two + a_three)

def march_step(padded, speed):
    wider = jnp.pad(padded, ((0, 0), (0, 0), (3, 3)), constant_values=1.0)
    size_z = padded.shape[0] - 6
    size_y = padded.shape[1] - 6
    size_x = padded.shape[2]
    centre = wider[3:3 + size_z, 3:3 + size_y, 3:3 + size_x]
    lines = (wider[:, 3:3 + size_y, 3:3 + size_x], wider[3:3 + size_z, :, 3:3 + size_x], wider[3:3 + size_z, 3:3 + size_y, :])
    grow_plus = None
    grow_minus = None
    for axis in range(3):
        line = lines[axis]
        count = centre.shape[axis]
        diffs = lax.slice_in_dim(line, 1, count + 6, axis=axis) - lax.slice_in_dim(line, 0, count + 5, axis=axis)
        parts = [lax.slice_in_dim(diffs, k, k + count, axis=axis) for k in range(6)]
        minus = weno_side(parts[0], parts[1], parts[2], parts[3], parts[4])
        plus = weno_side(parts[5], parts[4], parts[3], parts[2], parts[1])
        term_p = jnp.maximum(jnp.maximum(minus, 0.0) ** 2, jnp.minimum(plus, 0.0) ** 2)
        term_m = jnp.maximum(jnp.minimum(minus, 0.0) ** 2, jnp.maximum(plus, 0.0) ** 2)
        grow_plus = term_p if grow_plus is None else grow_plus + term_p
        grow_minus = term_m if grow_minus is None else grow_minus + term_m
    return centre - TIME_STEP * (jnp.maximum(speed, 0.0) * jnp.sqrt(grow_plus) + jnp.minimum(speed, 0.0) * jnp.sqrt(grow_minus))

def reference(displacement, material, level_set):
    padded = jnp.pad(displacement, ((0, 0), (0, 0), (2, 2), (2, 2), (2, 2)))
    size_x = displacement.shape[2]
    size_y = displacement.shape[3]
    size_z = displacement.shape[4]
    val_z = apply_taps(padded, VAL_TAPS, 4, size_z)
    der_z = apply_taps(padded, DER_TAPS, 4, size_z)
    vv = apply_taps(val_z, VAL_TAPS, 3, size_y)
    vd = apply_taps(val_z, DER_TAPS, 3, size_y)
    dv = apply_taps(der_z, VAL_TAPS, 3, size_y)
    grad_x = apply_taps(vv, DER_TAPS, 2, size_x)
    grad_y = apply_taps(vd, VAL_TAPS, 2, size_x)
    grad_z = apply_taps(dv, VAL_TAPS, 2, size_x)
    stiffness = 0.2 + 0.8 * jnp.repeat(material.astype(jnp.float32), BZ, axis=2)
    energy = strain_energy(grad_x, grad_y, grad_z, stiffness)
    peak = jnp.max(energy)
    velocity = jnp.transpose(energy / (peak + 1e-06) - 0.5, (2, 1, 0))
    weight = 1.0 / (1.0 + 4.0 * level_set * level_set)
    speed = velocity
    for step in range(EXT_PASSES):
        speed = weight * velocity + (1.0 - weight) * neighbour_mean(jnp.pad(speed, ((1, 1), (1, 1), (0, 0))))
    phi = level_set
    for step in range(HJ_STEPS):
        phi = march_step(jnp.pad(phi, ((3, 3), (3, 3), (0, 0)), constant_values=1.0), speed)
    return (phi, speed)
```

```python
import functools
import jax
import jax.numpy as jnp
from jax import lax
from jax.experimental import pallas as pl
from jax.experimental.pallas import tpu as pltpu
from jax.sharding import PartitionSpec as P

BZ = 16
EXT_PASSES = 4
HJ_STEPS = 3
SHEAR = 0.384615
LAME = 0.576923
WENO_EPS = 1e-06
TIME_STEP = 0.3
HALO = EXT_PASSES
GRAD_SCALE = 1.0 / (8.0 * 48.0 * 48.0)


def lane_shifts(value):
    blocks = [value[:, 128 * b : 128 * (b + 1)] for b in range(value.shape[1] // 128)]
    lane = lax.broadcasted_iota(jnp.int32, blocks[0].shape, 1)
    zero = jnp.zeros_like(blocks[0])
    outs = []
    for step in (-1, 1, 2):
        turned = [pltpu.roll(b, (-step) % 128, 1) for b in blocks]
        if step < 0:
            mask = lane < 1
            parts = [jnp.where(mask, turned[i - 1] if i > 0 else zero, turned[i]) for i in range(len(blocks))]
        else:
            mask = lane >= 128 - step
            parts = [
                jnp.where(mask, turned[i + 1] if i + 1 < len(blocks) else zero, turned[i])
                for i in range(len(blocks))
            ]
        outs.append(jnp.concatenate(parts, axis=1))
    return outs


def val4(a, b, c, d):
    return (a + d) + 23.0 * (b + c)


def der4(a, b, c, d):
    return (d - a) + 5.0 * (c - b)


def strain_kernel(last_ref, u_ref, yh_ref, xh_ref, ch_ref, stiff_ref, msg_ref, plane, filt, energy, turned):
    load = pl.program_id(0)
    own_x = u_ref.shape[2]
    rows = u_ref.shape[3]
    size_z = u_ref.shape[4]
    tiles = rows // 8
    keep = jnp.where(last_ref[0] == 1, 0.0, 1.0)

    def filter_plane(comp, layer, get_plane, low, high0, high1):
        plane[8 : 8 + rows, :] = get_plane
        plane[7:8, :] = low
        plane[8 + rows : 9 + rows, :] = high0
        plane[9 + rows : 10 + rows, :] = high1
        for tile in range(tiles):
            base = 8 + 8 * tile
            a = plane[base - 1 : base + 7, :]
            b = plane[base : base + 8, :]
            c = plane[base + 1 : base + 9, :]
            d = plane[base + 2 : base + 10, :]
            val_y = val4(a, b, c, d)
            der_y = der4(a, b, c, d)
            before, after, after2 = lane_shifts(val_y)
            span = pl.ds(8 * tile, 8)
            filt[comp, 0, layer, span, :] = val4(before, val_y, after, after2)
            filt[comp, 2, layer, span, :] = der4(before, val_y, after, after2)
            before, after, after2 = lane_shifts(der_y)
            filt[comp, 1, layer, span, :] = val4(before, der_y, after, after2)

    def own_layer(layer, carry):
        for comp in range(3):
            filter_plane(
                comp, layer, u_ref[0, comp, layer],
                yh_ref[0, comp, 0, pl.ds(layer, 1), :],
                yh_ref[0, comp, 1, pl.ds(layer, 1), :],
                yh_ref[0, comp, 2, pl.ds(layer, 1), :],
            )
        return carry

    lax.fori_loop(0, own_x, own_layer, 0)
    for k in range(3):
        for comp in range(3):
            filter_plane(
                comp, own_x + k, xh_ref[0, comp, k],
                ch_ref[0, comp, 0, k : k + 1, :],
                ch_ref[0, comp, 1, k : k + 1, :],
                ch_ref[0, comp, 2, k : k + 1, :],
            )

    def density_at(slot, masked):
        def field(comp, which, span):
            out = []
            for k in range(4):
                value = filt[comp, which, slot + k, span, :]
                if masked[k]:
                    value = value * keep
                out.append(value)
            return out

        for tile in range(tiles):
            span = pl.ds(8 * tile, 8)
            gx = [der4(*field(comp, 0, span)) for comp in range(3)]
            gy = [val4(*field(comp, 1, span)) for comp in range(3)]
            gz = [val4(*field(comp, 2, span)) for comp in range(3)]
            sxy = gy[0] + gx[1]
            sxz = gz[0] + gx[2]
            syz = gz[1] + gy[2]
            trace = gx[0] + gy[1] + gz[2]
            square = gx[0] * gx[0] + gy[1] * gy[1] + gz[2] * gz[2]
            shear = sxy * sxy + sxz * sxz + syz * syz
            scale = GRAD_SCALE * GRAD_SCALE
            density = (SHEAR * scale) * (square + 0.5 * shear) + (0.5 * LAME * scale) * (trace * trace)

            @pl.when(load == 0)
            def _():
                energy[slot, span, :] = density

            @pl.when(load > 0)
            def _():
                energy[slot, span, :] += density

    def slot_step(slot, carry):
        density_at(slot, (False,) * 4)
        return carry

    lax.fori_loop(0, own_x - 3, slot_step, 0)
    density_at(own_x - 3, (False, False, False, True))
    density_at(own_x - 2, (False, False, True, True))
    density_at(own_x - 1, (True, False, False, False))

    @pl.when(load == pl.num_programs(0) - 1)
    def _():
        peak = jnp.zeros((8, 128), jnp.float32)
        groups = own_x // 4
        zeros = jnp.zeros((8, 128), jnp.float32)
        for g in range(groups):
            stack = []
            for q in range(4):
                value = energy[4 * g + q] * stiff_ref[4 * g + q]
                stack.append(value)
                for tile in range(tiles):
                    for b in range(size_z // 128):
                        peak = jnp.maximum(peak, value[8 * tile : 8 * tile + 8, 128 * b : 128 * b + 128])
            turned[g, 0:8, :] = zeros
            turned[g, size_z : size_z + 16, :] = jnp.zeros((16, 128), jnp.float32)
            turned[g, HALO : HALO + size_z, :] = jnp.concatenate(stack, axis=0).T
        peak = jnp.broadcast_to(jnp.max(peak, axis=0, keepdims=True), (8, 128))
        peak = jnp.broadcast_to(jnp.max(peak, axis=1, keepdims=True), (8, 128))
        parts = msg_ref.shape[0] // 88
        own_z = size_z // parts
        quads = (own_z + 2 * HALO) // 4
        lane = lax.broadcasted_iota(jnp.int32, (parts, 128), 1) // rows
        for g in range(groups):
            for j in range(quads):
                picked = [turned[g, pl.ds(4 * j + k, parts, stride=own_z), :] for k in range(4)]
                for q in range(4):
                    out = None
                    for k in range(4):
                        shift = (rows * (k - q)) % 128
                        part = pltpu.roll(picked[k], shift, 1) if shift else picked[k]
                        out = part if out is None else jnp.where(lane == k, part, out)
                    msg_ref[pl.ds(16 * j + 4 * g + q, parts, stride=88), :] = out
        for t in range(parts):
            msg_ref[pl.ds(88 * t + 80, 8), :] = peak


def strain_message(last, disp, yh, xh, ch, stiff, parts):
    loads, comps, own_x, rows, size_z = disp.shape
    block = lambda *shape: pl.BlockSpec((1,) + shape, lambda l: (l,) + (0,) * len(shape))
    return pl.pallas_call(
        strain_kernel,
        grid=(loads,),
        out_shape=jax.ShapeDtypeStruct((parts * 88, 128), jnp.float32),
        in_specs=[
            pl.BlockSpec(memory_space=pltpu.SMEM),
            block(comps, own_x, rows, size_z),
            block(comps, 3, own_x, size_z),
            block(comps, 3, rows, size_z),
            block(comps, 3, 3, size_z),
            pl.BlockSpec((own_x, rows, size_z), lambda l: (0, 0, 0)),
        ],
        out_specs=pl.BlockSpec((parts * 88, 128), lambda l: (0, 0)),
        scratch_shapes=[
            pltpu.VMEM((rows + 16, size_z), jnp.float32),
            pltpu.VMEM((3, 3, own_x + 3, rows, size_z), jnp.float32),
            pltpu.VMEM((own_x, rows, size_z), jnp.float32),
            pltpu.VMEM((own_x // 4, size_z + 16, 128), jnp.float32),
        ],
        compiler_params=pltpu.CompilerParams(vmem_limit_bytes=48 * 1024 * 1024),
    )(last, disp, yh, xh, ch, stiff)


def unpack_kernel(recv_ref, tile_ref, peak_ref):
    parts = recv_ref.shape[0]
    rows = tile_ref.shape[1]
    for j in range(tile_ref.shape[0] // 4):
        block = recv_ref[:, 16 * j : 16 * j + 16, :].reshape(parts * 16, 128)
        wide = pltpu.roll(block.T, 1, 1)
        for k in range(4):
            tile_ref[4 * j + k] = wide[rows * k : rows * (k + 1), :]
    peak = recv_ref[0, 80:88, :]
    for s in range(1, parts):
        peak = jnp.maximum(peak, recv_ref[s, 80:88, :])
    peak_ref[...] = peak


def unpack(recv, own_z, rows):
    parts = recv.shape[0]
    return pl.pallas_call(
        unpack_kernel,
        out_shape=(
            jax.ShapeDtypeStruct((own_z + 2 * HALO, rows, parts * 16), jnp.float32),
            jax.ShapeDtypeStruct((8, 128), jnp.float32),
        ),
        compiler_params=pltpu.CompilerParams(vmem_limit_bytes=48 * 1024 * 1024),
    )(recv)


def ring(axis, step):
    count = lax.axis_size(axis)
    return [(i, i + step) for i in range(count) if 0 <= i + step < count]


def energy_message(displacement, material):
    wide = lax.axis_size("wide")
    backward = [(i, (i - 1) % wide) for i in range(wide)]
    xh = lax.ppermute(displacement[:, :, :3], "wide", backward)
    low = lax.ppermute(displacement[:, :, :, -1], "narrow", ring("narrow", 1))
    high = lax.ppermute(
        jnp.stack([displacement[:, :, :, 0], displacement[:, :, :, 1]], axis=2), "narrow", ring("narrow", -1)
    )
    yh = jnp.concatenate([low[:, :, None], high], axis=2)
    loads, comps, own_x, rows, size_z = displacement.shape
    blocks = material.shape[2]
    corner = yh[:, :, :, :3].reshape(loads * comps * 3, 3, size_z)
    first = material[0].astype(jnp.float32).reshape(-1)
    first = jnp.pad(first, (0, 3 * size_z - first.size)).reshape(1, 3, size_z)
    got = lax.ppermute(jnp.concatenate([corner, first], axis=0), "wide", backward)
    ch = got[: loads * comps * 3].reshape(loads, comps, 3, 3, size_z)
    beyond = got[loads * comps * 3].reshape(-1)[: rows * blocks].reshape(1, rows, blocks)
    solid = jnp.concatenate([material[1:].astype(jnp.float32), beyond], axis=0)
    stiff = 0.2 + 0.8 * jnp.repeat(solid, BZ, axis=2)
    last = (lax.axis_index("wide") == wide - 1).astype(jnp.int32).reshape(1)
    return strain_message(last, displacement, yh, xh, ch, stiff, wide)


def with_halo(block, sides, width):
    for axis, dim in sides:
        count = lax.axis_size(axis)
        forward = [(i, i + 1) for i in range(count - 1)]
        backward = [(target, source) for source, target in forward]
        low = lax.ppermute(
            lax.slice_in_dim(block, block.shape[dim] - width, None, axis=dim), axis, forward
        )
        high = lax.ppermute(lax.slice_in_dim(block, 0, width, axis=dim), axis, backward)
        block = jnp.concatenate([low, block, high], axis=dim)
    return block


def neighbour_mean(padded):
    wider = jnp.pad(padded, ((0, 0), (0, 0), (1, 1)))
    total = wider[2:, 1:-1, 1:-1] + wider[:-2, 1:-1, 1:-1]
    total = total + wider[1:-1, 2:, 1:-1] + wider[1:-1, :-2, 1:-1]
    total = total + wider[1:-1, 1:-1, 2:] + wider[1:-1, 1:-1, :-2]
    return total * (1.0 / 6.0)


def weno_side(v1, v2, v3, v4, v5):
    p_one = v1 / 3.0 - 7.0 * v2 / 6.0 + 11.0 * v3 / 6.0
    p_two = -v2 / 6.0 + 5.0 * v3 / 6.0 + v4 / 3.0
    p_three = v3 / 3.0 + 5.0 * v4 / 6.0 - v5 / 6.0
    b_one = 13.0 / 12.0 * (v1 - 2.0 * v2 + v3) ** 2 + 0.25 * (v1 - 4.0 * v2 + 3.0 * v3) ** 2
    b_two = 13.0 / 12.0 * (v2 - 2.0 * v3 + v4) ** 2 + 0.25 * (v2 - v4) ** 2
    b_three = 13.0 / 12.0 * (v3 - 2.0 * v4 + v5) ** 2 + 0.25 * (3.0 * v3 - 4.0 * v4 + v5) ** 2
    a_one = 0.1 / (WENO_EPS + b_one) ** 2
    a_two = 0.6 / (WENO_EPS + b_two) ** 2
    a_three = 0.3 / (WENO_EPS + b_three) ** 2
    return (a_one * p_one + a_two * p_two + a_three * p_three) / (a_one + a_two + a_three)


def march_step(padded, speed):
    wider = jnp.pad(padded, ((0, 0), (0, 0), (3, 3)), constant_values=1.0)
    size_z = padded.shape[0] - 6
    size_y = padded.shape[1] - 6
    size_x = padded.shape[2]
    centre = wider[3 : 3 + size_z, 3 : 3 + size_y, 3 : 3 + size_x]
    lines = (
        wider[:, 3 : 3 + size_y, 3 : 3 + size_x],
        wider[3 : 3 + size_z, :, 3 : 3 + size_x],
        wider[3 : 3 + size_z, 3 : 3 + size_y, :],
    )
    grow_plus = None
    grow_minus = None
    for axis in range(3):
        line = lines[axis]
        count = centre.shape[axis]
        diffs = lax.slice_in_dim(line, 1, count + 6, axis=axis) - lax.slice_in_dim(
            line, 0, count + 5, axis=axis
        )
        parts = [lax.slice_in_dim(diffs, k, k + count, axis=axis) for k in range(6)]
        minus = weno_side(parts[0], parts[1], parts[2], parts[3], parts[4])
        plus = weno_side(parts[5], parts[4], parts[3], parts[2], parts[1])
        term_p = jnp.maximum(jnp.maximum(minus, 0.0) ** 2, jnp.minimum(plus, 0.0) ** 2)
        term_m = jnp.maximum(jnp.minimum(minus, 0.0) ** 2, jnp.maximum(plus, 0.0) ** 2)
        grow_plus = term_p if grow_plus is None else grow_plus + term_p
        grow_minus = term_m if grow_minus is None else grow_minus + term_m
    return centre - TIME_STEP * (
        jnp.maximum(speed, 0.0) * jnp.sqrt(grow_plus)
        + jnp.minimum(speed, 0.0) * jnp.sqrt(grow_minus)
    )


def ghost_fill(array, margin, value):
    own_z = array.shape[0] - 2 * margin
    own_y = array.shape[1] - 2 * margin
    pos_z = lax.axis_index("wide") * own_z - margin + jnp.arange(array.shape[0], dtype=jnp.int32)
    pos_y = lax.axis_index("narrow") * own_y - margin + jnp.arange(array.shape[1], dtype=jnp.int32)
    valid_z = (pos_z >= 0) & (pos_z < own_z * lax.axis_size("wide"))
    valid_y = (pos_y >= 0) & (pos_y < own_y * lax.axis_size("narrow"))
    inside = valid_z[:, None, None] & valid_y[None, :, None]
    return jnp.where(inside, array, value)


def per_device(displacement, material, level_set):
    wide = lax.axis_size("wide")
    own_z, rows, size_x = level_set.shape
    message = energy_message(displacement, material).reshape(wide, 88, 128)
    recv = lax.all_to_all(message, "wide", split_axis=0, concat_axis=0, tiled=True)
    tile, wide_peak = unpack(recv, own_z, rows)
    peak = jnp.max(lax.all_gather(wide_peak, "narrow"))
    velocity = tile[HALO : HALO + own_z] / (peak + 1e-06) - 0.5
    weight = 1.0 / (1.0 + 4.0 * level_set * level_set)
    speed = velocity
    for step in range(EXT_PASSES):
        beside_all = with_halo(speed, (("wide", 0), ("narrow", 1)), 1)
        speed = weight * velocity + (1.0 - weight) * neighbour_mean(beside_all)
    phi = level_set
    for step in range(HJ_STEPS):
        beside_all = with_halo(phi, (("wide", 0), ("narrow", 1)), 3)
        phi = march_step(ghost_fill(beside_all, 3, 1.0), speed)
    return (phi, speed)


def solution(mesh):
    return jax.shard_map(
        per_device,
        mesh=mesh,
        in_specs=(
            P(None, None, "wide", "narrow", None),
            P("wide", "narrow", None),
            P("wide", "narrow", None),
        ),
        out_specs=(P("wide", "narrow", None), P("wide", "narrow", None)),
        check_vma=False,
    )
```

```python
import functools
import jax
import jax.numpy as jnp
from jax import lax
from jax.experimental import pallas as pl
from jax.experimental.pallas import tpu as pltpu
from jax.sharding import PartitionSpec as P

BZ = 16
EXT_PASSES = 4
HJ_STEPS = 3
SHEAR = 0.384615
LAME = 0.576923
WENO_EPS = 1e-06
TIME_STEP = 0.3
HALO = EXT_PASSES
GRAD_SCALE = 1.0 / (8.0 * 48.0 * 48.0)


def lane_shifts(value):
    blocks = [value[:, 128 * b : 128 * (b + 1)] for b in range(value.shape[1] // 128)]
    lane = lax.broadcasted_iota(jnp.int32, blocks[0].shape, 1)
    zero = jnp.zeros_like(blocks[0])
    outs = []
    for step in (-1, 1, 2):
        turned = [pltpu.roll(b, (-step) % 128, 1) for b in blocks]
        if step < 0:
            mask = lane < 1
            parts = [jnp.where(mask, turned[i - 1] if i > 0 else zero, turned[i]) for i in range(len(blocks))]
        else:
            mask = lane >= 128 - step
            parts = [
                jnp.where(mask, turned[i + 1] if i + 1 < len(blocks) else zero, turned[i])
                for i in range(len(blocks))
            ]
        outs.append(jnp.concatenate(parts, axis=1))
    return outs


def val4(a, b, c, d):
    return (a + d) + 23.0 * (b + c)


def der4(a, b, c, d):
    return (d - a) + 5.0 * (c - b)


def strain_kernel(last_ref, u_ref, yh_ref, xh_ref, ch_ref, stiff_ref, msg_ref, plane, filt, energy, turned):
    load = pl.program_id(0)
    own_x = u_ref.shape[2]
    rows = u_ref.shape[3]
    size_z = u_ref.shape[4]
    tiles = rows // 8
    keep = jnp.where(last_ref[0] == 1, 0.0, 1.0)

    def filter_plane(comp, layer, get_plane, low, high0, high1):
        plane[8 : 8 + rows, :] = get_plane
        plane[7:8, :] = low
        plane[8 + rows : 9 + rows, :] = high0
        plane[9 + rows : 10 + rows, :] = high1
        for tile in range(tiles):
            base = 8 + 8 * tile
            a = plane[base - 1 : base + 7, :]
            b = plane[base : base + 8, :]
            c = plane[base + 1 : base + 9, :]
            d = plane[base + 2 : base + 10, :]
            val_y = val4(a, b, c, d)
            der_y = der4(a, b, c, d)
            before, after, after2 = lane_shifts(val_y)
            span = pl.ds(8 * tile, 8)
            filt[comp, 0, layer, span, :] = val4(before, val_y, after, after2)
            filt[comp, 2, layer, span, :] = der4(before, val_y, after, after2)
            before, after, after2 = lane_shifts(der_y)
            filt[comp, 1, layer, span, :] = val4(before, der_y, after, after2)

    def own_layer(layer, carry):
        for comp in range(3):
            filter_plane(
                comp, layer, u_ref[0, comp, layer],
                yh_ref[0, comp, 0, pl.ds(layer, 1), :],
                yh_ref[0, comp, 1, pl.ds(layer, 1), :],
                yh_ref[0, comp, 2, pl.ds(layer, 1), :],
            )
        return carry

    lax.fori_loop(0, own_x, own_layer, 0)
    for k in range(3):
        for comp in range(3):
            filter_plane(
                comp, own_x + k, xh_ref[0, comp, k],
                ch_ref[0, comp, 0, k : k + 1, :],
                ch_ref[0, comp, 1, k : k + 1, :],
                ch_ref[0, comp, 2, k : k + 1, :],
            )

    def density_at(slot, masked):
        def field(comp, which, span):
            out = []
            for k in range(4):
                value = filt[comp, which, slot + k, span, :]
                if masked[k]:
                    value = value * keep
                out.append(value)
            return out

        for tile in range(tiles):
            span = pl.ds(8 * tile, 8)
            gx = [der4(*field(comp, 0, span)) for comp in range(3)]
            gy = [val4(*field(comp, 1, span)) for comp in range(3)]
            gz = [val4(*field(comp, 2, span)) for comp in range(3)]
            sxy = gy[0] + gx[1]
            sxz = gz[0] + gx[2]
            syz = gz[1] + gy[2]
            trace = gx[0] + gy[1] + gz[2]
            square = gx[0] * gx[0] + gy[1] * gy[1] + gz[2] * gz[2]
            shear = sxy * sxy + sxz * sxz + syz * syz
            scale = GRAD_SCALE * GRAD_SCALE
            density = (SHEAR * scale) * (square + 0.5 * shear) + (0.5 * LAME * scale) * (trace * trace)

            @pl.when(load == 0)
            def _():
                energy[slot, span, :] = density

            @pl.when(load > 0)
            def _():
                energy[slot, span, :] += density

    def slot_step(slot, carry):
        density_at(slot, (False,) * 4)
        return carry

    lax.fori_loop(0, own_x - 3, slot_step, 0)
    density_at(own_x - 3, (False, False, False, True))
    density_at(own_x - 2, (False, False, True, True))
    density_at(own_x - 1, (True, False, False, False))

    @pl.when(load == pl.num_programs(0) - 1)
    def _():
        peak = jnp.zeros((8, 128), jnp.float32)
        groups = own_x // 4
        zeros = jnp.zeros((8, 128), jnp.float32)
        for g in range(groups):
            stack = []
            for q in range(4):
                value = energy[4 * g + q] * stiff_ref[4 * g + q]
                stack.append(value)
                for tile in range(tiles):
                    for b in range(size_z // 128):
                        peak = jnp.maximum(peak, value[8 * tile : 8 * tile + 8, 128 * b : 128 * b + 128])
            turned[g, 0:8, :] = zeros
            turned[g, size_z : size_z + 16, :] = jnp.zeros((16, 128), jnp.float32)
            turned[g, HALO : HALO + size_z, :] = jnp.concatenate(stack, axis=0).T
        peak = jnp.broadcast_to(jnp.max(peak, axis=0, keepdims=True), (8, 128))
        peak = jnp.broadcast_to(jnp.max(peak, axis=1, keepdims=True), (8, 128))
        parts = msg_ref.shape[0] // 88
        own_z = size_z // parts
        quads = (own_z + 2 * HALO) // 4
        lane = lax.broadcasted_iota(jnp.int32, (parts, 128), 1) // rows
        for g in range(groups):
            for j in range(quads):
                picked = [turned[g, pl.ds(4 * j + k, parts, stride=own_z), :] for k in range(4)]
                for q in range(4):
                    out = None
                    for k in range(4):
                        shift = (rows * (k - q)) % 128
                        part = pltpu.roll(picked[k], shift, 1) if shift else picked[k]
                        out = part if out is None else jnp.where(lane == k, part, out)
                    msg_ref[pl.ds(16 * j + 4 * g + q, parts, stride=88), :] = out
        for t in range(parts):
            msg_ref[pl.ds(88 * t + 80, 8), :] = peak


def strain_message(last, disp, yh, xh, ch, stiff, parts):
    loads, comps, own_x, rows, size_z = disp.shape
    block = lambda *shape: pl.BlockSpec((1,) + shape, lambda l: (l,) + (0,) * len(shape))
    return pl.pallas_call(
        strain_kernel,
        grid=(loads,),
        out_shape=jax.ShapeDtypeStruct((parts * 88, 128), jnp.float32),
        in_specs=[
            pl.BlockSpec(memory_space=pltpu.SMEM),
            block(comps, own_x, rows, size_z),
            block(comps, 3, own_x, size_z),
            block(comps, 3, rows, size_z),
            block(comps, 3, 3, size_z),
            pl.BlockSpec((own_x, rows, size_z), lambda l: (0, 0, 0)),
        ],
        out_specs=pl.BlockSpec((parts * 88, 128), lambda l: (0, 0)),
        scratch_shapes=[
            pltpu.VMEM((rows + 16, size_z), jnp.float32),
            pltpu.VMEM((3, 3, own_x + 3, rows, size_z), jnp.float32),
            pltpu.VMEM((own_x, rows, size_z), jnp.float32),
            pltpu.VMEM((own_x // 4, size_z + 16, 128), jnp.float32),
        ],
        compiler_params=pltpu.CompilerParams(vmem_limit_bytes=48 * 1024 * 1024),
    )(last, disp, yh, xh, ch, stiff)


def ring(axis, step):
    count = lax.axis_size(axis)
    return [(i, i + step) for i in range(count) if 0 <= i + step < count]


def energy_message(displacement, material):
    wide = lax.axis_size("wide")
    backward = [(i, (i - 1) % wide) for i in range(wide)]
    xh = lax.ppermute(displacement[:, :, :3], "wide", backward)
    low = lax.ppermute(displacement[:, :, :, -1], "narrow", ring("narrow", 1))
    high = lax.ppermute(
        jnp.stack([displacement[:, :, :, 0], displacement[:, :, :, 1]], axis=2), "narrow", ring("narrow", -1)
    )
    yh = jnp.concatenate([low[:, :, None], high], axis=2)
    loads, comps, own_x, rows, size_z = displacement.shape
    blocks = material.shape[2]
    corner = yh[:, :, :, :3].reshape(loads * comps * 3, 3, size_z)
    first = material[0].astype(jnp.float32).reshape(-1)
    first = jnp.pad(first, (0, 3 * size_z - first.size)).reshape(1, 3, size_z)
    got = lax.ppermute(jnp.concatenate([corner, first], axis=0), "wide", backward)
    ch = got[: loads * comps * 3].reshape(loads, comps, 3, 3, size_z)
    beyond = got[loads * comps * 3].reshape(-1)[: rows * blocks].reshape(1, rows, blocks)
    solid = jnp.concatenate([material[1:].astype(jnp.float32), beyond], axis=0)
    stiff = 0.2 + 0.8 * jnp.repeat(solid, BZ, axis=2)
    last = (lax.axis_index("wide") == wide - 1).astype(jnp.int32).reshape(1)
    return strain_message(last, displacement, yh, xh, ch, stiff, wide)


YE = 10
Y1 = 6
Y2 = 3
VMEM_LIMIT = 48 * 1024 * 1024


def newton_reciprocal(x):
    r = pl.reciprocal(x, approx=True)
    return r * (2.0 - x * r)


def weno_cell(d, e0, e1, e2, e3):
    f0 = e1 - e0
    f1 = e2 - e1
    f2 = e3 - e2
    g0 = f1 - f0
    g1 = f2 - f1
    twice1 = e1 + e1
    twice2 = e2 + e2
    third = 13.0 / 3.0
    eps = 4.0 * WENO_EPS
    pa = twice1 + f0
    pb = twice1 + f1
    pc = twice2 - f2
    a = (f0 * f0 * third + eps) + pa * pa
    b = (f1 * f1 * third + eps) + pb * pb
    c = (f2 * f2 * third + eps) + pc * pc
    a = a * a
    b = b * b * (1.0 / 6.0)
    c = c * c
    ac = a * c
    ab = a * b
    cb = c * b
    u = cb * g0
    v = ab * g1
    both = u + v
    both = both + both
    s = e1 + e2
    d6 = 6.0 * d
    minus = d6 + (s + e2) - (both + v) * newton_reciprocal(ac + cb + 3.0 * ab)
    plus = (s + e1) - d6 - (both + u) * newton_reciprocal(ac + ab + 3.0 * cb)
    return minus, plus


def godunov(minus, plus):
    high = jnp.maximum(jnp.maximum(minus, plus), 0.0)
    low = jnp.minimum(jnp.minimum(minus, plus), 0.0)
    return high * high, low * low


def x_terms(phi):
    rows, size = phi.shape
    wide = size + 128
    phi = jnp.concatenate([phi, jnp.ones((rows, 128), jnp.float32)], axis=1)
    d = pltpu.roll(phi, wide - 1, 1) - phi
    e = pltpu.roll(d, wide - 1, 1) - d
    minus, plus = weno_cell(
        d, pltpu.roll(e, 2, 1), pltpu.roll(e, 1, 1), e, pltpu.roll(e, wide - 1, 1)
    )
    return godunov(pltpu.roll(minus, 1, 1)[:, :size], plus[:, :size])


def y_cells(ref, layer, row):
    p = [ref[layer, row + k : row + k + 8, :] for k in range(6)]
    d = [p[k + 1] - p[k] for k in range(5)]
    e = [d[k + 1] - d[k] for k in range(4)]
    return weno_cell(d[2], *e)


def xy_stage(phi_ref, offset, layer0, layers, gp_ref, gm_ref, exact=False):
    rows = gp_ref.shape[1]
    tiles = rows // 8

    def layer_step(z, carry):
        cells = [y_cells(phi_ref, z + layer0, 8 * t + offset - 3) for t in range(tiles)]
        turned = [pltpu.roll(c[1], 7, 0) for c in cells]
        if exact:
            start = min(rows + offset - 3, phi_ref.shape[1] - 13)
            extra = y_cells(phi_ref, z + layer0, start)[1]
            turned.append(pltpu.roll(extra, 7 - (rows + offset - 3 - start), 0))
        else:
            turned.append(turned[-1])
        row = lax.broadcasted_iota(jnp.int32, turned[0].shape, 0)
        for t in range(tiles):
            plus = jnp.where(row == 7, turned[t + 1], turned[t])
            yp, ym = godunov(cells[t][0], plus)
            xp, xm = x_terms(phi_ref[z + layer0, 8 * t + offset : 8 * t + offset + 8, :])
            gp_ref[z, 8 * t : 8 * t + 8, :] = xp + yp
            gm_ref[z, 8 * t : 8 * t + 8, :] = xm + ym
        return carry

    lax.fori_loop(0, layers, layer_step, 0)


def z_stage(get_phi, layers, rows, lanes, finish):
    def lane_step(block, carry):
        span = pl.ds(pl.multiple_of(128 * block, 128), 128)
        for t in range(rows // 8):
            p = [get_phi(z, t, span) for z in range(-3, layers + 3)]
            d = [p[k + 1] - p[k] for k in range(len(p) - 1)]
            e = [d[k + 1] - d[k] for k in range(len(d) - 1)]
            before = None
            for cell in range(layers + 1):
                minus, plus = weno_cell(d[cell + 2], e[cell], e[cell + 1], e[cell + 2], e[cell + 3])
                if before is not None:
                    finish(cell - 1, t, span, *godunov(before, plus))
                before = minus
        return carry

    lax.fori_loop(0, lanes // 128, lane_step, 0)


def first_gradient_kernel(ls_ref, sp_ref, sm_ref):
    layers, rows, lanes = sp_ref.shape
    offset = YE - Y1
    xy_stage(ls_ref, offset, 3, layers, sp_ref, sm_ref)

    def finish(z, t, span, gp, gm):
        where = pl.ds(8 * t, 8)
        scale = TIME_STEP / 6.0
        sp_ref[z, where, span] = scale * jnp.sqrt(sp_ref[z, where, span] + gp)
        sm_ref[z, where, span] = scale * jnp.sqrt(sm_ref[z, where, span] + gm)

    z_stage(
        lambda z, t, span: ls_ref[z + 3, 8 * t + offset : 8 * t + offset + 8, span], layers, rows, lanes, finish
    )


def vmem_call(kernel, outs, args, scratch=(), cycles=0):
    specs = []
    for arg in args:
        space = pltpu.SMEM if arg.dtype == jnp.int32 else pltpu.VMEM
        specs.append(pl.BlockSpec(memory_space=space))
    return pl.pallas_call(
        kernel,
        out_shape=tuple(jax.ShapeDtypeStruct(shape, jnp.float32) for shape in outs),
        in_specs=specs,
        out_specs=tuple(pl.BlockSpec(memory_space=pltpu.VMEM) for _ in outs),
        scratch_shapes=[pltpu.VMEM(shape, jnp.float32) for shape in scratch],
        compiler_params=pltpu.CompilerParams(vmem_limit_bytes=VMEM_LIMIT),
        cost_estimate=pl.CostEstimate(flops=cycles * 4096, bytes_accessed=1 << 20, transcendentals=0),
    )(*args)


def place_flags():
    wide, narrow = lax.axis_index("wide"), lax.axis_index("narrow")
    flags = [
        1 - wide % 2, wide == 0, wide == lax.axis_size("wide") - 1,
        1 - narrow % 2, narrow == 0, narrow == lax.axis_size("narrow") - 1,
    ]
    return jnp.stack([jnp.asarray(f).astype(jnp.int32) for f in flags])


def y_inside(place_ref, base, first_row, shape, rows):
    row = lax.broadcasted_iota(jnp.int32, shape, 0) + (first_row - base)
    inside = (row >= 0) | (place_ref[4] == 0)
    return inside & ((row < rows) | (place_ref[5] == 0))


def extend_kernel(
    place_ref, tile_ref, ra_ref, rb_ref, pa_ref, pb_ref, pc_ref, po_ref, ls_ref, sp_ref, sm_ref,
    speed_ref, speed6_ref, phi_ref, ma_ref, mb_ref, one, two, keep, pull,
):
    depth, rows, lanes = tile_ref.shape
    layers = depth - 2 * HALO
    tall = ls_ref.shape[1]
    margin = 8
    base = margin + YE
    peak = jnp.maximum(jnp.maximum(pa_ref[...], pb_ref[...]), jnp.maximum(pc_ref[...], po_ref[...]))
    scale = 1.0 / (peak[0:1, 0:1] + 1e-06)

    def assemble(z, carry):
        one[z, base : base + rows, :] = tile_ref[z]
        return carry

    lax.fori_loop(0, depth, assemble, 0)

    def below(ref):
        for z in range(depth):
            one[z, base - 8 : base, :] = ref[z]
            one[z, base - 10 : base - 8, :] = ref[depth + z // 4, 2 * (z % 4) : 2 * (z % 4) + 2, :]

    def above(ref):
        for z in range(depth):
            one[z, base + rows : base + rows + 8, :] = ref[z]
            one[z, base + rows + 8 : base + rows + 10, :] = ref[depth + z // 4, 2 * (z % 4) : 2 * (z % 4) + 2, :]

    @pl.when(place_ref[3] == 1)
    def _():
        above(ra_ref)
        below(rb_ref)

    @pl.when(place_ref[3] == 0)
    def _():
        below(ra_ref)
        above(rb_ref)

    def normalise(z, carry):
        outside = ((z < HALO) & (place_ref[1] == 1)) | ((z >= depth - HALO) & (place_ref[2] == 1))
        for t in range(tall // 8):
            at = slice(margin + 8 * t, margin + 8 * t + 8)
            ok = y_inside(place_ref, YE, 8 * t, (8, lanes), rows) & jnp.logical_not(outside)
            velocity = jnp.where(ok, one[z, at, :] * scale - 0.5, 0.0)
            one[z, at, :] = velocity

            @pl.when((z >= 1) & (z < depth - 1))
            def _():
                ls = ls_ref[z - 1, 8 * t : 8 * t + 8, :]
                weight = 1.0 / (1.0 + 4.0 * ls * ls)
                keep[z, 8 * t : 8 * t + 8, :] = weight * velocity
                pull[z, 8 * t : 8 * t + 8, :] = jnp.where(ok, (1.0 - weight) * (1.0 / 6.0), 0.0)

        return carry

    lax.fori_loop(0, depth, normalise, 0)
    for step in range(EXT_PASSES):
        source, target = (one, two) if step % 2 == 0 else (two, one)

        def extend(z, carry):
            for t in range(tall // 8):
                at = margin + 8 * t
                centre = source[z, at : at + 8, :]
                lane = lax.broadcasted_iota(jnp.int32, centre.shape, 1)
                total = source[z - 1, at : at + 8, :] + source[z + 1, at : at + 8, :]
                total = total + (source[z, at - 1 : at + 7, :] + source[z, at + 1 : at + 9, :])
                total = total + jnp.where(lane == 0, 0.0, pltpu.roll(centre, 1, 1))
                total = total + jnp.where(lane == lanes - 1, 0.0, pltpu.roll(centre, lanes - 1, 1))
                span = slice(8 * t, 8 * t + 8)
                target[z, at : at + 8, :] = keep[z, span, :] + pull[z, span, :] * total
            return carry

        lax.fori_loop(step + 1, depth - 1 - step, extend, 0)

    final = one if EXT_PASSES % 2 == 0 else two

    def march(z, carry):
        speed_ref[z] = final[z + HALO, base : base + rows, :]
        shift = YE - Y1
        for t in range(speed6_ref.shape[1] // 8):
            span = slice(8 * t, 8 * t + 8)
            speed = final[z + HALO, margin + shift + 8 * t : margin + shift + 8 * t + 8, :]
            speed6_ref[z, span, :] = speed
            change = jnp.maximum(speed, 0.0) * sp_ref[z, span, :] + jnp.minimum(speed, 0.0) * sm_ref[z, span, :]
            phi = ls_ref[z + 3, shift + 8 * t : shift + 8 * t + 8, :] - change
            phi_ref[z, span, :] = jnp.where(y_inside(place_ref, Y1, 8 * t, phi.shape, rows), phi, 1.0)
        return carry

    lax.fori_loop(0, layers, march, 0)
    send_edges(place_ref, phi_ref, Y1 - Y2, ma_ref, mb_ref)


def send_edges(place_ref, phi_ref, offset, ma_ref, mb_ref):
    layers = phi_ref.shape[0]
    count = ma_ref.shape[1]
    upper = place_ref[0] * (layers - 3)
    lower = (1 - place_ref[0]) * (layers - 3)
    for k in range(3):
        ma_ref[k] = phi_ref[upper + k, offset : offset + count, :]
        mb_ref[k] = phi_ref[lower + k, offset : offset + count, :]


def take_edges(place_ref, ra_ref, rb_ref, edges):
    upper = 3 * place_ref[0]
    lower = 3 - upper
    for k in range(3):
        edges[upper + k] = ra_ref[k]
        edges[lower + k] = rb_ref[k]

    @pl.when(place_ref[1] == 1)
    def _():
        edges[0:3] = jnp.ones((3,) + tuple(edges.shape[1:]), jnp.float32)

    @pl.when(place_ref[2] == 1)
    def _():
        edges[3:6] = jnp.ones((3,) + tuple(edges.shape[1:]), jnp.float32)


def plane_kernel(offset, exact, phi_ref, gp_ref, gm_ref):
    xy_stage(phi_ref, offset, 0, gp_ref.shape[0], gp_ref, gm_ref, exact)


def finish_kernel(
    offset, rows, place_ref, phi_ref, ra_ref, rb_ref, gp_ref, gm_ref, speed_ref, *rest
):
    out_ref, edges = rest[0], rest[-1]
    layers, count, lanes = out_ref.shape
    base = Y2 if count > rows else 0
    speed_offset = offset if count > rows else 0
    take_edges(place_ref, ra_ref, rb_ref, edges)

    def get_phi(z, t, span):
        if z < 0:
            return edges[z + 3, 8 * t : 8 * t + 8, span]
        if z >= layers:
            return edges[z - layers + 3, 8 * t : 8 * t + 8, span]
        return phi_ref[z, 8 * t + offset : 8 * t + offset + 8, span]

    def finish(z, t, span, gp, gm):
        where = pl.ds(8 * t, 8)
        speed = speed_ref[z, 8 * t + speed_offset : 8 * t + speed_offset + 8, span]
        total = jnp.where(speed > 0.0, gp_ref[z, where, span] + gp, gm_ref[z, where, span] + gm)
        phi = get_phi(z, t, span) - (TIME_STEP / 6.0) * speed * jnp.sqrt(total)
        if count > rows:
            phi = jnp.where(y_inside(place_ref, base, 8 * t, phi.shape, rows), phi, 1.0)
        out_ref[z, where, span] = phi

    z_stage(get_phi, layers, count, lanes, finish)
    if len(rest) > 2:
        send_edges(place_ref, out_ref, Y2, rest[1], rest[2])


def swaps(axis):
    count = lax.axis_size(axis)
    first, second = [], []
    for i in range(0, count, 2):
        first += [(i, i + 1), (i + 1, i)]
        j = (i + 2) % count
        second += [(i + 1, j), (j, i + 1)]
    return first, second


def level_halo(level_set, place):
    first, second = swaps("wide")
    layers, rows, lanes = level_set.shape
    even = place[0] == 1
    low, high = level_set[:3], level_set[layers - 3 :]
    got_a = lax.ppermute(jnp.where(even, high, low), "wide", first)
    got_b = lax.ppermute(jnp.where(even, low, high), "wide", second)
    below = jnp.where(even, got_b, got_a)
    above = jnp.where(even, got_a, got_b)
    below = jnp.where(place[1] == 1, 1.0, below)
    above = jnp.where(place[2] == 1, 1.0, above)
    tall = jnp.concatenate([below, level_set, above], axis=0)
    low = lax.ppermute(tall[:, rows - 9 :], "narrow", ring("narrow", 1))
    high = lax.ppermute(tall[:, :9], "narrow", ring("narrow", -1))
    low = jnp.where(place[4] == 1, 1.0, low)
    high = jnp.where(place[5] == 1, 1.0, high)
    total = -(-(rows + 2 * YE) // 8) * 8
    left = jnp.ones((layers + 6, YE - 9, lanes), jnp.float32)
    right = jnp.ones((layers + 6, total - rows - 9 - YE, lanes), jnp.float32)
    return jnp.concatenate([left, low, tall, high, right], axis=1)


def level_part(place, tile, ma, mb, wide_peak, level_set, ls, sp, sm):
    layers, rows, lanes = level_set.shape
    nfirst, nsecond = swaps("narrow")
    wfirst, wsecond = swaps("wide")
    count = lax.axis_size("narrow")
    across = [(i, (i + count // 2) % count) for i in range(count)]
    ra = lax.ppermute(ma, "narrow", nfirst)
    rb = lax.ppermute(mb, "narrow", nsecond)
    pc = lax.ppermute(wide_peak, "narrow", across)
    pa, pb = ra[-1, :, :128], rb[-1, :, :128]
    tall = ls.shape[1]
    rows1 = -(-(rows + 2 * Y1) // 8) * 8
    rows2 = -(-(rows + 2 * Y2) // 8) * 8
    depth = layers + 2 * HALO
    speed, speed6, phi, sa, sb = vmem_call(
        extend_kernel,
        [(layers, rows, lanes), (layers, rows1, lanes), (layers, rows1, lanes), (3, rows2, lanes), (3, rows2, lanes)],
        (place, tile, ra, rb, pa, pb, pc, wide_peak, ls, sp, sm),
        [(depth, tall + 16, lanes)] * 2 + [(depth, tall, lanes)] * 2,
        8000,
    )
    ga = lax.ppermute(sa, "wide", wfirst)
    gb = lax.ppermute(sb, "wide", wsecond)
    gp, gm = vmem_call(functools.partial(plane_kernel, Y1 - Y2, False), [(layers, rows2, lanes)] * 2, (phi,), (), 12000)
    phi, sa, sb = vmem_call(
        functools.partial(finish_kernel, Y1 - Y2, rows),
        [(layers, rows2, lanes), (3, rows, lanes), (3, rows, lanes)],
        (place, phi, ga, gb, gp, gm, speed6),
        [(6, rows2, lanes)],
        5000,
    )
    ga = lax.ppermute(sa, "wide", wfirst)
    gb = lax.ppermute(sb, "wide", wsecond)
    gp, gm = vmem_call(functools.partial(plane_kernel, Y2, True), [(layers, rows, lanes)] * 2, (phi,), (), 12000)
    (phi,) = vmem_call(
        functools.partial(finish_kernel, Y2, rows),
        [(layers, rows, lanes)],
        (place, phi, ga, gb, gp, gm, speed),
        [(6, rows, lanes)],
        5000,
    )
    return phi, speed


def first_gradient(ls, layers, rows):
    rows1 = -(-(rows + 2 * Y1) // 8) * 8
    return vmem_call(first_gradient_kernel, [(layers, rows1, ls.shape[2])] * 2, (ls,), (), 25000)


def unpack_kernel(place_ref, recv_ref, tile_ref, peak_ref, ma_ref, mb_ref):
    parts = recv_ref.shape[0]
    depth, rows, lanes = tile_ref.shape
    for j in range(depth // 4):
        block = recv_ref[:, 16 * j : 16 * j + 16, :].reshape(parts * 16, 128)
        wide = pltpu.roll(block.T, 1, 1)
        for k in range(4):
            tile_ref[4 * j + k] = wide[rows * k : rows * (k + 1), :]
    peak = recv_ref[0, 80:88, :]
    for s in range(1, parts):
        peak = jnp.maximum(peak, recv_ref[s, 80:88, :])
    peak_ref[...] = peak
    fill_edges(place_ref, tile_ref, peak, ma_ref, mb_ref)


def fill_edges(place_ref, tile_ref, peak, ma_ref, mb_ref):
    depth, rows, lanes = tile_ref.shape

    def upper(ref):
        for z in range(depth):
            ref[z] = tile_ref[z, rows - 8 : rows, :]
            ref[depth + z // 4, 2 * (z % 4) : 2 * (z % 4) + 2, :] = tile_ref[z, rows - 10 : rows - 8, :]

    def lower(ref):
        for z in range(depth):
            ref[z] = tile_ref[z, 0:8, :]
            ref[depth + z // 4, 2 * (z % 4) : 2 * (z % 4) + 2, :] = tile_ref[z, 8:10, :]

    last = ma_ref.shape[0] - 1
    ma_ref[last, :, 0:128] = peak
    mb_ref[last, :, 0:128] = peak

    @pl.when(place_ref[3] == 1)
    def _():
        upper(ma_ref)
        lower(mb_ref)

    @pl.when(place_ref[3] == 0)
    def _():
        lower(ma_ref)
        upper(mb_ref)


def unpack(place, recv, own_z, rows):
    parts = recv.shape[0]
    lanes = parts * 16
    depth = own_z + 2 * HALO
    edge = (depth + depth // 4 + 1, 8, lanes)
    return vmem_call(
        unpack_kernel, [(depth, rows, lanes), (8, 128), edge, edge], (place, recv), (), 1500
    )


def per_device(displacement, material, level_set):
    wide = lax.axis_size("wide")
    own_z, rows, size_x = level_set.shape
    place = place_flags()
    message = energy_message(displacement, material).reshape(wide, 88, 128)
    ls = level_halo(level_set, place)
    sp, sm = first_gradient(ls, own_z, rows)
    recv = lax.all_to_all(message, "wide", split_axis=0, concat_axis=0, tiled=True)
    tile, wide_peak, ma, mb = unpack(place, recv, own_z, rows)
    return level_part(place, tile, ma, mb, wide_peak, level_set, ls, sp, sm)


def solution(mesh):
    return jax.shard_map(
        per_device,
        mesh=mesh,
        in_specs=(
            P(None, None, "wide", "narrow", None),
            P("wide", "narrow", None),
            P("wide", "narrow", None),
        ),
        out_specs=(P("wide", "narrow", None), P("wide", "narrow", None)),
        check_vma=False,
    )
```

```python
import functools
import jax
import jax.numpy as jnp
from jax import lax
from jax.experimental import pallas as pl
from jax.experimental.pallas import tpu as pltpu
from jax.sharding import PartitionSpec as P

BZ = 16
EXT_PASSES = 4
HJ_STEPS = 3
SHEAR = 0.384615
LAME = 0.576923
WENO_EPS = 1e-06
TIME_STEP = 0.3
HALO = EXT_PASSES
GRAD_SCALE = 1.0 / (8.0 * 48.0 * 48.0)
YE = 10
Y1 = 6
Y2 = 3
VMEM_LIMIT = 48 * 1024 * 1024


def lane_shifts(value):
    blocks = [value[:, 128 * b : 128 * (b + 1)] for b in range(value.shape[1] // 128)]
    lane = lax.broadcasted_iota(jnp.int32, blocks[0].shape, 1)
    zero = jnp.zeros_like(blocks[0])
    outs = []
    for step in (-1, 1, 2):
        turned = [pltpu.roll(b, (-step) % 128, 1) for b in blocks]
        if step < 0:
            mask = lane < 1
            parts = [jnp.where(mask, turned[i - 1] if i > 0 else zero, turned[i]) for i in range(len(blocks))]
        else:
            mask = lane >= 128 - step
            parts = [
                jnp.where(mask, turned[i + 1] if i + 1 < len(blocks) else zero, turned[i])
                for i in range(len(blocks))
            ]
        outs.append(jnp.concatenate(parts, axis=1))
    return outs


def val4(a, b, c, d):
    return (a + d) + 23.0 * (b + c)


def der4(a, b, c, d):
    return (d - a) + 5.0 * (c - b)


def filter_plane(plane, filt, comp, layer, value, low, high0, high1):
    rows = value.shape[0]
    plane[8 : 8 + rows, :] = value
    plane[7:8, :] = low
    plane[8 + rows : 9 + rows, :] = high0
    plane[9 + rows : 10 + rows, :] = high1
    for tile in range(rows // 8):
        base = 8 + 8 * tile
        a = plane[base - 1 : base + 7, :]
        b = plane[base : base + 8, :]
        c = plane[base + 1 : base + 9, :]
        d = plane[base + 2 : base + 10, :]
        val_y = val4(a, b, c, d)
        der_y = der4(a, b, c, d)
        before, after, after2 = lane_shifts(val_y)
        span = pl.ds(8 * tile, 8)
        filt[comp, 0, layer, span, :] = val4(before, val_y, after, after2)
        filt[comp, 2, layer, span, :] = der4(before, val_y, after, after2)
        before, after, after2 = lane_shifts(der_y)
        filt[comp, 1, layer, span, :] = val4(before, der_y, after, after2)


def densities(field, rows, finish):
    for tile in range(rows // 8):
        span = pl.ds(8 * tile, 8)
        gx = [der4(*field(comp, 0, span)) for comp in range(3)]
        gy = [val4(*field(comp, 1, span)) for comp in range(3)]
        gz = [val4(*field(comp, 2, span)) for comp in range(3)]
        sxy = gy[0] + gx[1]
        sxz = gz[0] + gx[2]
        syz = gz[1] + gy[2]
        trace = gx[0] + gy[1] + gz[2]
        square = gx[0] * gx[0] + gy[1] * gy[1] + gz[2] * gz[2]
        shear = sxy * sxy + sxz * sxz + syz * syz
        scale = GRAD_SCALE * GRAD_SCALE
        finish(span, (SHEAR * scale) * (square + 0.5 * shear) + (0.5 * LAME * scale) * (trace * trace))


def accumulate(ref, slot):
    load = pl.program_id(0)

    def finish(span, density):
        @pl.when(load == 0)
        def _():
            ref[slot, span, :] = density

        @pl.when(load > 0)
        def _():
            ref[slot, span, :] += density

    return finish


def inner_kernel(u_ref, yh_ref, energy_ref, tail_ref, plane, filt):
    own_x, rows = u_ref.shape[2:4]

    def own_layer(layer, carry):
        for comp in range(3):
            edge = [yh_ref[0, comp, k, pl.ds(layer, 1), :] for k in range(3)]
            filter_plane(plane, filt, comp, layer, u_ref[0, comp, layer], *edge)
        return carry

    lax.fori_loop(0, own_x, own_layer, 0)

    def slot_step(slot, carry):
        field = lambda comp, which, span: [filt[comp, which, slot + k, span, :] for k in range(4)]
        densities(field, rows, accumulate(energy_ref, slot))
        return carry

    lax.fori_loop(0, own_x - 3, slot_step, 0)
    for comp in range(3):
        for which in range(3):
            for k in range(3):
                tail_ref[0, comp, which, k] = filt[comp, which, own_x - 3 + k]


def outer_kernel(place_ref, tail_ref, xh_ref, ch_ref, inner_ref, stiff_ref, msg_ref, plane, filt, energy, turned):
    load = pl.program_id(0)
    rows, size_z = xh_ref.shape[3:5]
    own_x = stiff_ref.shape[0]
    inner = own_x - 3
    tiles = rows // 8
    keep = jnp.where(place_ref[2] == 1, 0.0, 1.0)
    for comp in range(3):
        for k in range(3):
            edge = [ch_ref[0, comp, which, k : k + 1, :] for which in range(3)]
            filter_plane(plane, filt, comp, k, xh_ref[0, comp, k], *edge)

    def density_at(slot, masked):
        def field(comp, which, span):
            out = []
            for k in range(4):
                at = slot + k
                value = tail_ref[0, comp, which, at, span, :] if at < 3 else filt[comp, which, at - 3, span, :]
                out.append(value * keep if masked[k] else value)
            return out

        densities(field, rows, accumulate(energy, slot))

    density_at(0, (False, False, False, True))
    density_at(1, (False, False, True, True))
    density_at(2, (True, False, False, False))

    @pl.when(load == pl.num_programs(0) - 1)
    def _():
        peak = jnp.zeros((8, 128), jnp.float32)
        groups = own_x // 4
        for g in range(groups):
            stack = []
            for q in range(4):
                x = 4 * g + q
                value = (inner_ref[x] if x < inner else energy[x - inner]) * stiff_ref[x]
                stack.append(value)
                for tile in range(tiles):
                    for b in range(size_z // 128):
                        peak = jnp.maximum(peak, value[8 * tile : 8 * tile + 8, 128 * b : 128 * b + 128])
            turned[g, 0:8, :] = jnp.zeros((8, 128), jnp.float32)
            turned[g, size_z : size_z + 16, :] = jnp.zeros((16, 128), jnp.float32)
            turned[g, HALO : HALO + size_z, :] = jnp.concatenate(stack, axis=0).T
        peak = jnp.broadcast_to(jnp.max(peak, axis=0, keepdims=True), (8, 128))
        peak = jnp.broadcast_to(jnp.max(peak, axis=1, keepdims=True), (8, 128))
        parts = msg_ref.shape[0] // 88
        own_z = size_z // parts
        quads = (own_z + 2 * HALO) // 4
        lane = lax.broadcasted_iota(jnp.int32, (parts, 128), 1) // rows
        for g in range(groups):
            for j in range(quads):
                picked = [turned[g, pl.ds(4 * j + k, parts, stride=own_z), :] for k in range(4)]
                for q in range(4):
                    out = None
                    for k in range(4):
                        shift = (rows * (k - q)) % 128
                        part = pltpu.roll(picked[k], shift, 1) if shift else picked[k]
                        out = part if out is None else jnp.where(lane == k, part, out)
                    msg_ref[pl.ds(16 * j + 4 * g + q, parts, stride=88), :] = out
        for t in range(parts):
            msg_ref[pl.ds(88 * t + 80, 8), :] = peak


def load_block(*shape):
    return pl.BlockSpec((1,) + shape, lambda l: (l,) + (0,) * len(shape))


def fixed_block(*shape):
    return pl.BlockSpec(shape, lambda l: (0,) * len(shape))


def inner_strain(disp, yh):
    loads, comps, own_x, rows, size_z = disp.shape
    return pl.pallas_call(
        inner_kernel,
        grid=(loads,),
        out_shape=(
            jax.ShapeDtypeStruct((own_x - 3, rows, size_z), jnp.float32),
            jax.ShapeDtypeStruct((loads, comps, 3, 3, rows, size_z), jnp.float32),
        ),
        in_specs=[load_block(comps, own_x, rows, size_z), load_block(comps, 3, own_x, size_z)],
        out_specs=(fixed_block(own_x - 3, rows, size_z), load_block(comps, 3, 3, rows, size_z)),
        scratch_shapes=[
            pltpu.VMEM((rows + 16, size_z), jnp.float32),
            pltpu.VMEM((3, 3, own_x, rows, size_z), jnp.float32),
        ],
        compiler_params=pltpu.CompilerParams(vmem_limit_bytes=VMEM_LIMIT),
        cost_estimate=pl.CostEstimate(flops=40000 * 4096, bytes_accessed=1 << 20, transcendentals=0),
    )(disp, yh)


def strain_message(place, tail, xh, ch, inner, stiff, parts):
    loads, comps = xh.shape[:2]
    own_x, rows, size_z = stiff.shape
    return pl.pallas_call(
        outer_kernel,
        grid=(loads,),
        out_shape=jax.ShapeDtypeStruct((parts * 88, 128), jnp.float32),
        in_specs=[
            pl.BlockSpec(memory_space=pltpu.SMEM),
            load_block(comps, 3, 3, rows, size_z),
            load_block(comps, 3, rows, size_z),
            load_block(comps, 3, 3, size_z),
            fixed_block(own_x - 3, rows, size_z),
            fixed_block(own_x, rows, size_z),
        ],
        out_specs=fixed_block(parts * 88, 128),
        scratch_shapes=[
            pltpu.VMEM((rows + 16, size_z), jnp.float32),
            pltpu.VMEM((3, 3, 3, rows, size_z), jnp.float32),
            pltpu.VMEM((3, rows, size_z), jnp.float32),
            pltpu.VMEM((own_x // 4, size_z + 16, 128), jnp.float32),
        ],
        compiler_params=pltpu.CompilerParams(vmem_limit_bytes=VMEM_LIMIT),
        cost_estimate=pl.CostEstimate(flops=10000 * 4096, bytes_accessed=1 << 20, transcendentals=0),
    )(place, tail, xh, ch, inner, stiff)


def ring(axis, step):
    count = lax.axis_size(axis)
    return [(i, i + step) for i in range(count) if 0 <= i + step < count]


def newton_reciprocal(x):
    r = pl.reciprocal(x, approx=True)
    return r * (2.0 - x * r)


def weno_cell(d, e0, e1, e2, e3):
    f0 = e1 - e0
    f1 = e2 - e1
    f2 = e3 - e2
    g0 = f1 - f0
    g1 = f2 - f1
    twice1 = e1 + e1
    twice2 = e2 + e2
    third = 13.0 / 3.0
    eps = 4.0 * WENO_EPS
    pa = twice1 + f0
    pb = twice1 + f1
    pc = twice2 - f2
    a = (f0 * f0 * third + eps) + pa * pa
    b = (f1 * f1 * third + eps) + pb * pb
    c = (f2 * f2 * third + eps) + pc * pc
    a = a * a
    b = b * b * (1.0 / 6.0)
    c = c * c
    ac = a * c
    ab = a * b
    cb = c * b
    u = cb * g0
    v = ab * g1
    both = u + v
    both = both + both
    s = e1 + e2
    d6 = 6.0 * d
    minus = d6 + (s + e2) - (both + v) * newton_reciprocal(ac + cb + 3.0 * ab)
    plus = (s + e1) - d6 - (both + u) * newton_reciprocal(ac + ab + 3.0 * cb)
    return minus, plus


def godunov(minus, plus):
    high = jnp.maximum(jnp.maximum(minus, plus), 0.0)
    low = jnp.minimum(jnp.minimum(minus, plus), 0.0)
    return high * high, low * low


def x_terms(phi):
    rows, size = phi.shape
    wide = size + 128
    phi = jnp.concatenate([phi, jnp.ones((rows, 128), jnp.float32)], axis=1)
    d = pltpu.roll(phi, wide - 1, 1) - phi
    e = pltpu.roll(d, wide - 1, 1) - d
    minus, plus = weno_cell(
        d, pltpu.roll(e, 2, 1), pltpu.roll(e, 1, 1), e, pltpu.roll(e, wide - 1, 1)
    )
    return godunov(pltpu.roll(minus, 1, 1)[:, :size], plus[:, :size])


def y_cells(ref, layer, row):
    p = [ref[layer, row + k : row + k + 8, :] for k in range(6)]
    d = [p[k + 1] - p[k] for k in range(5)]
    e = [d[k + 1] - d[k] for k in range(4)]
    return weno_cell(d[2], *e)


def xy_stage(phi_ref, offset, layer0, layers, gp_ref, gm_ref, exact=False):
    rows = gp_ref.shape[1]
    tiles = rows // 8

    def layer_step(z, carry):
        cells = [y_cells(phi_ref, z + layer0, 8 * t + offset - 3) for t in range(tiles)]
        turned = [pltpu.roll(c[1], 7, 0) for c in cells]
        if exact:
            start = min(rows + offset - 3, phi_ref.shape[1] - 13)
            extra = y_cells(phi_ref, z + layer0, start)[1]
            turned.append(pltpu.roll(extra, 7 - (rows + offset - 3 - start), 0))
        else:
            turned.append(turned[-1])
        row = lax.broadcasted_iota(jnp.int32, turned[0].shape, 0)
        for t in range(tiles):
            plus = jnp.where(row == 7, turned[t + 1], turned[t])
            yp, ym = godunov(cells[t][0], plus)
            xp, xm = x_terms(phi_ref[z + layer0, 8 * t + offset : 8 * t + offset + 8, :])
            gp_ref[z, 8 * t : 8 * t + 8, :] = xp + yp
            gm_ref[z, 8 * t : 8 * t + 8, :] = xm + ym
        return carry

    lax.fori_loop(0, layers, layer_step, 0)


def z_stage(get_phi, layers, rows, lanes, finish):
    def lane_step(block, carry):
        span = pl.ds(pl.multiple_of(128 * block, 128), 128)
        for t in range(rows // 8):
            p = [get_phi(z, t, span) for z in range(-3, layers + 3)]
            d = [p[k + 1] - p[k] for k in range(len(p) - 1)]
            e = [d[k + 1] - d[k] for k in range(len(d) - 1)]
            before = None
            for cell in range(layers + 1):
                minus, plus = weno_cell(d[cell + 2], e[cell], e[cell + 1], e[cell + 2], e[cell + 3])
                if before is not None:
                    finish(cell - 1, t, span, *godunov(before, plus))
                before = minus
        return carry

    lax.fori_loop(0, lanes // 128, lane_step, 0)


def first_gradient_kernel(place_ref, tall_ref, ra_ref, rb_ref, ls_ref, sp_ref, sm_ref):
    layers, rows, lanes = sp_ref.shape
    depth, own, _ = tall_ref.shape
    ones = jnp.ones((8, lanes), jnp.float32)

    def copy(z, carry):
        for t in range(ls_ref.shape[1] // 8):
            ls_ref[z, 8 * t : 8 * t + 8, :] = ones
        ls_ref[z, YE : YE + own, :] = tall_ref[z]
        return carry

    lax.fori_loop(0, depth, copy, 0)

    def below(ref):
        @pl.when(place_ref[4] == 0)
        def _():
            for z in range(depth):
                ls_ref[z, YE - 8 : YE, :] = ref[z]
                ls_ref[z, YE - 9 : YE - 8, :] = ref[depth + z // 8, z % 8 : z % 8 + 1, :]

    def above(ref):
        @pl.when(place_ref[5] == 0)
        def _():
            for z in range(depth):
                ls_ref[z, YE + own : YE + own + 8, :] = ref[z]
                ls_ref[z, YE + own + 8 : YE + own + 9, :] = ref[depth + z // 8, z % 8 : z % 8 + 1, :]

    @pl.when(place_ref[3] == 1)
    def _():
        above(ra_ref)
        below(rb_ref)

    @pl.when(place_ref[3] == 0)
    def _():
        below(ra_ref)
        above(rb_ref)

    offset = YE - Y1
    xy_stage(ls_ref, offset, 3, layers, sp_ref, sm_ref)

    def finish(z, t, span, gp, gm):
        where = pl.ds(8 * t, 8)
        scale = TIME_STEP / 6.0
        sp_ref[z, where, span] = scale * jnp.sqrt(sp_ref[z, where, span] + gp)
        sm_ref[z, where, span] = scale * jnp.sqrt(sm_ref[z, where, span] + gm)

    z_stage(
        lambda z, t, span: ls_ref[z + 3, 8 * t + offset : 8 * t + offset + 8, span], layers, rows, lanes, finish
    )


def vmem_call(kernel, outs, args, scratch=(), cycles=0):
    specs = []
    for arg in args:
        space = pltpu.SMEM if arg.dtype == jnp.int32 else pltpu.VMEM
        specs.append(pl.BlockSpec(memory_space=space))
    return pl.pallas_call(
        kernel,
        out_shape=tuple(jax.ShapeDtypeStruct(shape, jnp.float32) for shape in outs),
        in_specs=specs,
        out_specs=tuple(pl.BlockSpec(memory_space=pltpu.VMEM) for _ in outs),
        scratch_shapes=[pltpu.VMEM(shape, jnp.float32) for shape in scratch],
        compiler_params=pltpu.CompilerParams(vmem_limit_bytes=VMEM_LIMIT),
        cost_estimate=pl.CostEstimate(flops=cycles * 4096, bytes_accessed=1 << 20, transcendentals=0),
    )(*args)


def place_flags():
    wide, narrow = lax.axis_index("wide"), lax.axis_index("narrow")
    flags = [
        1 - wide % 2, wide == 0, wide == lax.axis_size("wide") - 1,
        1 - narrow % 2, narrow == 0, narrow == lax.axis_size("narrow") - 1,
    ]
    return jnp.stack([jnp.asarray(f).astype(jnp.int32) for f in flags])


def y_inside(place_ref, base, first_row, shape, rows):
    row = lax.broadcasted_iota(jnp.int32, shape, 0) + (first_row - base)
    inside = (row >= 0) | (place_ref[4] == 0)
    return inside & ((row < rows) | (place_ref[5] == 0))


def extend_kernel(
    place_ref, tile_ref, ra_ref, rb_ref, pa_ref, pb_ref, pc_ref, po_ref, ls_ref, sp_ref, sm_ref,
    speed_ref, speed6_ref, phi_ref, ma_ref, mb_ref, one, two, keep, pull,
):
    depth, rows, lanes = tile_ref.shape
    layers = depth - 2 * HALO
    tall = ls_ref.shape[1]
    margin = 8
    base = margin + YE
    peak = jnp.maximum(jnp.maximum(pa_ref[...], pb_ref[...]), jnp.maximum(pc_ref[...], po_ref[...]))
    scale = 1.0 / (peak[0:1, 0:1] + 1e-06)

    def assemble(z, carry):
        one[z, base : base + rows, :] = tile_ref[z]
        return carry

    lax.fori_loop(0, depth, assemble, 0)

    def below(ref):
        for z in range(depth):
            one[z, base - 8 : base, :] = ref[z]
            one[z, base - 10 : base - 8, :] = ref[depth + z // 4, 2 * (z % 4) : 2 * (z % 4) + 2, :]

    def above(ref):
        for z in range(depth):
            one[z, base + rows : base + rows + 8, :] = ref[z]
            one[z, base + rows + 8 : base + rows + 10, :] = ref[depth + z // 4, 2 * (z % 4) : 2 * (z % 4) + 2, :]

    @pl.when(place_ref[3] == 1)
    def _():
        above(ra_ref)
        below(rb_ref)

    @pl.when(place_ref[3] == 0)
    def _():
        below(ra_ref)
        above(rb_ref)

    def normalise(z, carry):
        outside = ((z < HALO) & (place_ref[1] == 1)) | ((z >= depth - HALO) & (place_ref[2] == 1))
        for t in range(tall // 8):
            at = slice(margin + 8 * t, margin + 8 * t + 8)
            ok = y_inside(place_ref, YE, 8 * t, (8, lanes), rows) & jnp.logical_not(outside)
            velocity = jnp.where(ok, one[z, at, :] * scale - 0.5, 0.0)
            one[z, at, :] = velocity

            @pl.when((z >= 1) & (z < depth - 1))
            def _():
                ls = ls_ref[z - 1, 8 * t : 8 * t + 8, :]
                weight = 1.0 / (1.0 + 4.0 * ls * ls)
                keep[z, 8 * t : 8 * t + 8, :] = weight * velocity
                pull[z, 8 * t : 8 * t + 8, :] = jnp.where(ok, (1.0 - weight) * (1.0 / 6.0), 0.0)

        return carry

    lax.fori_loop(0, depth, normalise, 0)
    for step in range(EXT_PASSES):
        source, target = (one, two) if step % 2 == 0 else (two, one)

        def extend(z, carry):
            for t in range(tall // 8):
                at = margin + 8 * t
                centre = source[z, at : at + 8, :]
                lane = lax.broadcasted_iota(jnp.int32, centre.shape, 1)
                total = source[z - 1, at : at + 8, :] + source[z + 1, at : at + 8, :]
                total = total + (source[z, at - 1 : at + 7, :] + source[z, at + 1 : at + 9, :])
                total = total + jnp.where(lane == 0, 0.0, pltpu.roll(centre, 1, 1))
                total = total + jnp.where(lane == lanes - 1, 0.0, pltpu.roll(centre, lanes - 1, 1))
                span = slice(8 * t, 8 * t + 8)
                target[z, at : at + 8, :] = keep[z, span, :] + pull[z, span, :] * total
            return carry

        lax.fori_loop(step + 1, depth - 1 - step, extend, 0)

    final = one if EXT_PASSES % 2 == 0 else two

    def march(z, carry):
        speed_ref[z] = final[z + HALO, base : base + rows, :]
        shift = YE - Y1
        for t in range(speed6_ref.shape[1] // 8):
            span = slice(8 * t, 8 * t + 8)
            speed = final[z + HALO, margin + shift + 8 * t : margin + shift + 8 * t + 8, :]
            speed6_ref[z, span, :] = speed
            change = jnp.maximum(speed, 0.0) * sp_ref[z, span, :] + jnp.minimum(speed, 0.0) * sm_ref[z, span, :]
            phi = ls_ref[z + 3, shift + 8 * t : shift + 8 * t + 8, :] - change
            phi_ref[z, span, :] = jnp.where(y_inside(place_ref, Y1, 8 * t, phi.shape, rows), phi, 1.0)
        return carry

    lax.fori_loop(0, layers, march, 0)
    send_edges(place_ref, phi_ref, Y1 - Y2, ma_ref, mb_ref)


def send_edges(place_ref, phi_ref, offset, ma_ref, mb_ref):
    layers = phi_ref.shape[0]
    count = ma_ref.shape[1]
    upper = place_ref[0] * (layers - 3)
    lower = (1 - place_ref[0]) * (layers - 3)
    for k in range(3):
        ma_ref[k] = phi_ref[upper + k, offset : offset + count, :]
        mb_ref[k] = phi_ref[lower + k, offset : offset + count, :]


def take_edges(place_ref, ra_ref, rb_ref, edges):
    upper = 3 * place_ref[0]
    lower = 3 - upper
    for k in range(3):
        edges[upper + k] = ra_ref[k]
        edges[lower + k] = rb_ref[k]

    @pl.when(place_ref[1] == 1)
    def _():
        edges[0:3] = jnp.ones((3,) + tuple(edges.shape[1:]), jnp.float32)

    @pl.when(place_ref[2] == 1)
    def _():
        edges[3:6] = jnp.ones((3,) + tuple(edges.shape[1:]), jnp.float32)


def plane_kernel(offset, exact, phi_ref, gp_ref, gm_ref):
    xy_stage(phi_ref, offset, 0, gp_ref.shape[0], gp_ref, gm_ref, exact)


def finish_kernel(
    offset, rows, place_ref, phi_ref, ra_ref, rb_ref, gp_ref, gm_ref, speed_ref, *rest
):
    out_ref, edges = rest[0], rest[-1]
    layers, count, lanes = out_ref.shape
    base = Y2 if count > rows else 0
    speed_offset = offset if count > rows else 0
    take_edges(place_ref, ra_ref, rb_ref, edges)

    def get_phi(z, t, span):
        if z < 0:
            return edges[z + 3, 8 * t : 8 * t + 8, span]
        if z >= layers:
            return edges[z - layers + 3, 8 * t : 8 * t + 8, span]
        return phi_ref[z, 8 * t + offset : 8 * t + offset + 8, span]

    def finish(z, t, span, gp, gm):
        where = pl.ds(8 * t, 8)
        speed = speed_ref[z, 8 * t + speed_offset : 8 * t + speed_offset + 8, span]
        total = jnp.where(speed > 0.0, gp_ref[z, where, span] + gp, gm_ref[z, where, span] + gm)
        phi = get_phi(z, t, span) - (TIME_STEP / 6.0) * speed * jnp.sqrt(total)
        if count > rows:
            phi = jnp.where(y_inside(place_ref, base, 8 * t, phi.shape, rows), phi, 1.0)
        out_ref[z, where, span] = phi

    z_stage(get_phi, layers, count, lanes, finish)
    if len(rest) > 2:
        send_edges(place_ref, out_ref, Y2, rest[1], rest[2])


def swaps(axis):
    count = lax.axis_size(axis)
    first, second = [], []
    for i in range(0, count, 2):
        first += [(i, i + 1), (i + 1, i)]
        j = (i + 2) % count
        second += [(i + 1, j), (j, i + 1)]
    return first, second


def stack_kernel(place_ref, ls_ref, ra_ref, rb_ref, tall_ref, ma_ref, mb_ref, edges):
    layers, rows = ls_ref.shape[:2]
    take_edges(place_ref, ra_ref, rb_ref, edges)
    for k in range(3):
        tall_ref[k] = edges[k]
        tall_ref[layers + 3 + k] = edges[3 + k]

    def copy(z, carry):
        tall_ref[z + 3] = ls_ref[z]
        return carry

    lax.fori_loop(0, layers, copy, 0)
    depth = layers + 6

    def upper(ref):
        for z in range(depth):
            ref[z] = tall_ref[z, rows - 8 : rows, :]
            ref[depth + z // 8, z % 8 : z % 8 + 1, :] = tall_ref[z, rows - 9 : rows - 8, :]

    def lower(ref):
        for z in range(depth):
            ref[z] = tall_ref[z, 0:8, :]
            ref[depth + z // 8, z % 8 : z % 8 + 1, :] = tall_ref[z, 8:9, :]

    @pl.when(place_ref[3] == 1)
    def _():
        upper(ma_ref)
        lower(mb_ref)

    @pl.when(place_ref[3] == 0)
    def _():
        lower(ma_ref)
        upper(mb_ref)


def level_part(place, tile, ma, mb, wide_peak, level_set, ls, sp, sm):
    layers, rows, lanes = level_set.shape
    nfirst, nsecond = swaps("narrow")
    wfirst, wsecond = swaps("wide")
    count = lax.axis_size("narrow")
    across = [(i, (i + count // 2) % count) for i in range(count)]
    ra = lax.ppermute(ma, "narrow", nfirst)
    rb = lax.ppermute(mb, "narrow", nsecond)
    pc = lax.ppermute(wide_peak, "narrow", across)
    pa, pb = ra[-1, :, :128], rb[-1, :, :128]
    tall = ls.shape[1]
    rows1 = -(-(rows + 2 * Y1) // 8) * 8
    rows2 = -(-(rows + 2 * Y2) // 8) * 8
    depth = layers + 2 * HALO
    speed, speed6, phi, sa, sb = vmem_call(
        extend_kernel,
        [(layers, rows, lanes), (layers, rows1, lanes), (layers, rows1, lanes), (3, rows2, lanes), (3, rows2, lanes)],
        (place, tile, ra, rb, pa, pb, pc, wide_peak, ls, sp, sm),
        [(depth, tall + 16, lanes)] * 2 + [(depth, tall, lanes)] * 2,
        8000,
    )
    ga = lax.ppermute(sa, "wide", wfirst)
    gb = lax.ppermute(sb, "wide", wsecond)
    gp, gm = vmem_call(functools.partial(plane_kernel, Y1 - Y2, False), [(layers, rows2, lanes)] * 2, (phi,), (), 12000)
    phi, sa, sb = vmem_call(
        functools.partial(finish_kernel, Y1 - Y2, rows),
        [(layers, rows2, lanes), (3, rows, lanes), (3, rows, lanes)],
        (place, phi, ga, gb, gp, gm, speed6),
        [(6, rows2, lanes)],
        5000,
    )
    ga = lax.ppermute(sa, "wide", wfirst)
    gb = lax.ppermute(sb, "wide", wsecond)
    gp, gm = vmem_call(functools.partial(plane_kernel, Y2, True), [(layers, rows, lanes)] * 2, (phi,), (), 12000)
    (phi,) = vmem_call(
        functools.partial(finish_kernel, Y2, rows),
        [(layers, rows, lanes)],
        (place, phi, ga, gb, gp, gm, speed),
        [(6, rows, lanes)],
        5000,
    )
    return phi, speed


def first_gradient(place, tall, ra, rb):
    depth, rows, lanes = tall.shape
    rows1 = -(-(rows + 2 * Y1) // 8) * 8
    total = -(-(rows + 2 * YE) // 8) * 8
    return vmem_call(
        first_gradient_kernel, [(depth, total, lanes)] + [(depth - 6, rows1, lanes)] * 2, (place, tall, ra, rb), (), 35000
    )


def stack_level(place, level_set, ra, rb):
    layers, rows, lanes = level_set.shape
    depth = layers + 6
    edge = (depth + -(-depth // 8), 8, lanes)
    return vmem_call(
        stack_kernel, [(depth, rows, lanes), edge, edge], (place, level_set, ra, rb), [(6, rows, lanes)], 1500
    )


def unpack_kernel(place_ref, recv_ref, tile_ref, peak_ref, ma_ref, mb_ref):
    parts = recv_ref.shape[0]
    depth, rows, lanes = tile_ref.shape
    for j in range(depth // 4):
        block = recv_ref[:, 16 * j : 16 * j + 16, :].reshape(parts * 16, 128)
        wide = pltpu.roll(block.T, 1, 1)
        for k in range(4):
            tile_ref[4 * j + k] = wide[rows * k : rows * (k + 1), :]
    peak = recv_ref[0, 80:88, :]
    for s in range(1, parts):
        peak = jnp.maximum(peak, recv_ref[s, 80:88, :])
    peak_ref[...] = peak
    fill_edges(place_ref, tile_ref, peak, ma_ref, mb_ref)


def fill_edges(place_ref, tile_ref, peak, ma_ref, mb_ref):
    depth, rows, lanes = tile_ref.shape

    def upper(ref):
        for z in range(depth):
            ref[z] = tile_ref[z, rows - 8 : rows, :]
            ref[depth + z // 4, 2 * (z % 4) : 2 * (z % 4) + 2, :] = tile_ref[z, rows - 10 : rows - 8, :]

    def lower(ref):
        for z in range(depth):
            ref[z] = tile_ref[z, 0:8, :]
            ref[depth + z // 4, 2 * (z % 4) : 2 * (z % 4) + 2, :] = tile_ref[z, 8:10, :]

    last = ma_ref.shape[0] - 1
    ma_ref[last, :, 0:128] = peak
    mb_ref[last, :, 0:128] = peak

    @pl.when(place_ref[3] == 1)
    def _():
        upper(ma_ref)
        lower(mb_ref)

    @pl.when(place_ref[3] == 0)
    def _():
        lower(ma_ref)
        upper(mb_ref)


def unpack(place, recv, own_z, rows):
    parts = recv.shape[0]
    lanes = parts * 16
    depth = own_z + 2 * HALO
    edge = (depth + depth // 4 + 1, 8, lanes)
    return vmem_call(
        unpack_kernel, [(depth, rows, lanes), (8, 128), edge, edge], (place, recv), (), 1500
    )


def per_device(displacement, material, level_set):
    wide = lax.axis_size("wide")
    loads, comps, own_x, rows, size_z = displacement.shape
    own_z, _, size_x = level_set.shape
    place = place_flags()
    backward = [(i, (i - 1) % wide) for i in range(wide)]
    wfirst, wsecond = swaps("wide")
    nfirst, nsecond = swaps("narrow")

    xh = lax.ppermute(displacement[:, :, :3], "wide", backward)
    low = lax.ppermute(displacement[:, :, :, -1], "narrow", ring("narrow", 1))
    high = lax.ppermute(
        jnp.stack([displacement[:, :, :, 0], displacement[:, :, :, 1]], axis=2), "narrow", ring("narrow", -1)
    )
    yh = jnp.concatenate([low[:, :, None], high], axis=2)
    blocks = material.shape[2]
    corner = yh[:, :, :, :3].reshape(loads * comps * 3, 3, size_z)
    first = material[0].astype(jnp.float32).reshape(-1)
    first = jnp.pad(first, (0, 3 * size_z - first.size)).reshape(1, 3, size_z)
    got = lax.ppermute(jnp.concatenate([corner, first], axis=0), "wide", backward)
    ch = got[: loads * comps * 3].reshape(loads, comps, 3, 3, size_z)
    beyond = got[loads * comps * 3].reshape(-1)[: rows * blocks].reshape(1, rows, blocks)
    solid = jnp.concatenate([material[1:].astype(jnp.float32), beyond], axis=0)
    stiff = 0.2 + 0.8 * jnp.repeat(solid, BZ, axis=2)

    bounds = level_set[:3], level_set[own_z - 3 :]
    even = place[0] == 1
    la = lax.ppermute(jnp.where(even, bounds[1], bounds[0]), "wide", wfirst)
    lb = lax.ppermute(jnp.where(even, bounds[0], bounds[1]), "wide", wsecond)

    inner, tail = inner_strain(displacement, yh)
    la, lb, inner = lax.optimization_barrier((la, lb, inner))
    tall, ya, yb = stack_level(place, level_set, la, lb)
    ya = lax.ppermute(ya, "narrow", nfirst)
    yb = lax.ppermute(yb, "narrow", nsecond)
    xh, ya, yb = lax.optimization_barrier((xh, ya, yb))
    message = strain_message(place, tail, xh, ch, inner, stiff, wide)
    message, tall = lax.optimization_barrier((message, tall))
    recv = lax.all_to_all(message.reshape(wide, 88, 128), "wide", split_axis=0, concat_axis=0, tiled=True)
    ls, sp, sm = first_gradient(place, tall, ya, yb)
    recv, sp = lax.optimization_barrier((recv, sp))
    tile, wide_peak, ma, mb = unpack(place, recv, own_z, rows)
    return level_part(place, tile, ma, mb, wide_peak, level_set, ls, sp, sm)


def solution(mesh):
    return jax.shard_map(
        per_device,
        mesh=mesh,
        in_specs=(
            P(None, None, "wide", "narrow", None),
            P("wide", "narrow", None),
            P("wide", "narrow", None),
        ),
        out_specs=(P("wide", "narrow", None), P("wide", "narrow", None)),
        check_vma=False,
    )
```

```python
import functools
import jax
import jax.numpy as jnp
from jax import lax
from jax.experimental import pallas as pl
from jax.experimental.pallas import tpu as pltpu
from jax.sharding import PartitionSpec as P

BZ = 16
EXT_PASSES = 4
HJ_STEPS = 3
SHEAR = 0.384615
LAME = 0.576923
WENO_EPS = 1e-06
TIME_STEP = 0.3
HALO = EXT_PASSES
GRAD_SCALE = 1.0 / (8.0 * 48.0 * 48.0)
YE = 10
Y1 = 6
Y2 = 3
VMEM_LIMIT = 48 * 1024 * 1024


def lane_shifts(value):
    blocks = [value[:, 128 * b : 128 * (b + 1)] for b in range(value.shape[1] // 128)]
    lane = lax.broadcasted_iota(jnp.int32, blocks[0].shape, 1)
    zero = jnp.zeros_like(blocks[0])
    outs = []
    for step in (-1, 1, 2):
        turned = [pltpu.roll(b, (-step) % 128, 1) for b in blocks]
        if step < 0:
            mask = lane < 1
            parts = [jnp.where(mask, turned[i - 1] if i > 0 else zero, turned[i]) for i in range(len(blocks))]
        else:
            mask = lane >= 128 - step
            parts = [
                jnp.where(mask, turned[i + 1] if i + 1 < len(blocks) else zero, turned[i])
                for i in range(len(blocks))
            ]
        outs.append(jnp.concatenate(parts, axis=1))
    return outs


def val4(a, b, c, d):
    return (a + d) + 23.0 * (b + c)


def der4(a, b, c, d):
    return (d - a) + 5.0 * (c - b)


def filter_plane(plane, filt, comp, layer, value, low, high0, high1):
    rows = value.shape[0]
    plane[8 : 8 + rows, :] = value
    plane[7:8, :] = low
    plane[8 + rows : 9 + rows, :] = high0
    plane[9 + rows : 10 + rows, :] = high1
    for tile in range(rows // 8):
        base = 8 + 8 * tile
        a = plane[base - 1 : base + 7, :]
        b = plane[base : base + 8, :]
        c = plane[base + 1 : base + 9, :]
        d = plane[base + 2 : base + 10, :]
        val_y = val4(a, b, c, d)
        der_y = der4(a, b, c, d)
        before, after, after2 = lane_shifts(val_y)
        span = pl.ds(8 * tile, 8)
        filt[comp, 0, layer, span, :] = val4(before, val_y, after, after2)
        filt[comp, 2, layer, span, :] = der4(before, val_y, after, after2)
        before, after, after2 = lane_shifts(der_y)
        filt[comp, 1, layer, span, :] = val4(before, der_y, after, after2)


def densities(field, rows, finish):
    for tile in range(rows // 8):
        span = pl.ds(8 * tile, 8)
        gx = [der4(*field(comp, 0, span)) for comp in range(3)]
        gy = [val4(*field(comp, 1, span)) for comp in range(3)]
        gz = [val4(*field(comp, 2, span)) for comp in range(3)]
        sxy = gy[0] + gx[1]
        sxz = gz[0] + gx[2]
        syz = gz[1] + gy[2]
        trace = gx[0] + gy[1] + gz[2]
        square = gx[0] * gx[0] + gy[1] * gy[1] + gz[2] * gz[2]
        shear = sxy * sxy + sxz * sxz + syz * syz
        scale = GRAD_SCALE * GRAD_SCALE
        finish(span, (SHEAR * scale) * (square + 0.5 * shear) + (0.5 * LAME * scale) * (trace * trace))


def accumulate(ref, slot):
    load = pl.program_id(0)

    def finish(span, density):
        @pl.when(load == 0)
        def _():
            ref[slot, span, :] = density

        @pl.when(load > 0)
        def _():
            ref[slot, span, :] += density

    return finish


def inner_kernel(u_ref, yh_ref, energy_ref, tail_ref, plane, filt):
    own_x, rows = u_ref.shape[2:4]

    def own_layer(layer, carry):
        for comp in range(3):
            edge = [yh_ref[0, comp, k, pl.ds(layer, 1), :] for k in range(3)]
            filter_plane(plane, filt, comp, layer, u_ref[0, comp, layer], *edge)
        return carry

    lax.fori_loop(0, own_x, own_layer, 0)

    def slot_step(slot, carry):
        field = lambda comp, which, span: [filt[comp, which, slot + k, span, :] for k in range(4)]
        densities(field, rows, accumulate(energy_ref, slot))
        return carry

    lax.fori_loop(0, own_x - 3, slot_step, 0)
    for comp in range(3):
        for which in range(3):
            for k in range(3):
                tail_ref[0, comp, which, k] = filt[comp, which, own_x - 3 + k]


def outer_kernel(place_ref, tail_ref, xh_ref, ch_ref, inner_ref, solid_ref, msg_ref, plane, filt, energy, turned):
    load = pl.program_id(0)
    rows, size_z = xh_ref.shape[3:5]
    own_x, _, blocks = solid_ref.shape
    inner = own_x - 3
    tiles = rows // 8
    keep = jnp.where(place_ref[2] == 1, 0.0, 1.0)
    for comp in range(3):
        for k in range(3):
            edge = [ch_ref[0, comp, which, k : k + 1, :] for which in range(3)]
            filter_plane(plane, filt, comp, k, xh_ref[0, comp, k], *edge)

    def density_at(slot, masked):
        def field(comp, which, span):
            out = []
            for k in range(4):
                at = slot + k
                value = tail_ref[0, comp, which, at, span, :] if at < 3 else filt[comp, which, at - 3, span, :]
                out.append(value * keep if masked[k] else value)
            return out

        densities(field, rows, accumulate(energy, slot))

    density_at(0, (False, False, False, True))
    density_at(1, (False, False, True, True))
    density_at(2, (True, False, False, False))

    @pl.when(load == pl.num_programs(0) - 1)
    def _():
        peak = jnp.zeros((8, 128), jnp.float32)
        groups = own_x // 4
        block_of = lax.broadcasted_iota(jnp.int32, (blocks, size_z), 1) // (size_z // blocks)
        spread = jnp.where(block_of == lax.broadcasted_iota(jnp.int32, (blocks, size_z), 0), 1.0, 0.0)
        for g in range(groups):
            stack = []
            for q in range(4):
                x = 4 * g + q
                solid = jnp.dot(solid_ref[x], spread, preferred_element_type=jnp.float32)
                value = (inner_ref[x] if x < inner else energy[x - inner]) * (0.2 + 0.8 * solid)
                stack.append(value)
                for tile in range(tiles):
                    for b in range(size_z // 128):
                        peak = jnp.maximum(peak, value[8 * tile : 8 * tile + 8, 128 * b : 128 * b + 128])
            turned[g, 0:8, :] = jnp.zeros((8, 128), jnp.float32)
            turned[g, size_z : size_z + 16, :] = jnp.zeros((16, 128), jnp.float32)
            turned[g, HALO : HALO + size_z, :] = jnp.concatenate(stack, axis=0).T
        peak = jnp.broadcast_to(jnp.max(peak, axis=0, keepdims=True), (8, 128))
        peak = jnp.broadcast_to(jnp.max(peak, axis=1, keepdims=True), (8, 128))
        parts = msg_ref.shape[0] // 88
        own_z = size_z // parts
        quads = (own_z + 2 * HALO) // 4
        lane = lax.broadcasted_iota(jnp.int32, (parts, 128), 1) // rows
        for g in range(groups):
            for j in range(quads):
                picked = [turned[g, pl.ds(4 * j + k, parts, stride=own_z), :] for k in range(4)]
                for q in range(4):
                    out = None
                    for k in range(4):
                        shift = (rows * (k - q)) % 128
                        part = pltpu.roll(picked[k], shift, 1) if shift else picked[k]
                        out = part if out is None else jnp.where(lane == k, part, out)
                    msg_ref[pl.ds(16 * j + 4 * g + q, parts, stride=88), :] = out
        for t in range(parts):
            msg_ref[pl.ds(88 * t + 80, 8), :] = peak


def load_block(*shape):
    return pl.BlockSpec((1,) + shape, lambda l: (l,) + (0,) * len(shape))


def fixed_block(*shape):
    return pl.BlockSpec(shape, lambda l: (0,) * len(shape))


def inner_strain(disp, yh):
    loads, comps, own_x, rows, size_z = disp.shape
    return pl.pallas_call(
        inner_kernel,
        grid=(loads,),
        out_shape=(
            jax.ShapeDtypeStruct((own_x - 3, rows, size_z), jnp.float32),
            jax.ShapeDtypeStruct((loads, comps, 3, 3, rows, size_z), jnp.float32),
        ),
        in_specs=[load_block(comps, own_x, rows, size_z), load_block(comps, 3, own_x, size_z)],
        out_specs=(fixed_block(own_x - 3, rows, size_z), load_block(comps, 3, 3, rows, size_z)),
        scratch_shapes=[
            pltpu.VMEM((rows + 16, size_z), jnp.float32),
            pltpu.VMEM((3, 3, own_x, rows, size_z), jnp.float32),
        ],
        compiler_params=pltpu.CompilerParams(vmem_limit_bytes=VMEM_LIMIT),
        cost_estimate=pl.CostEstimate(flops=40000 * 4096, bytes_accessed=1 << 20, transcendentals=0),
    )(disp, yh)


def strain_message(place, tail, xh, ch, inner, solid, parts):
    loads, comps = xh.shape[:2]
    own_x, rows, blocks = solid.shape
    size_z = xh.shape[4]
    return pl.pallas_call(
        outer_kernel,
        grid=(loads,),
        out_shape=jax.ShapeDtypeStruct((parts * 88, 128), jnp.float32),
        in_specs=[
            pl.BlockSpec(memory_space=pltpu.SMEM),
            load_block(comps, 3, 3, rows, size_z),
            load_block(comps, 3, rows, size_z),
            load_block(comps, 3, 3, size_z),
            fixed_block(own_x - 3, rows, size_z),
            fixed_block(own_x, rows, blocks),
        ],
        out_specs=fixed_block(parts * 88, 128),
        scratch_shapes=[
            pltpu.VMEM((rows + 16, size_z), jnp.float32),
            pltpu.VMEM((3, 3, 3, rows, size_z), jnp.float32),
            pltpu.VMEM((3, rows, size_z), jnp.float32),
            pltpu.VMEM((own_x // 4, size_z + 16, 128), jnp.float32),
        ],
        compiler_params=pltpu.CompilerParams(vmem_limit_bytes=VMEM_LIMIT),
        cost_estimate=pl.CostEstimate(flops=10000 * 4096, bytes_accessed=1 << 20, transcendentals=0),
    )(place, tail, xh, ch, inner, solid)


def ring(axis, step):
    count = lax.axis_size(axis)
    return [(i, i + step) for i in range(count) if 0 <= i + step < count]


def newton_reciprocal(x):
    r = pl.reciprocal(x, approx=True)
    return r * (2.0 - x * r)


def weno_cell(d, e0, e1, e2, e3):
    f0 = e1 - e0
    f1 = e2 - e1
    f2 = e3 - e2
    g0 = f1 - f0
    g1 = f2 - f1
    twice1 = e1 + e1
    twice2 = e2 + e2
    third = 13.0 / 3.0
    eps = 4.0 * WENO_EPS
    pa = twice1 + f0
    pb = twice1 + f1
    pc = twice2 - f2
    a = (f0 * f0 * third + eps) + pa * pa
    b = (f1 * f1 * third + eps) + pb * pb
    c = (f2 * f2 * third + eps) + pc * pc
    a = a * a
    b = b * b * (1.0 / 6.0)
    c = c * c
    ac = a * c
    ab = a * b
    cb = c * b
    u = cb * g0
    v = ab * g1
    both = u + v
    both = both + both
    s = e1 + e2
    d6 = 6.0 * d
    minus = d6 + (s + e2) - (both + v) * newton_reciprocal(ac + cb + 3.0 * ab)
    plus = (s + e1) - d6 - (both + u) * newton_reciprocal(ac + ab + 3.0 * cb)
    return minus, plus


def godunov(minus, plus):
    high = jnp.maximum(jnp.maximum(minus, plus), 0.0)
    low = jnp.minimum(jnp.minimum(minus, plus), 0.0)
    return high * high, low * low


def x_terms(phi):
    rows, size = phi.shape
    wide = size + 128
    phi = jnp.concatenate([phi, jnp.ones((rows, 128), jnp.float32)], axis=1)
    d = pltpu.roll(phi, wide - 1, 1) - phi
    e = pltpu.roll(d, wide - 1, 1) - d
    minus, plus = weno_cell(
        d, pltpu.roll(e, 2, 1), pltpu.roll(e, 1, 1), e, pltpu.roll(e, wide - 1, 1)
    )
    return godunov(pltpu.roll(minus, 1, 1)[:, :size], plus[:, :size])


def y_cells(ref, layer, row):
    p = [ref[layer, row + k : row + k + 8, :] for k in range(6)]
    d = [p[k + 1] - p[k] for k in range(5)]
    e = [d[k + 1] - d[k] for k in range(4)]
    return weno_cell(d[2], *e)


def xy_stage(phi_ref, offset, layer0, layers, gp_ref, gm_ref, exact=False):
    rows = gp_ref.shape[1]
    tiles = rows // 8

    def layer_step(z, carry):
        cells = [y_cells(phi_ref, z + layer0, 8 * t + offset - 3) for t in range(tiles)]
        turned = [pltpu.roll(c[1], 7, 0) for c in cells]
        if exact:
            start = min(rows + offset - 3, phi_ref.shape[1] - 13)
            extra = y_cells(phi_ref, z + layer0, start)[1]
            turned.append(pltpu.roll(extra, 7 - (rows + offset - 3 - start), 0))
        else:
            turned.append(turned[-1])
        row = lax.broadcasted_iota(jnp.int32, turned[0].shape, 0)
        for t in range(tiles):
            plus = jnp.where(row == 7, turned[t + 1], turned[t])
            yp, ym = godunov(cells[t][0], plus)
            xp, xm = x_terms(phi_ref[z + layer0, 8 * t + offset : 8 * t + offset + 8, :])
            gp_ref[z, 8 * t : 8 * t + 8, :] = xp + yp
            gm_ref[z, 8 * t : 8 * t + 8, :] = xm + ym
        return carry

    lax.fori_loop(0, layers, layer_step, 0)


def z_stage(get_phi, layers, rows, lanes, finish):
    def lane_step(block, carry):
        span = pl.ds(pl.multiple_of(128 * block, 128), 128)
        for t in range(rows // 8):
            p = [get_phi(z, t, span) for z in range(-3, layers + 3)]
            d = [p[k + 1] - p[k] for k in range(len(p) - 1)]
            e = [d[k + 1] - d[k] for k in range(len(d) - 1)]
            before = None
            for cell in range(layers + 1):
                minus, plus = weno_cell(d[cell + 2], e[cell], e[cell + 1], e[cell + 2], e[cell + 3])
                if before is not None:
                    finish(cell - 1, t, span, *godunov(before, plus))
                before = minus
        return carry

    lax.fori_loop(0, lanes // 128, lane_step, 0)


def first_gradient_kernel(place_ref, tall_ref, ra_ref, rb_ref, ls_ref, sp_ref, sm_ref):
    layers, rows, lanes = sp_ref.shape
    depth, own, _ = tall_ref.shape
    ones = jnp.ones((8, lanes), jnp.float32)

    def copy(z, carry):
        for t in range(ls_ref.shape[1] // 8):
            ls_ref[z, 8 * t : 8 * t + 8, :] = ones
        ls_ref[z, YE : YE + own, :] = tall_ref[z]
        return carry

    lax.fori_loop(0, depth, copy, 0)

    def below(ref):
        @pl.when(place_ref[4] == 0)
        def _():
            for z in range(depth):
                ls_ref[z, YE - 8 : YE, :] = ref[z]
                ls_ref[z, YE - 9 : YE - 8, :] = ref[depth + z // 8, z % 8 : z % 8 + 1, :]

    def above(ref):
        @pl.when(place_ref[5] == 0)
        def _():
            for z in range(depth):
                ls_ref[z, YE + own : YE + own + 8, :] = ref[z]
                ls_ref[z, YE + own + 8 : YE + own + 9, :] = ref[depth + z // 8, z % 8 : z % 8 + 1, :]

    @pl.when(place_ref[3] == 1)
    def _():
        above(ra_ref)
        below(rb_ref)

    @pl.when(place_ref[3] == 0)
    def _():
        below(ra_ref)
        above(rb_ref)

    offset = YE - Y1
    xy_stage(ls_ref, offset, 3, layers, sp_ref, sm_ref)

    def finish(z, t, span, gp, gm):
        where = pl.ds(8 * t, 8)
        scale = TIME_STEP / 6.0
        sp_ref[z, where, span] = scale * jnp.sqrt(sp_ref[z, where, span] + gp)
        sm_ref[z, where, span] = scale * jnp.sqrt(sm_ref[z, where, span] + gm)

    z_stage(
        lambda z, t, span: ls_ref[z + 3, 8 * t + offset : 8 * t + offset + 8, span], layers, rows, lanes, finish
    )


def vmem_call(kernel, outs, args, scratch=(), cycles=0):
    specs = []
    for arg in args:
        space = pltpu.SMEM if arg.dtype == jnp.int32 else pltpu.VMEM
        specs.append(pl.BlockSpec(memory_space=space))
    return pl.pallas_call(
        kernel,
        out_shape=tuple(jax.ShapeDtypeStruct(shape, jnp.float32) for shape in outs),
        in_specs=specs,
        out_specs=tuple(pl.BlockSpec(memory_space=pltpu.VMEM) for _ in outs),
        scratch_shapes=[pltpu.VMEM(shape, jnp.float32) for shape in scratch],
        compiler_params=pltpu.CompilerParams(vmem_limit_bytes=VMEM_LIMIT),
        cost_estimate=pl.CostEstimate(flops=cycles * 4096, bytes_accessed=1 << 20, transcendentals=0),
    )(*args)


def place_flags():
    wide, narrow = lax.axis_index("wide"), lax.axis_index("narrow")
    flags = [
        1 - wide % 2, wide == 0, wide == lax.axis_size("wide") - 1,
        1 - narrow % 2, narrow == 0, narrow == lax.axis_size("narrow") - 1,
    ]
    return jnp.stack([jnp.asarray(f).astype(jnp.int32) for f in flags])


def y_inside(place_ref, base, first_row, shape, rows):
    row = lax.broadcasted_iota(jnp.int32, shape, 0) + (first_row - base)
    inside = (row >= 0) | (place_ref[4] == 0)
    return inside & ((row < rows) | (place_ref[5] == 0))


def extend_kernel(
    place_ref, tile_ref, ra_ref, rb_ref, pa_ref, pb_ref, pc_ref, po_ref, ls_ref, sp_ref, sm_ref,
    speed_ref, speed6_ref, phi_ref, ma_ref, mb_ref, one, two, keep, pull,
):
    depth, rows, lanes = tile_ref.shape
    layers = depth - 2 * HALO
    tall = ls_ref.shape[1]
    margin = 8
    base = margin + YE
    peak = jnp.maximum(jnp.maximum(pa_ref[...], pb_ref[...]), jnp.maximum(pc_ref[...], po_ref[...]))
    scale = 1.0 / (peak[0:1, 0:1] + 1e-06)

    def assemble(z, carry):
        one[z, base : base + rows, :] = tile_ref[z]
        return carry

    lax.fori_loop(0, depth, assemble, 0)

    def below(ref):
        for z in range(depth):
            one[z, base - 8 : base, :] = ref[z]
            one[z, base - 10 : base - 8, :] = ref[depth + z // 4, 2 * (z % 4) : 2 * (z % 4) + 2, :]

    def above(ref):
        for z in range(depth):
            one[z, base + rows : base + rows + 8, :] = ref[z]
            one[z, base + rows + 8 : base + rows + 10, :] = ref[depth + z // 4, 2 * (z % 4) : 2 * (z % 4) + 2, :]

    @pl.when(place_ref[3] == 1)
    def _():
        above(ra_ref)
        below(rb_ref)

    @pl.when(place_ref[3] == 0)
    def _():
        below(ra_ref)
        above(rb_ref)

    def normalise(z, carry):
        outside = ((z < HALO) & (place_ref[1] == 1)) | ((z >= depth - HALO) & (place_ref[2] == 1))
        for t in range(tall // 8):
            at = slice(margin + 8 * t, margin + 8 * t + 8)
            ok = y_inside(place_ref, YE, 8 * t, (8, lanes), rows) & jnp.logical_not(outside)
            velocity = jnp.where(ok, one[z, at, :] * scale - 0.5, 0.0)
            one[z, at, :] = velocity

            @pl.when((z >= 1) & (z < depth - 1))
            def _():
                ls = ls_ref[z - 1, 8 * t : 8 * t + 8, :]
                weight = 1.0 / (1.0 + 4.0 * ls * ls)
                keep[z, 8 * t : 8 * t + 8, :] = weight * velocity
                pull[z, 8 * t : 8 * t + 8, :] = jnp.where(ok, (1.0 - weight) * (1.0 / 6.0), 0.0)

        return carry

    lax.fori_loop(0, depth, normalise, 0)
    for step in range(EXT_PASSES):
        source, target = (one, two) if step % 2 == 0 else (two, one)

        def extend(z, carry):
            for t in range(tall // 8):
                at = margin + 8 * t
                centre = source[z, at : at + 8, :]
                lane = lax.broadcasted_iota(jnp.int32, centre.shape, 1)
                total = source[z - 1, at : at + 8, :] + source[z + 1, at : at + 8, :]
                total = total + (source[z, at - 1 : at + 7, :] + source[z, at + 1 : at + 9, :])
                total = total + jnp.where(lane == 0, 0.0, pltpu.roll(centre, 1, 1))
                total = total + jnp.where(lane == lanes - 1, 0.0, pltpu.roll(centre, lanes - 1, 1))
                span = slice(8 * t, 8 * t + 8)
                target[z, at : at + 8, :] = keep[z, span, :] + pull[z, span, :] * total
            return carry

        lax.fori_loop(step + 1, depth - 1 - step, extend, 0)

    final = one if EXT_PASSES % 2 == 0 else two

    def march(z, carry):
        speed_ref[z] = final[z + HALO, base : base + rows, :]
        shift = YE - Y1
        for t in range(speed6_ref.shape[1] // 8):
            span = slice(8 * t, 8 * t + 8)
            speed = final[z + HALO, margin + shift + 8 * t : margin + shift + 8 * t + 8, :]
            speed6_ref[z, span, :] = speed
            change = jnp.maximum(speed, 0.0) * sp_ref[z, span, :] + jnp.minimum(speed, 0.0) * sm_ref[z, span, :]
            phi = ls_ref[z + 3, shift + 8 * t : shift + 8 * t + 8, :] - change
            phi_ref[z, span, :] = jnp.where(y_inside(place_ref, Y1, 8 * t, phi.shape, rows), phi, 1.0)
        return carry

    lax.fori_loop(0, layers, march, 0)
    send_edges(place_ref, phi_ref, Y1 - Y2, ma_ref, mb_ref)


def send_edges(place_ref, phi_ref, offset, ma_ref, mb_ref):
    layers = phi_ref.shape[0]
    count = ma_ref.shape[1]
    upper = place_ref[0] * (layers - 3)
    lower = (1 - place_ref[0]) * (layers - 3)
    for k in range(3):
        ma_ref[k] = phi_ref[upper + k, offset : offset + count, :]
        mb_ref[k] = phi_ref[lower + k, offset : offset + count, :]


def take_edges(place_ref, ra_ref, rb_ref, edges):
    upper = 3 * place_ref[0]
    lower = 3 - upper
    for k in range(3):
        edges[upper + k] = ra_ref[k]
        edges[lower + k] = rb_ref[k]

    @pl.when(place_ref[1] == 1)
    def _():
        edges[0:3] = jnp.ones((3,) + tuple(edges.shape[1:]), jnp.float32)

    @pl.when(place_ref[2] == 1)
    def _():
        edges[3:6] = jnp.ones((3,) + tuple(edges.shape[1:]), jnp.float32)


def plane_kernel(offset, exact, phi_ref, gp_ref, gm_ref):
    xy_stage(phi_ref, offset, 0, gp_ref.shape[0], gp_ref, gm_ref, exact)


def finish_kernel(
    offset, rows, place_ref, phi_ref, ra_ref, rb_ref, gp_ref, gm_ref, speed_ref, *rest
):
    out_ref, edges = rest[0], rest[-1]
    layers, count, lanes = out_ref.shape
    base = Y2 if count > rows else 0
    speed_offset = offset if count > rows else 0
    take_edges(place_ref, ra_ref, rb_ref, edges)

    def get_phi(z, t, span):
        if z < 0:
            return edges[z + 3, 8 * t : 8 * t + 8, span]
        if z >= layers:
            return edges[z - layers + 3, 8 * t : 8 * t + 8, span]
        return phi_ref[z, 8 * t + offset : 8 * t + offset + 8, span]

    def finish(z, t, span, gp, gm):
        where = pl.ds(8 * t, 8)
        speed = speed_ref[z, 8 * t + speed_offset : 8 * t + speed_offset + 8, span]
        total = jnp.where(speed > 0.0, gp_ref[z, where, span] + gp, gm_ref[z, where, span] + gm)
        phi = get_phi(z, t, span) - (TIME_STEP / 6.0) * speed * jnp.sqrt(total)
        if count > rows:
            phi = jnp.where(y_inside(place_ref, base, 8 * t, phi.shape, rows), phi, 1.0)
        out_ref[z, where, span] = phi

    z_stage(get_phi, layers, count, lanes, finish)
    if len(rest) > 2:
        send_edges(place_ref, out_ref, Y2, rest[1], rest[2])


def swaps(axis):
    count = lax.axis_size(axis)
    first, second = [], []
    for i in range(0, count, 2):
        first += [(i, i + 1), (i + 1, i)]
        j = (i + 2) % count
        second += [(i + 1, j), (j, i + 1)]
    return first, second


def stack_kernel(place_ref, ls_ref, ra_ref, rb_ref, tall_ref, ma_ref, mb_ref, edges):
    layers, rows = ls_ref.shape[:2]
    take_edges(place_ref, ra_ref, rb_ref, edges)
    for k in range(3):
        tall_ref[k] = edges[k]
        tall_ref[layers + 3 + k] = edges[3 + k]

    def copy(z, carry):
        tall_ref[z + 3] = ls_ref[z]
        return carry

    lax.fori_loop(0, layers, copy, 0)
    depth = layers + 6

    def upper(ref):
        for z in range(depth):
            ref[z] = tall_ref[z, rows - 8 : rows, :]
            ref[depth + z // 8, z % 8 : z % 8 + 1, :] = tall_ref[z, rows - 9 : rows - 8, :]

    def lower(ref):
        for z in range(depth):
            ref[z] = tall_ref[z, 0:8, :]
            ref[depth + z // 8, z % 8 : z % 8 + 1, :] = tall_ref[z, 8:9, :]

    @pl.when(place_ref[3] == 1)
    def _():
        upper(ma_ref)
        lower(mb_ref)

    @pl.when(place_ref[3] == 0)
    def _():
        lower(ma_ref)
        upper(mb_ref)


def level_part(place, tile, ma, mb, wide_peak, level_set, ls, sp, sm):
    layers, rows, lanes = level_set.shape
    nfirst, nsecond = swaps("narrow")
    wfirst, wsecond = swaps("wide")
    count = lax.axis_size("narrow")
    across = [(i, (i + count // 2) % count) for i in range(count)]
    ra = lax.ppermute(ma, "narrow", nfirst)
    rb = lax.ppermute(mb, "narrow", nsecond)
    pc = lax.ppermute(wide_peak, "narrow", across)
    pa, pb = ra[-1, :, :128], rb[-1, :, :128]
    tall = ls.shape[1]
    rows1 = -(-(rows + 2 * Y1) // 8) * 8
    rows2 = -(-(rows + 2 * Y2) // 8) * 8
    depth = layers + 2 * HALO
    speed, speed6, phi, sa, sb = vmem_call(
        extend_kernel,
        [(layers, rows, lanes), (layers, rows1, lanes), (layers, rows1, lanes), (3, rows2, lanes), (3, rows2, lanes)],
        (place, tile, ra, rb, pa, pb, pc, wide_peak, ls, sp, sm),
        [(depth, tall + 16, lanes)] * 2 + [(depth, tall, lanes)] * 2,
        8000,
    )
    ga = lax.ppermute(sa, "wide", wfirst)
    gb = lax.ppermute(sb, "wide", wsecond)
    gp, gm = vmem_call(functools.partial(plane_kernel, Y1 - Y2, False), [(layers, rows2, lanes)] * 2, (phi,), (), 12000)
    phi, sa, sb = vmem_call(
        functools.partial(finish_kernel, Y1 - Y2, rows),
        [(layers, rows2, lanes), (3, rows, lanes), (3, rows, lanes)],
        (place, phi, ga, gb, gp, gm, speed6),
        [(6, rows2, lanes)],
        5000,
    )
    ga = lax.ppermute(sa, "wide", wfirst)
    gb = lax.ppermute(sb, "wide", wsecond)
    gp, gm = vmem_call(functools.partial(plane_kernel, Y2, True), [(layers, rows, lanes)] * 2, (phi,), (), 12000)
    (phi,) = vmem_call(
        functools.partial(finish_kernel, Y2, rows),
        [(layers, rows, lanes)],
        (place, phi, ga, gb, gp, gm, speed),
        [(6, rows, lanes)],
        5000,
    )
    return phi, speed


def first_gradient(place, tall, ra, rb):
    depth, rows, lanes = tall.shape
    rows1 = -(-(rows + 2 * Y1) // 8) * 8
    total = -(-(rows + 2 * YE) // 8) * 8
    return vmem_call(
        first_gradient_kernel, [(depth, total, lanes)] + [(depth - 6, rows1, lanes)] * 2, (place, tall, ra, rb), (), 35000
    )


def stack_level(place, level_set, ra, rb):
    layers, rows, lanes = level_set.shape
    depth = layers + 6
    edge = (depth + -(-depth // 8), 8, lanes)
    return vmem_call(
        stack_kernel, [(depth, rows, lanes), edge, edge], (place, level_set, ra, rb), [(6, rows, lanes)], 1500
    )


def unpack_kernel(place_ref, recv_ref, tile_ref, peak_ref, ma_ref, mb_ref):
    parts = recv_ref.shape[0]
    depth, rows, lanes = tile_ref.shape
    for j in range(depth // 4):
        block = recv_ref[:, 16 * j : 16 * j + 16, :].reshape(parts * 16, 128)
        wide = pltpu.roll(block.T, 1, 1)
        for k in range(4):
            tile_ref[4 * j + k] = wide[rows * k : rows * (k + 1), :]
    peak = recv_ref[0, 80:88, :]
    for s in range(1, parts):
        peak = jnp.maximum(peak, recv_ref[s, 80:88, :])
    peak_ref[...] = peak
    fill_edges(place_ref, tile_ref, peak, ma_ref, mb_ref)


def fill_edges(place_ref, tile_ref, peak, ma_ref, mb_ref):
    depth, rows, lanes = tile_ref.shape

    def upper(ref):
        for z in range(depth):
            ref[z] = tile_ref[z, rows - 8 : rows, :]
            ref[depth + z // 4, 2 * (z % 4) : 2 * (z % 4) + 2, :] = tile_ref[z, rows - 10 : rows - 8, :]

    def lower(ref):
        for z in range(depth):
            ref[z] = tile_ref[z, 0:8, :]
            ref[depth + z // 4, 2 * (z % 4) : 2 * (z % 4) + 2, :] = tile_ref[z, 8:10, :]

    last = ma_ref.shape[0] - 1
    ma_ref[last, :, 0:128] = peak
    mb_ref[last, :, 0:128] = peak

    @pl.when(place_ref[3] == 1)
    def _():
        upper(ma_ref)
        lower(mb_ref)

    @pl.when(place_ref[3] == 0)
    def _():
        lower(ma_ref)
        upper(mb_ref)


def unpack(place, recv, own_z, rows):
    parts = recv.shape[0]
    lanes = parts * 16
    depth = own_z + 2 * HALO
    edge = (depth + depth // 4 + 1, 8, lanes)
    return vmem_call(
        unpack_kernel, [(depth, rows, lanes), (8, 128), edge, edge], (place, recv), (), 1500
    )


def per_device(displacement, material, level_set):
    wide = lax.axis_size("wide")
    loads, comps, own_x, rows, size_z = displacement.shape
    own_z, _, size_x = level_set.shape
    place = place_flags()
    backward = [(i, (i - 1) % wide) for i in range(wide)]
    wfirst, wsecond = swaps("wide")
    nfirst, nsecond = swaps("narrow")

    low = lax.ppermute(displacement[:, :, :, -1], "narrow", ring("narrow", 1))
    high = lax.ppermute(
        jnp.stack([displacement[:, :, :, 0], displacement[:, :, :, 1]], axis=2), "narrow", ring("narrow", -1)
    )
    yh = jnp.concatenate([low[:, :, None], high], axis=2)
    blocks = material.shape[2]
    corner = yh[:, :, :, :3].reshape(loads * comps * 3, 3, size_z)
    first = material[0].astype(jnp.float32).reshape(-1)
    first = jnp.pad(first, (0, 3 * size_z - first.size)).reshape(1, 3, size_z)
    got = lax.ppermute(jnp.concatenate([corner, first], axis=0), "wide", backward)
    ch = got[: loads * comps * 3].reshape(loads, comps, 3, 3, size_z)
    beyond = got[loads * comps * 3].reshape(-1)[: rows * blocks].reshape(1, rows, blocks)
    solid = jnp.concatenate([material[1:].astype(jnp.float32), beyond], axis=0)

    bounds = level_set[:3], level_set[own_z - 3 :]
    even = place[0] == 1
    la = lax.ppermute(jnp.where(even, bounds[1], bounds[0]), "wide", wfirst)
    lb = lax.ppermute(jnp.where(even, bounds[0], bounds[1]), "wide", wsecond)

    layers, yh, ch, la, lb = lax.optimization_barrier((displacement[:, :, :3], yh, ch, la, lb))
    xh = lax.ppermute(layers, "wide", backward)
    inner, tail = inner_strain(displacement, yh)
    la, lb, inner = lax.optimization_barrier((la, lb, inner))
    tall, ya, yb = stack_level(place, level_set, la, lb)
    ya = lax.ppermute(ya, "narrow", nfirst)
    yb = lax.ppermute(yb, "narrow", nsecond)
    xh, tall = lax.optimization_barrier((xh, tall))
    message = strain_message(place, tail, xh, ch, inner, solid, wide)
    message, tall = lax.optimization_barrier((message, tall))
    recv = lax.all_to_all(message.reshape(wide, 88, 128), "wide", split_axis=0, concat_axis=0, tiled=True)
    ls, sp, sm = first_gradient(place, tall, ya, yb)
    recv, sp = lax.optimization_barrier((recv, sp))
    tile, wide_peak, ma, mb = unpack(place, recv, own_z, rows)
    return level_part(place, tile, ma, mb, wide_peak, level_set, ls, sp, sm)


def solution(mesh):
    return jax.shard_map(
        per_device,
        mesh=mesh,
        in_specs=(
            P(None, None, "wide", "narrow", None),
            P("wide", "narrow", None),
            P("wide", "narrow", None),
        ),
        out_specs=(P("wide", "narrow", None), P("wide", "narrow", None)),
        check_vma=False,
    )
```

```python
import functools
import jax
import jax.numpy as jnp
from jax import lax
from jax.experimental import pallas as pl
from jax.experimental.pallas import tpu as pltpu
from jax.sharding import PartitionSpec as P

BZ = 16
EXT_PASSES = 4
HJ_STEPS = 3
SHEAR = 0.384615
LAME = 0.576923
WENO_EPS = 1e-06
TIME_STEP = 0.3
HALO = EXT_PASSES
GRAD_SCALE = 1.0 / (8.0 * 48.0 * 48.0)
YE = 10
Y1 = 6
Y2 = 3
VMEM_LIMIT = 48 * 1024 * 1024


def lane_shifts(value):
    blocks = [value[:, 128 * b : 128 * (b + 1)] for b in range(value.shape[1] // 128)]
    lane = lax.broadcasted_iota(jnp.int32, blocks[0].shape, 1)
    zero = jnp.zeros_like(blocks[0])
    outs = []
    for step in (-1, 1, 2):
        turned = [pltpu.roll(b, (-step) % 128, 1) for b in blocks]
        if step < 0:
            mask = lane < 1
            parts = [jnp.where(mask, turned[i - 1] if i > 0 else zero, turned[i]) for i in range(len(blocks))]
        else:
            mask = lane >= 128 - step
            parts = [
                jnp.where(mask, turned[i + 1] if i + 1 < len(blocks) else zero, turned[i])
                for i in range(len(blocks))
            ]
        outs.append(jnp.concatenate(parts, axis=1))
    return outs


def val4(a, b, c, d):
    return (a + d) + 23.0 * (b + c)


def der4(a, b, c, d):
    return (d - a) + 5.0 * (c - b)


def filter_plane(plane, filt, comp, layer, value, low, high0, high1):
    rows = value.shape[0]
    plane[8 : 8 + rows, :] = value
    plane[7:8, :] = low
    plane[8 + rows : 9 + rows, :] = high0
    plane[9 + rows : 10 + rows, :] = high1
    for tile in range(rows // 8):
        base = 8 + 8 * tile
        a = plane[base - 1 : base + 7, :]
        b = plane[base : base + 8, :]
        c = plane[base + 1 : base + 9, :]
        d = plane[base + 2 : base + 10, :]
        val_y = val4(a, b, c, d)
        der_y = der4(a, b, c, d)
        before, after, after2 = lane_shifts(val_y)
        span = pl.ds(8 * tile, 8)
        filt[comp, 0, layer, span, :] = val4(before, val_y, after, after2)
        filt[comp, 2, layer, span, :] = der4(before, val_y, after, after2)
        before, after, after2 = lane_shifts(der_y)
        filt[comp, 1, layer, span, :] = val4(before, der_y, after, after2)


def densities(field, rows, finish):
    for tile in range(rows // 8):
        span = pl.ds(8 * tile, 8)
        gx = [der4(*field(comp, 0, span)) for comp in range(3)]
        gy = [val4(*field(comp, 1, span)) for comp in range(3)]
        gz = [val4(*field(comp, 2, span)) for comp in range(3)]
        sxy = gy[0] + gx[1]
        sxz = gz[0] + gx[2]
        syz = gz[1] + gy[2]
        trace = gx[0] + gy[1] + gz[2]
        square = gx[0] * gx[0] + gy[1] * gy[1] + gz[2] * gz[2]
        shear = sxy * sxy + sxz * sxz + syz * syz
        scale = GRAD_SCALE * GRAD_SCALE
        finish(span, (SHEAR * scale) * (square + 0.5 * shear) + (0.5 * LAME * scale) * (trace * trace))


def accumulate(ref, slot):
    load = pl.program_id(0)

    def finish(span, density):
        @pl.when(load == 0)
        def _():
            ref[slot, span, :] = density

        @pl.when(load > 0)
        def _():
            ref[slot, span, :] += density

    return finish


def inner_kernel(u_ref, yh_ref, energy_ref, tail_ref, plane, filt):
    own_x, rows = u_ref.shape[2:4]

    def own_layer(layer, carry):
        for comp in range(3):
            edge = [yh_ref[0, comp, k, pl.ds(layer, 1), :] for k in range(3)]
            filter_plane(plane, filt, comp, layer, u_ref[0, comp, layer], *edge)
        return carry

    lax.fori_loop(0, own_x, own_layer, 0)

    def slot_step(slot, carry):
        field = lambda comp, which, span: [filt[comp, which, slot + k, span, :] for k in range(4)]
        densities(field, rows, accumulate(energy_ref, slot))
        return carry

    lax.fori_loop(0, own_x - 3, slot_step, 0)
    for comp in range(3):
        for which in range(3):
            for k in range(3):
                tail_ref[0, comp, which, k] = filt[comp, which, own_x - 3 + k]


def outer_kernel(place_ref, tail_ref, next_ref, inner_ref, solid_ref, msg_ref, plane, filt, energy, turned):
    load = pl.program_id(0)
    own_x, rows, blocks = solid_ref.shape
    size_z = next_ref.shape[1]
    loads = 3
    inner = own_x - 3
    tiles = rows // 8
    keep = jnp.where(place_ref[2] == 1, 0.0, 1.0)
    for comp in range(3):
        for k in range(3):
            layer = (load * 3 + comp) * 3 + k
            corner = loads * 9 * rows + rows
            edge = [next_ref[pl.ds(corner + (load * 3 + comp) * 9 + 3 * which + k, 1), :] for which in range(3)]
            value = next_ref[pl.ds(pl.multiple_of(layer * rows, 8), rows), :]
            filter_plane(plane, filt, comp, k, value, *edge)

    def density_at(slot, masked):
        def field(comp, which, span):
            out = []
            for k in range(4):
                at = slot + k
                value = tail_ref[0, comp, which, at, span, :] if at < 3 else filt[comp, which, at - 3, span, :]
                out.append(value * keep if masked[k] else value)
            return out

        densities(field, rows, accumulate(energy, slot))

    density_at(0, (False, False, False, True))
    density_at(1, (False, False, True, True))
    density_at(2, (True, False, False, False))

    @pl.when(load == pl.num_programs(0) - 1)
    def _():
        peak = jnp.zeros((8, 128), jnp.float32)
        groups = own_x // 4
        block_of = lax.broadcasted_iota(jnp.int32, (blocks, size_z), 1) // (size_z // blocks)
        spread = jnp.where(block_of == lax.broadcasted_iota(jnp.int32, (blocks, size_z), 0), 1.0, 0.0)
        for g in range(groups):
            stack = []
            for q in range(4):
                x = 4 * g + q
                if x < own_x - 1:
                    solid = jnp.dot(solid_ref[x + 1].astype(jnp.float32), spread, preferred_element_type=jnp.float32)
                    stiff = 0.2 + 0.8 * solid
                else:
                    stiff = next_ref[loads * 9 * rows : loads * 9 * rows + rows, :]
                value = (inner_ref[x] if x < inner else energy[x - inner]) * stiff
                stack.append(value)
                for tile in range(tiles):
                    for b in range(size_z // 128):
                        peak = jnp.maximum(peak, value[8 * tile : 8 * tile + 8, 128 * b : 128 * b + 128])
            turned[g, 0:8, :] = jnp.zeros((8, 128), jnp.float32)
            turned[g, size_z : size_z + 16, :] = jnp.zeros((16, 128), jnp.float32)
            turned[g, HALO : HALO + size_z, :] = jnp.concatenate(stack, axis=0).T
        peak = jnp.broadcast_to(jnp.max(peak, axis=0, keepdims=True), (8, 128))
        peak = jnp.broadcast_to(jnp.max(peak, axis=1, keepdims=True), (8, 128))
        parts = msg_ref.shape[0] // 88
        own_z = size_z // parts
        quads = (own_z + 2 * HALO) // 4
        lane = lax.broadcasted_iota(jnp.int32, (parts, 128), 1) // rows
        for g in range(groups):
            for j in range(quads):
                picked = [turned[g, pl.ds(4 * j + k, parts, stride=own_z), :] for k in range(4)]
                for q in range(4):
                    out = None
                    for k in range(4):
                        shift = (rows * (k - q)) % 128
                        part = pltpu.roll(picked[k], shift, 1) if shift else picked[k]
                        out = part if out is None else jnp.where(lane == k, part, out)
                    msg_ref[pl.ds(16 * j + 4 * g + q, parts, stride=88), :] = out
        for t in range(parts):
            msg_ref[pl.ds(88 * t + 80, 8), :] = peak


def load_block(*shape):
    return pl.BlockSpec((1,) + shape, lambda l: (l,) + (0,) * len(shape))


def fixed_block(*shape):
    return pl.BlockSpec(shape, lambda l: (0,) * len(shape))


def inner_strain(disp, yh):
    loads, comps, own_x, rows, size_z = disp.shape
    return pl.pallas_call(
        inner_kernel,
        grid=(loads,),
        out_shape=(
            jax.ShapeDtypeStruct((own_x - 3, rows, size_z), jnp.float32),
            jax.ShapeDtypeStruct((loads, comps, 3, 3, rows, size_z), jnp.float32),
        ),
        in_specs=[load_block(comps, own_x, rows, size_z), load_block(comps, 3, own_x, size_z)],
        out_specs=(fixed_block(own_x - 3, rows, size_z), load_block(comps, 3, 3, rows, size_z)),
        scratch_shapes=[
            pltpu.VMEM((rows + 16, size_z), jnp.float32),
            pltpu.VMEM((3, 3, own_x, rows, size_z), jnp.float32),
        ],
        compiler_params=pltpu.CompilerParams(vmem_limit_bytes=VMEM_LIMIT),
        cost_estimate=pl.CostEstimate(flops=40000 * 4096, bytes_accessed=1 << 20, transcendentals=0),
    )(disp, yh)


def strain_message(place, tail, beyond, inner, solid, parts):
    loads, comps = tail.shape[:2]
    own_x, rows, blocks = solid.shape
    size_z = beyond.shape[1]
    return pl.pallas_call(
        outer_kernel,
        grid=(loads,),
        out_shape=jax.ShapeDtypeStruct((parts * 88, 128), jnp.float32),
        in_specs=[
            pl.BlockSpec(memory_space=pltpu.SMEM),
            load_block(comps, 3, 3, rows, size_z),
            fixed_block(*beyond.shape),
            fixed_block(own_x - 3, rows, size_z),
            fixed_block(own_x, rows, blocks),
        ],
        out_specs=fixed_block(parts * 88, 128),
        scratch_shapes=[
            pltpu.VMEM((rows + 16, size_z), jnp.float32),
            pltpu.VMEM((3, 3, 3, rows, size_z), jnp.float32),
            pltpu.VMEM((3, rows, size_z), jnp.float32),
            pltpu.VMEM((own_x // 4, size_z + 16, 128), jnp.float32),
        ],
        compiler_params=pltpu.CompilerParams(vmem_limit_bytes=VMEM_LIMIT),
        cost_estimate=pl.CostEstimate(flops=10000 * 4096, bytes_accessed=1 << 20, transcendentals=0),
    )(place, tail, beyond, inner, solid)


def ring(axis, step):
    count = lax.axis_size(axis)
    return [(i, i + step) for i in range(count) if 0 <= i + step < count]


def newton_reciprocal(x):
    r = pl.reciprocal(x, approx=True)
    return r * (2.0 - x * r)


def weno_cell(d, e0, e1, e2, e3):
    f0 = e1 - e0
    f1 = e2 - e1
    f2 = e3 - e2
    g0 = f1 - f0
    g1 = f2 - f1
    twice1 = e1 + e1
    twice2 = e2 + e2
    third = 13.0 / 3.0
    eps = 4.0 * WENO_EPS
    pa = twice1 + f0
    pb = twice1 + f1
    pc = twice2 - f2
    a = (f0 * f0 * third + eps) + pa * pa
    b = (f1 * f1 * third + eps) + pb * pb
    c = (f2 * f2 * third + eps) + pc * pc
    a = a * a
    b = b * b * (1.0 / 6.0)
    c = c * c
    ac = a * c
    ab = a * b
    cb = c * b
    u = cb * g0
    v = ab * g1
    both = u + v
    both = both + both
    s = e1 + e2
    d6 = 6.0 * d
    minus = d6 + (s + e2) - (both + v) * newton_reciprocal(ac + cb + 3.0 * ab)
    plus = (s + e1) - d6 - (both + u) * newton_reciprocal(ac + ab + 3.0 * cb)
    return minus, plus


def godunov(minus, plus):
    high = jnp.maximum(jnp.maximum(minus, plus), 0.0)
    low = jnp.minimum(jnp.minimum(minus, plus), 0.0)
    return high * high, low * low


def x_terms(phi):
    rows, size = phi.shape
    wide = size + 128
    phi = jnp.concatenate([phi, jnp.ones((rows, 128), jnp.float32)], axis=1)
    d = pltpu.roll(phi, wide - 1, 1) - phi
    e = pltpu.roll(d, wide - 1, 1) - d
    minus, plus = weno_cell(
        d, pltpu.roll(e, 2, 1), pltpu.roll(e, 1, 1), e, pltpu.roll(e, wide - 1, 1)
    )
    return godunov(pltpu.roll(minus, 1, 1)[:, :size], plus[:, :size])


def y_cells(ref, layer, row):
    p = [ref[layer, row + k : row + k + 8, :] for k in range(6)]
    d = [p[k + 1] - p[k] for k in range(5)]
    e = [d[k + 1] - d[k] for k in range(4)]
    return weno_cell(d[2], *e)


def xy_stage(phi_ref, offset, layer0, layers, gp_ref, gm_ref, exact=False):
    rows = gp_ref.shape[1]
    tiles = rows // 8

    def layer_step(z, carry):
        cells = [y_cells(phi_ref, z + layer0, 8 * t + offset - 3) for t in range(tiles)]
        turned = [pltpu.roll(c[1], 7, 0) for c in cells]
        if exact:
            start = min(rows + offset - 3, phi_ref.shape[1] - 13)
            extra = y_cells(phi_ref, z + layer0, start)[1]
            turned.append(pltpu.roll(extra, 7 - (rows + offset - 3 - start), 0))
        else:
            turned.append(turned[-1])
        row = lax.broadcasted_iota(jnp.int32, turned[0].shape, 0)
        for t in range(tiles):
            plus = jnp.where(row == 7, turned[t + 1], turned[t])
            yp, ym = godunov(cells[t][0], plus)
            xp, xm = x_terms(phi_ref[z + layer0, 8 * t + offset : 8 * t + offset + 8, :])
            gp_ref[z, 8 * t : 8 * t + 8, :] = xp + yp
            gm_ref[z, 8 * t : 8 * t + 8, :] = xm + ym
        return carry

    lax.fori_loop(0, layers, layer_step, 0)


def z_stage(get_phi, layers, rows, lanes, finish):
    def lane_step(block, carry):
        span = pl.ds(pl.multiple_of(128 * block, 128), 128)
        for t in range(rows // 8):
            p = [get_phi(z, t, span) for z in range(-3, layers + 3)]
            d = [p[k + 1] - p[k] for k in range(len(p) - 1)]
            e = [d[k + 1] - d[k] for k in range(len(d) - 1)]
            before = None
            for cell in range(layers + 1):
                minus, plus = weno_cell(d[cell + 2], e[cell], e[cell + 1], e[cell + 2], e[cell + 3])
                if before is not None:
                    finish(cell - 1, t, span, *godunov(before, plus))
                before = minus
        return carry

    lax.fori_loop(0, lanes // 128, lane_step, 0)


def first_gradient_kernel(place_ref, tall_ref, ra_ref, rb_ref, ls_ref, sp_ref, sm_ref):
    layers, rows, lanes = sp_ref.shape
    depth, own, _ = tall_ref.shape
    ones = jnp.ones((8, lanes), jnp.float32)

    def copy(z, carry):
        for t in range(ls_ref.shape[1] // 8):
            ls_ref[z, 8 * t : 8 * t + 8, :] = ones
        ls_ref[z, YE : YE + own, :] = tall_ref[z]
        return carry

    lax.fori_loop(0, depth, copy, 0)

    def below(ref):
        @pl.when(place_ref[4] == 0)
        def _():
            for z in range(depth):
                ls_ref[z, YE - 8 : YE, :] = ref[z]
                ls_ref[z, YE - 9 : YE - 8, :] = ref[depth + z // 8, z % 8 : z % 8 + 1, :]

    def above(ref):
        @pl.when(place_ref[5] == 0)
        def _():
            for z in range(depth):
                ls_ref[z, YE + own : YE + own + 8, :] = ref[z]
                ls_ref[z, YE + own + 8 : YE + own + 9, :] = ref[depth + z // 8, z % 8 : z % 8 + 1, :]

    @pl.when(place_ref[3] == 1)
    def _():
        above(ra_ref)
        below(rb_ref)

    @pl.when(place_ref[3] == 0)
    def _():
        below(ra_ref)
        above(rb_ref)

    offset = YE - Y1
    xy_stage(ls_ref, offset, 3, layers, sp_ref, sm_ref)

    def finish(z, t, span, gp, gm):
        where = pl.ds(8 * t, 8)
        scale = TIME_STEP / 6.0
        sp_ref[z, where, span] = scale * jnp.sqrt(sp_ref[z, where, span] + gp)
        sm_ref[z, where, span] = scale * jnp.sqrt(sm_ref[z, where, span] + gm)

    z_stage(
        lambda z, t, span: ls_ref[z + 3, 8 * t + offset : 8 * t + offset + 8, span], layers, rows, lanes, finish
    )


def vmem_call(kernel, outs, args, scratch=(), cycles=0):
    specs = []
    for arg in args:
        space = pltpu.SMEM if arg.dtype == jnp.int32 else pltpu.VMEM
        specs.append(pl.BlockSpec(memory_space=space))
    return pl.pallas_call(
        kernel,
        out_shape=tuple(jax.ShapeDtypeStruct(shape, jnp.float32) for shape in outs),
        in_specs=specs,
        out_specs=tuple(pl.BlockSpec(memory_space=pltpu.VMEM) for _ in outs),
        scratch_shapes=[pltpu.VMEM(shape, jnp.float32) for shape in scratch],
        compiler_params=pltpu.CompilerParams(vmem_limit_bytes=VMEM_LIMIT),
        cost_estimate=pl.CostEstimate(flops=cycles * 4096, bytes_accessed=1 << 20, transcendentals=0),
    )(*args)


def place_flags():
    wide, narrow = lax.axis_index("wide"), lax.axis_index("narrow")
    flags = [
        1 - wide % 2, wide == 0, wide == lax.axis_size("wide") - 1,
        1 - narrow % 2, narrow == 0, narrow == lax.axis_size("narrow") - 1,
    ]
    return jnp.stack([jnp.asarray(f).astype(jnp.int32) for f in flags])


def y_inside(place_ref, base, first_row, shape, rows):
    row = lax.broadcasted_iota(jnp.int32, shape, 0) + (first_row - base)
    inside = (row >= 0) | (place_ref[4] == 0)
    return inside & ((row < rows) | (place_ref[5] == 0))


def extend_kernel(
    place_ref, tile_ref, ra_ref, rb_ref, pa_ref, pb_ref, pc_ref, po_ref, ls_ref, sp_ref, sm_ref,
    speed_ref, speed6_ref, phi_ref, ma_ref, mb_ref, one, two, keep, pull,
):
    depth, rows, lanes = tile_ref.shape
    layers = depth - 2 * HALO
    tall = ls_ref.shape[1]
    margin = 8
    base = margin + YE
    peak = jnp.maximum(jnp.maximum(pa_ref[...], pb_ref[...]), jnp.maximum(pc_ref[...], po_ref[...]))
    scale = 1.0 / (peak[0:1, 0:1] + 1e-06)

    def assemble(z, carry):
        one[z, base : base + rows, :] = tile_ref[z]
        return carry

    lax.fori_loop(0, depth, assemble, 0)

    def below(ref):
        for z in range(depth):
            one[z, base - 8 : base, :] = ref[z]
            one[z, base - 10 : base - 8, :] = ref[depth + z // 4, 2 * (z % 4) : 2 * (z % 4) + 2, :]

    def above(ref):
        for z in range(depth):
            one[z, base + rows : base + rows + 8, :] = ref[z]
            one[z, base + rows + 8 : base + rows + 10, :] = ref[depth + z // 4, 2 * (z % 4) : 2 * (z % 4) + 2, :]

    @pl.when(place_ref[3] == 1)
    def _():
        above(ra_ref)
        below(rb_ref)

    @pl.when(place_ref[3] == 0)
    def _():
        below(ra_ref)
        above(rb_ref)

    def normalise(z, carry):
        outside = ((z < HALO) & (place_ref[1] == 1)) | ((z >= depth - HALO) & (place_ref[2] == 1))
        for t in range(tall // 8):
            at = slice(margin + 8 * t, margin + 8 * t + 8)
            ok = y_inside(place_ref, YE, 8 * t, (8, lanes), rows) & jnp.logical_not(outside)
            velocity = jnp.where(ok, one[z, at, :] * scale - 0.5, 0.0)
            one[z, at, :] = velocity

            @pl.when((z >= 1) & (z < depth - 1))
            def _():
                ls = ls_ref[z - 1, 8 * t : 8 * t + 8, :]
                weight = 1.0 / (1.0 + 4.0 * ls * ls)
                keep[z, 8 * t : 8 * t + 8, :] = weight * velocity
                pull[z, 8 * t : 8 * t + 8, :] = jnp.where(ok, (1.0 - weight) * (1.0 / 6.0), 0.0)

        return carry

    lax.fori_loop(0, depth, normalise, 0)
    for step in range(EXT_PASSES):
        source, target = (one, two) if step % 2 == 0 else (two, one)

        def extend(z, carry):
            for t in range(tall // 8):
                at = margin + 8 * t
                centre = source[z, at : at + 8, :]
                lane = lax.broadcasted_iota(jnp.int32, centre.shape, 1)
                total = source[z - 1, at : at + 8, :] + source[z + 1, at : at + 8, :]
                total = total + (source[z, at - 1 : at + 7, :] + source[z, at + 1 : at + 9, :])
                total = total + jnp.where(lane == 0, 0.0, pltpu.roll(centre, 1, 1))
                total = total + jnp.where(lane == lanes - 1, 0.0, pltpu.roll(centre, lanes - 1, 1))
                span = slice(8 * t, 8 * t + 8)
                target[z, at : at + 8, :] = keep[z, span, :] + pull[z, span, :] * total
            return carry

        lax.fori_loop(step + 1, depth - 1 - step, extend, 0)

    final = one if EXT_PASSES % 2 == 0 else two

    def march(z, carry):
        speed_ref[z] = final[z + HALO, base : base + rows, :]
        shift = YE - Y1
        for t in range(speed6_ref.shape[1] // 8):
            span = slice(8 * t, 8 * t + 8)
            speed = final[z + HALO, margin + shift + 8 * t : margin + shift + 8 * t + 8, :]
            speed6_ref[z, span, :] = speed
            change = jnp.maximum(speed, 0.0) * sp_ref[z, span, :] + jnp.minimum(speed, 0.0) * sm_ref[z, span, :]
            phi = ls_ref[z + 3, shift + 8 * t : shift + 8 * t + 8, :] - change
            phi_ref[z, span, :] = jnp.where(y_inside(place_ref, Y1, 8 * t, phi.shape, rows), phi, 1.0)
        return carry

    lax.fori_loop(0, layers, march, 0)
    send_edges(place_ref, phi_ref, Y1 - Y2, ma_ref, mb_ref)


def send_edges(place_ref, phi_ref, offset, ma_ref, mb_ref):
    layers = phi_ref.shape[0]
    count = ma_ref.shape[1]
    upper = place_ref[0] * (layers - 3)
    lower = (1 - place_ref[0]) * (layers - 3)
    for k in range(3):
        ma_ref[k] = phi_ref[upper + k, offset : offset + count, :]
        mb_ref[k] = phi_ref[lower + k, offset : offset + count, :]


def take_edges(place_ref, ra_ref, rb_ref, edges):
    upper = 3 * place_ref[0]
    lower = 3 - upper
    for k in range(3):
        edges[upper + k] = ra_ref[k]
        edges[lower + k] = rb_ref[k]

    @pl.when(place_ref[1] == 1)
    def _():
        edges[0:3] = jnp.ones((3,) + tuple(edges.shape[1:]), jnp.float32)

    @pl.when(place_ref[2] == 1)
    def _():
        edges[3:6] = jnp.ones((3,) + tuple(edges.shape[1:]), jnp.float32)


def plane_kernel(offset, exact, phi_ref, gp_ref, gm_ref):
    xy_stage(phi_ref, offset, 0, gp_ref.shape[0], gp_ref, gm_ref, exact)


def finish_kernel(
    offset, rows, place_ref, phi_ref, ra_ref, rb_ref, gp_ref, gm_ref, speed_ref, *rest
):
    out_ref, edges = rest[0], rest[-1]
    layers, count, lanes = out_ref.shape
    base = Y2 if count > rows else 0
    speed_offset = offset if count > rows else 0
    take_edges(place_ref, ra_ref, rb_ref, edges)

    def get_phi(z, t, span):
        if z < 0:
            return edges[z + 3, 8 * t : 8 * t + 8, span]
        if z >= layers:
            return edges[z - layers + 3, 8 * t : 8 * t + 8, span]
        return phi_ref[z, 8 * t + offset : 8 * t + offset + 8, span]

    def finish(z, t, span, gp, gm):
        where = pl.ds(8 * t, 8)
        speed = speed_ref[z, 8 * t + speed_offset : 8 * t + speed_offset + 8, span]
        total = jnp.where(speed > 0.0, gp_ref[z, where, span] + gp, gm_ref[z, where, span] + gm)
        phi = get_phi(z, t, span) - (TIME_STEP / 6.0) * speed * jnp.sqrt(total)
        if count > rows:
            phi = jnp.where(y_inside(place_ref, base, 8 * t, phi.shape, rows), phi, 1.0)
        out_ref[z, where, span] = phi

    z_stage(get_phi, layers, count, lanes, finish)
    if len(rest) > 2:
        send_edges(place_ref, out_ref, Y2, rest[1], rest[2])


def swaps(axis):
    count = lax.axis_size(axis)
    first, second = [], []
    for i in range(0, count, 2):
        first += [(i, i + 1), (i + 1, i)]
        j = (i + 2) % count
        second += [(i + 1, j), (j, i + 1)]
    return first, second


def stack_kernel(place_ref, ls_ref, ra_ref, rb_ref, tall_ref, ma_ref, mb_ref, edges):
    layers, rows = ls_ref.shape[:2]
    take_edges(place_ref, ra_ref, rb_ref, edges)
    for k in range(3):
        tall_ref[k] = edges[k]
        tall_ref[layers + 3 + k] = edges[3 + k]

    def copy(z, carry):
        tall_ref[z + 3] = ls_ref[z]
        return carry

    lax.fori_loop(0, layers, copy, 0)
    depth = layers + 6

    def upper(ref):
        for z in range(depth):
            ref[z] = tall_ref[z, rows - 8 : rows, :]
            ref[depth + z // 8, z % 8 : z % 8 + 1, :] = tall_ref[z, rows - 9 : rows - 8, :]

    def lower(ref):
        for z in range(depth):
            ref[z] = tall_ref[z, 0:8, :]
            ref[depth + z // 8, z % 8 : z % 8 + 1, :] = tall_ref[z, 8:9, :]

    @pl.when(place_ref[3] == 1)
    def _():
        upper(ma_ref)
        lower(mb_ref)

    @pl.when(place_ref[3] == 0)
    def _():
        lower(ma_ref)
        upper(mb_ref)


def level_part(place, tile, ma, mb, wide_peak, level_set, ls, sp, sm):
    layers, rows, lanes = level_set.shape
    nfirst, nsecond = swaps("narrow")
    wfirst, wsecond = swaps("wide")
    count = lax.axis_size("narrow")
    across = [(i, (i + count // 2) % count) for i in range(count)]
    ra = lax.ppermute(ma, "narrow", nfirst)
    rb = lax.ppermute(mb, "narrow", nsecond)
    pc = lax.ppermute(wide_peak, "narrow", across)
    pa, pb = ra[-1, :, :128], rb[-1, :, :128]
    tall = ls.shape[1]
    rows1 = -(-(rows + 2 * Y1) // 8) * 8
    rows2 = -(-(rows + 2 * Y2) // 8) * 8
    depth = layers + 2 * HALO
    speed, speed6, phi, sa, sb = vmem_call(
        extend_kernel,
        [(layers, rows, lanes), (layers, rows1, lanes), (layers, rows1, lanes), (3, rows2, lanes), (3, rows2, lanes)],
        (place, tile, ra, rb, pa, pb, pc, wide_peak, ls, sp, sm),
        [(depth, tall + 16, lanes)] * 2 + [(depth, tall, lanes)] * 2,
        8000,
    )
    ga = lax.ppermute(sa, "wide", wfirst)
    gb = lax.ppermute(sb, "wide", wsecond)
    gp, gm = vmem_call(functools.partial(plane_kernel, Y1 - Y2, False), [(layers, rows2, lanes)] * 2, (phi,), (), 12000)
    phi, sa, sb = vmem_call(
        functools.partial(finish_kernel, Y1 - Y2, rows),
        [(layers, rows2, lanes), (3, rows, lanes), (3, rows, lanes)],
        (place, phi, ga, gb, gp, gm, speed6),
        [(6, rows2, lanes)],
        5000,
    )
    ga = lax.ppermute(sa, "wide", wfirst)
    gb = lax.ppermute(sb, "wide", wsecond)
    gp, gm = vmem_call(functools.partial(plane_kernel, Y2, True), [(layers, rows, lanes)] * 2, (phi,), (), 12000)
    (phi,) = vmem_call(
        functools.partial(finish_kernel, Y2, rows),
        [(layers, rows, lanes)],
        (place, phi, ga, gb, gp, gm, speed),
        [(6, rows, lanes)],
        5000,
    )
    return phi, speed


def first_gradient(place, tall, ra, rb):
    depth, rows, lanes = tall.shape
    rows1 = -(-(rows + 2 * Y1) // 8) * 8
    total = -(-(rows + 2 * YE) // 8) * 8
    return vmem_call(
        first_gradient_kernel, [(depth, total, lanes)] + [(depth - 6, rows1, lanes)] * 2, (place, tall, ra, rb), (), 35000
    )


def stack_level(place, level_set, ra, rb):
    layers, rows, lanes = level_set.shape
    depth = layers + 6
    edge = (depth + -(-depth // 8), 8, lanes)
    return vmem_call(
        stack_kernel, [(depth, rows, lanes), edge, edge], (place, level_set, ra, rb), [(6, rows, lanes)], 1500
    )


def unpack_kernel(place_ref, recv_ref, tile_ref, peak_ref, ma_ref, mb_ref):
    parts = recv_ref.shape[0]
    depth, rows, lanes = tile_ref.shape
    for j in range(depth // 4):
        block = recv_ref[:, 16 * j : 16 * j + 16, :].reshape(parts * 16, 128)
        wide = pltpu.roll(block.T, 1, 1)
        for k in range(4):
            tile_ref[4 * j + k] = wide[rows * k : rows * (k + 1), :]
    peak = recv_ref[0, 80:88, :]
    for s in range(1, parts):
        peak = jnp.maximum(peak, recv_ref[s, 80:88, :])
    peak_ref[...] = peak
    fill_edges(place_ref, tile_ref, peak, ma_ref, mb_ref)


def fill_edges(place_ref, tile_ref, peak, ma_ref, mb_ref):
    depth, rows, lanes = tile_ref.shape

    def upper(ref):
        for z in range(depth):
            ref[z] = tile_ref[z, rows - 8 : rows, :]
            ref[depth + z // 4, 2 * (z % 4) : 2 * (z % 4) + 2, :] = tile_ref[z, rows - 10 : rows - 8, :]

    def lower(ref):
        for z in range(depth):
            ref[z] = tile_ref[z, 0:8, :]
            ref[depth + z // 4, 2 * (z % 4) : 2 * (z % 4) + 2, :] = tile_ref[z, 8:10, :]

    last = ma_ref.shape[0] - 1
    ma_ref[last, :, 0:128] = peak
    mb_ref[last, :, 0:128] = peak

    @pl.when(place_ref[3] == 1)
    def _():
        upper(ma_ref)
        lower(mb_ref)

    @pl.when(place_ref[3] == 0)
    def _():
        lower(ma_ref)
        upper(mb_ref)


def unpack(place, recv, own_z, rows):
    parts = recv.shape[0]
    lanes = parts * 16
    depth = own_z + 2 * HALO
    edge = (depth + depth // 4 + 1, 8, lanes)
    return vmem_call(
        unpack_kernel, [(depth, rows, lanes), (8, 128), edge, edge], (place, recv), (), 1500
    )


def per_device(displacement, material, level_set):
    wide = lax.axis_size("wide")
    loads, comps, own_x, rows, size_z = displacement.shape
    own_z, _, size_x = level_set.shape
    place = place_flags()
    backward = [(i, (i - 1) % wide) for i in range(wide)]
    wfirst, wsecond = swaps("wide")
    nfirst, nsecond = swaps("narrow")

    low = lax.ppermute(displacement[:, :, :, -1], "narrow", ring("narrow", 1))
    high = lax.ppermute(
        jnp.stack([displacement[:, :, :, 0], displacement[:, :, :, 1]], axis=2), "narrow", ring("narrow", -1)
    )
    yh = jnp.concatenate([low[:, :, None], high], axis=2)
    bounds = level_set[:3], level_set[own_z - 3 :]
    even = place[0] == 1
    la = lax.ppermute(jnp.where(even, bounds[1], bounds[0]), "wide", wfirst)
    lb = lax.ppermute(jnp.where(even, bounds[0], bounds[1]), "wide", wsecond)

    stiff = 0.2 + 0.8 * jnp.repeat(material[0].astype(jnp.float32), BZ, axis=1)
    layers, yh, la, lb = lax.optimization_barrier((displacement[:, :, :3], yh, la, lb))
    flat = [layers.reshape(-1, size_z), stiff, yh[:, :, :, :3].reshape(-1, size_z)]
    flat.append(jnp.zeros((-sum(f.shape[0] for f in flat) % 8, size_z), jnp.float32))
    beyond = lax.ppermute(jnp.concatenate(flat, axis=0), "wide", backward)
    inner, tail = inner_strain(displacement, yh)
    la, lb, inner = lax.optimization_barrier((la, lb, inner))
    tall, ya, yb = stack_level(place, level_set, la, lb)
    ya = lax.ppermute(ya, "narrow", nfirst)
    yb = lax.ppermute(yb, "narrow", nsecond)
    beyond, ya, yb = lax.optimization_barrier((beyond, ya, yb))
    message = strain_message(place, tail, beyond, inner, material, wide)
    message, tall = lax.optimization_barrier((message, tall))
    recv = lax.all_to_all(message.reshape(wide, 88, 128), "wide", split_axis=0, concat_axis=0, tiled=True)
    ls, sp, sm = first_gradient(place, tall, ya, yb)
    recv, sp = lax.optimization_barrier((recv, sp))
    tile, wide_peak, ma, mb = unpack(place, recv, own_z, rows)
    return level_part(place, tile, ma, mb, wide_peak, level_set, ls, sp, sm)


def solution(mesh):
    return jax.shard_map(
        per_device,
        mesh=mesh,
        in_specs=(
            P(None, None, "wide", "narrow", None),
            P("wide", "narrow", None),
            P("wide", "narrow", None),
        ),
        out_specs=(P("wide", "narrow", None), P("wide", "narrow", None)),
        check_vma=False,
    )
```

```python
import functools
import jax
import jax.numpy as jnp
from jax import lax
from jax.experimental import pallas as pl
from jax.experimental.pallas import tpu as pltpu
from jax.sharding import PartitionSpec as P

BZ = 16
EXT_PASSES = 4
HJ_STEPS = 3
SHEAR = 0.384615
LAME = 0.576923
WENO_EPS = 1e-06
TIME_STEP = 0.3
HALO = EXT_PASSES
GRAD_SCALE = 1.0 / (8.0 * 48.0 * 48.0)
YE = 10
Y1 = 6
Y2 = 3


def lane_shifts(value):
    blocks = [value[:, 128 * b : 128 * (b + 1)] for b in range(value.shape[1] // 128)]
    lane = lax.broadcasted_iota(jnp.int32, blocks[0].shape, 1)
    zero = jnp.zeros_like(blocks[0])
    outs = []
    for step in (-1, 1, 2):
        turned = [pltpu.roll(b, (-step) % 128, 1) for b in blocks]
        if step < 0:
            mask = lane < 1
            parts = [jnp.where(mask, turned[i - 1] if i > 0 else zero, turned[i]) for i in range(len(blocks))]
        else:
            mask = lane >= 128 - step
            parts = [
                jnp.where(mask, turned[i + 1] if i + 1 < len(blocks) else zero, turned[i])
                for i in range(len(blocks))
            ]
        outs.append(jnp.concatenate(parts, axis=1))
    return outs


def val4(a, b, c, d):
    return (a + d) + 23.0 * (b + c)


def der4(a, b, c, d):
    return (d - a) + 5.0 * (c - b)


def filter_plane(filt, comp, layer, get_rows, tiles, low, high0, high1):
    tile_rows = [get_rows(t) for t in range(tiles)]
    row = lax.broadcasted_iota(jnp.int32, tile_rows[0].shape, 0)
    down = [pltpu.roll(v, 1, 0) for v in tile_rows]
    up = [pltpu.roll(v, 7, 0) for v in tile_rows]
    up2 = [pltpu.roll(v, 6, 0) for v in tile_rows]
    for t in range(tiles):
        b = tile_rows[t]
        a = jnp.where(row == 0, down[t - 1] if t else low, down[t])
        if t + 1 < tiles:
            c = jnp.where(row == 7, up[t + 1], up[t])
            d = jnp.where(row >= 6, up2[t + 1], up2[t])
        else:
            c = jnp.where(row == 7, high0, up[t])
            d = jnp.where(row == 6, high0, jnp.where(row == 7, high1, up2[t]))
        val_y = val4(a, b, c, d)
        der_y = der4(a, b, c, d)
        before, after, after2 = lane_shifts(val_y)
        span = pl.ds(8 * t, 8)
        filt[comp, 0, layer, span, :] = val4(before, val_y, after, after2)
        filt[comp, 2, layer, span, :] = der4(before, val_y, after, after2)
        before, after, after2 = lane_shifts(der_y)
        filt[comp, 1, layer, span, :] = val4(before, der_y, after, after2)


def densities(field, rows, finish):
    for tile in range(rows // 8):
        span = pl.ds(8 * tile, 8)
        gx = [der4(*field(comp, 0, span)) for comp in range(3)]
        gy = [val4(*field(comp, 1, span)) for comp in range(3)]
        gz = [val4(*field(comp, 2, span)) for comp in range(3)]
        sxy = gy[0] + gx[1]
        sxz = gz[0] + gx[2]
        syz = gz[1] + gy[2]
        trace = gx[0] + gy[1] + gz[2]
        square = gx[0] * gx[0] + gy[1] * gy[1] + gz[2] * gz[2]
        shear = sxy * sxy + sxz * sxz + syz * syz
        scale = GRAD_SCALE * GRAD_SCALE
        finish(span, (SHEAR * scale) * (square + 0.5 * shear) + (0.5 * LAME * scale) * (trace * trace))


def accumulate(ref, slot):
    load = pl.program_id(0)

    def finish(span, density):
        @pl.when(load == 0)
        def _():
            ref[slot, span, :] = density

        @pl.when(load > 0)
        def _():
            ref[slot, span, :] += density

    return finish


def inner_kernel(u_ref, yh_ref, energy_ref, tail_ref, filt):
    own_x, rows = u_ref.shape[2:4]

    def own_layer(layer, carry):
        for comp in range(3):
            edge = [yh_ref[0, comp, k, pl.ds(layer, 1), :] for k in range(3)]
            get_rows = lambda t: u_ref[0, comp, layer, 8 * t : 8 * t + 8, :]
            filter_plane(filt, comp, layer, get_rows, rows // 8, *edge)
        return carry

    lax.fori_loop(0, own_x, own_layer, 0)

    def slot_step(slot, carry):
        field = lambda comp, which, span: [filt[comp, which, slot + k, span, :] for k in range(4)]
        densities(field, rows, accumulate(energy_ref, slot))
        return carry

    lax.fori_loop(0, own_x - 3, slot_step, 0)
    for comp in range(3):
        for which in range(3):
            for k in range(3):
                tail_ref[0, comp, which, k] = filt[comp, which, own_x - 3 + k]


def outer_kernel(place_ref, tail_ref, next_ref, inner_ref, solid_ref, msg_ref, filt, energy, turned):
    load = pl.program_id(0)
    own_x, rows, blocks = solid_ref.shape
    size_z = next_ref.shape[1]
    loads = 3
    inner = own_x - 3
    tiles = rows // 8
    keep = jnp.where(place_ref[2] == 1, 0.0, 1.0)
    for comp in range(3):
        for k in range(3):
            layer = (load * 3 + comp) * 3 + k
            corner = loads * 9 * rows + rows
            edge = [next_ref[pl.ds(corner + (load * 3 + comp) * 9 + 3 * which + k, 1), :] for which in range(3)]
            get_rows = lambda t: next_ref[pl.ds(pl.multiple_of(layer * rows + 8 * t, 8), 8), :]
            filter_plane(filt, comp, k, get_rows, tiles, *edge)

    def density_at(slot, masked):
        def field(comp, which, span):
            out = []
            for k in range(4):
                at = slot + k
                value = tail_ref[0, comp, which, at, span, :] if at < 3 else filt[comp, which, at - 3, span, :]
                out.append(value * keep if masked[k] else value)
            return out

        densities(field, rows, accumulate(energy, slot))

    density_at(0, (False, False, False, True))
    density_at(1, (False, False, True, True))
    density_at(2, (True, False, False, False))

    @pl.when(load == pl.num_programs(0) - 1)
    def _():
        peak = jnp.zeros((8, 128), jnp.float32)
        groups = own_x // 4
        block_of = lax.broadcasted_iota(jnp.int32, (blocks, size_z), 1) // (size_z // blocks)
        spread = jnp.where(block_of == lax.broadcasted_iota(jnp.int32, (blocks, size_z), 0), 1.0, 0.0)
        for g in range(groups):
            stack = []
            for q in range(4):
                x = 4 * g + q
                if x < own_x - 1:
                    solid = jnp.dot(solid_ref[x + 1].astype(jnp.float32), spread, preferred_element_type=jnp.float32)
                    stiff = 0.2 + 0.8 * solid
                else:
                    stiff = next_ref[loads * 9 * rows : loads * 9 * rows + rows, :]
                value = (inner_ref[x] if x < inner else energy[x - inner]) * stiff
                stack.append(value)
                for tile in range(tiles):
                    for b in range(size_z // 128):
                        peak = jnp.maximum(peak, value[8 * tile : 8 * tile + 8, 128 * b : 128 * b + 128])
            turned[g, 0:8, :] = jnp.zeros((8, 128), jnp.float32)
            turned[g, size_z : size_z + 16, :] = jnp.zeros((16, 128), jnp.float32)
            turned[g, HALO : HALO + size_z, :] = jnp.concatenate(stack, axis=0).T
        peak = jnp.broadcast_to(jnp.max(peak, axis=0, keepdims=True), (8, 128))
        peak = jnp.broadcast_to(jnp.max(peak, axis=1, keepdims=True), (8, 128))
        parts = msg_ref.shape[0] // 88
        own_z = size_z // parts
        quads = (own_z + 2 * HALO) // 4
        lane = lax.broadcasted_iota(jnp.int32, (parts, 128), 1) // rows
        for g in range(groups):
            for j in range(quads):
                picked = [turned[g, pl.ds(4 * j + k, parts, stride=own_z), :] for k in range(4)]
                for q in range(4):
                    out = None
                    for k in range(4):
                        shift = (rows * (k - q)) % 128
                        part = pltpu.roll(picked[k], shift, 1) if shift else picked[k]
                        out = part if out is None else jnp.where(lane == k, part, out)
                    msg_ref[pl.ds(16 * j + 4 * g + q, parts, stride=88), :] = out
        for t in range(parts):
            msg_ref[pl.ds(88 * t + 80, 8), :] = peak


def load_block(*shape):
    return pl.BlockSpec((1,) + shape, lambda l: (l,) + (0,) * len(shape))


def fixed_block(*shape):
    return pl.BlockSpec(shape, lambda l: (0,) * len(shape))


def inner_strain(disp, yh):
    loads, comps, own_x, rows, size_z = disp.shape
    return pl.pallas_call(
        inner_kernel,
        grid=(loads,),
        out_shape=(
            jax.ShapeDtypeStruct((own_x - 3, rows, size_z), jnp.float32),
            jax.ShapeDtypeStruct((loads, comps, 3, 3, rows, size_z), jnp.float32),
        ),
        in_specs=[load_block(comps, own_x, rows, size_z), load_block(comps, 3, own_x, size_z)],
        out_specs=(fixed_block(own_x - 3, rows, size_z), load_block(comps, 3, 3, rows, size_z)),
        scratch_shapes=[
            pltpu.VMEM((3, 3, own_x, rows, size_z), jnp.float32),
        ],
        compiler_params=pltpu.CompilerParams(vmem_limit_bytes=48 << 20),
        cost_estimate=pl.CostEstimate(flops=40000 * 4096, bytes_accessed=1 << 20, transcendentals=0),
    )(disp, yh)


def strain_message(place, tail, beyond, inner, solid, parts):
    loads, comps = tail.shape[:2]
    own_x, rows, blocks = solid.shape
    size_z = beyond.shape[1]
    return pl.pallas_call(
        outer_kernel,
        grid=(loads,),
        out_shape=jax.ShapeDtypeStruct((parts * 88, 128), jnp.float32),
        in_specs=[
            pl.BlockSpec(memory_space=pltpu.SMEM),
            load_block(comps, 3, 3, rows, size_z),
            fixed_block(*beyond.shape),
            fixed_block(own_x - 3, rows, size_z),
            fixed_block(own_x, rows, blocks),
        ],
        out_specs=fixed_block(parts * 88, 128),
        scratch_shapes=[
            pltpu.VMEM((3, 3, 3, rows, size_z), jnp.float32),
            pltpu.VMEM((3, rows, size_z), jnp.float32),
            pltpu.VMEM((own_x // 4, size_z + 16, 128), jnp.float32),
        ],
        compiler_params=pltpu.CompilerParams(vmem_limit_bytes=48 << 20),
        cost_estimate=pl.CostEstimate(flops=10000 * 4096, bytes_accessed=1 << 20, transcendentals=0),
    )(place, tail, beyond, inner, solid)


def ring(axis, step):
    count = lax.axis_size(axis)
    return [(i, i + step) for i in range(count) if 0 <= i + step < count]


def newton_reciprocal(x):
    r = pl.reciprocal(x, approx=True)
    return r * (2.0 - x * r)


def weno_cell(d, e0, e1, e2, e3):
    f0 = e1 - e0
    f1 = e2 - e1
    f2 = e3 - e2
    g0 = f1 - f0
    g1 = f2 - f1
    twice1 = e1 + e1
    twice2 = e2 + e2
    third = 13.0 / 3.0
    eps = 4.0 * WENO_EPS
    pa = twice1 + f0
    pb = twice1 + f1
    pc = twice2 - f2
    a = (f0 * f0 * third + eps) + pa * pa
    b = (f1 * f1 * third + eps) + pb * pb
    c = (f2 * f2 * third + eps) + pc * pc
    a = a * a
    b = b * b * (1.0 / 6.0)
    c = c * c
    ac = a * c
    ab = a * b
    cb = c * b
    u = cb * g0
    v = ab * g1
    both = u + v
    both = both + both
    s = e1 + e2
    d6 = 6.0 * d
    minus = d6 + (s + e2) - (both + v) * newton_reciprocal(ac + cb + 3.0 * ab)
    plus = (s + e1) - d6 - (both + u) * newton_reciprocal(ac + ab + 3.0 * cb)
    return minus, plus


def godunov(minus, plus):
    high = jnp.maximum(jnp.maximum(minus, plus), 0.0)
    low = jnp.minimum(jnp.minimum(minus, plus), 0.0)
    return high * high, low * low


def x_terms(phi):
    rows, size = phi.shape
    wide = size + 128
    phi = jnp.concatenate([phi, jnp.ones((rows, 128), jnp.float32)], axis=1)
    d = pltpu.roll(phi, wide - 1, 1) - phi
    e = pltpu.roll(d, wide - 1, 1) - d
    minus, plus = weno_cell(
        d, pltpu.roll(e, 2, 1), pltpu.roll(e, 1, 1), e, pltpu.roll(e, wide - 1, 1)
    )
    return godunov(pltpu.roll(minus, 1, 1)[:, :size], plus[:, :size])


def next_rows(tiles, step, count):
    row = lax.broadcasted_iota(jnp.int32, tiles[0].shape, 0)
    turned = [pltpu.roll(v, 8 - step, 0) for v in tiles]
    last = len(tiles) - 1
    return [jnp.where(row < 8 - step, turned[t], turned[min(t + 1, last)]) for t in range(count)]


def y_stage(phi_ref, layer, span, gp_ref, gm_ref, z, exact):
    tiles = gp_ref.shape[1] // 8
    cells = tiles + 1 if exact else tiles
    count = min(cells + 1, phi_ref.shape[1] // 8)
    phi = [phi_ref[layer, 8 * t : 8 * t + 8, span] for t in range(count)]
    d = [n - p for n, p in zip(next_rows(phi, 1, count), phi)]
    e = [n - p for n, p in zip(next_rows(d, 1, count), d)]
    d2 = next_rows(d, 2, cells)
    e1, e2, e3 = (next_rows(e, k, cells) for k in (1, 2, 3))
    sides = [weno_cell(d2[t], e[t], e1[t], e2[t], e3[t]) for t in range(cells)]
    plus = next_rows([p for _, p in sides], 1, tiles)
    for t in range(tiles):
        rows = slice(8 * t, 8 * t + 8)
        gp_ref[z, rows, span], gm_ref[z, rows, span] = godunov(sides[t][0], plus[t])


def xy_stage(phi_ref, layer0, layers, gp_ref, gm_ref, exact=False):
    _, rows, lanes = gp_ref.shape

    def layer_step(z, carry):
        for block in range(lanes // 128):
            y_stage(phi_ref, z + layer0, slice(128 * block, 128 * block + 128), gp_ref, gm_ref, z, exact)
        for t in range(rows // 8):
            xp, xm = x_terms(phi_ref[z + layer0, 8 * t + 3 : 8 * t + 11, :])
            gp_ref[z, 8 * t : 8 * t + 8, :] += xp
            gm_ref[z, 8 * t : 8 * t + 8, :] += xm
        return carry

    lax.fori_loop(0, layers, layer_step, 0)


def z_stage(get_phi, layers, rows, lanes, finish):
    def lane_step(block, carry):
        span = pl.ds(pl.multiple_of(128 * block, 128), 128)
        for t in range(rows // 8):
            p = [get_phi(z, t, span) for z in range(-3, layers + 3)]
            d = [p[k + 1] - p[k] for k in range(len(p) - 1)]
            e = [d[k + 1] - d[k] for k in range(len(d) - 1)]
            before = None
            for cell in range(layers + 1):
                minus, plus = weno_cell(d[cell + 2], e[cell], e[cell + 1], e[cell + 2], e[cell + 3])
                if before is not None:
                    finish(cell - 1, t, span, *godunov(before, plus))
                before = minus
        return carry

    lax.fori_loop(0, lanes // 128, lane_step, 0)


def first_gradient_kernel(place_ref, tall_ref, ra_ref, rb_ref, ls_ref, sp_ref, sm_ref, near):
    layers, rows, lanes = sp_ref.shape
    depth, own, _ = tall_ref.shape
    ones = jnp.ones((8, lanes), jnp.float32)

    def copy(z, carry):
        for t in range(ls_ref.shape[1] // 8):
            ls_ref[z, 8 * t : 8 * t + 8, :] = ones
        ls_ref[z, YE : YE + own, :] = tall_ref[z]
        return carry

    lax.fori_loop(0, depth, copy, 0)

    def below(ref):
        @pl.when(place_ref[4] == 0)
        def _():
            for z in range(depth):
                ls_ref[z, YE - 8 : YE, :] = ref[z]
                ls_ref[z, YE - 9 : YE - 8, :] = ref[depth + z // 8, z % 8 : z % 8 + 1, :]

    def above(ref):
        @pl.when(place_ref[5] == 0)
        def _():
            for z in range(depth):
                ls_ref[z, YE + own : YE + own + 8, :] = ref[z]
                ls_ref[z, YE + own + 8 : YE + own + 9, :] = ref[depth + z // 8, z % 8 : z % 8 + 1, :]

    @pl.when(place_ref[3] == 1)
    def _():
        above(ra_ref)
        below(rb_ref)

    @pl.when(place_ref[3] == 0)
    def _():
        below(ra_ref)
        above(rb_ref)

    skip = YE - Y1 - 3

    def move(z, carry):
        near[z, 0 : near.shape[1] - 8, :] = ls_ref[z, skip : skip + near.shape[1] - 8, :]
        near[z, near.shape[1] - 8 :, :] = ls_ref[z, near.shape[1] - 8 :, :]
        near[z, near.shape[1] - 8 : near.shape[1] - skip, :] = ls_ref[z, near.shape[1] - 8 + skip :, :]
        return carry

    lax.fori_loop(0, depth, move, 0)
    xy_stage(near, 3, layers, sp_ref, sm_ref)

    def finish(z, t, span, gp, gm):
        where = pl.ds(8 * t, 8)
        scale = TIME_STEP / 6.0
        sp_ref[z, where, span] = scale * jnp.sqrt(sp_ref[z, where, span] + gp)
        sm_ref[z, where, span] = scale * jnp.sqrt(sm_ref[z, where, span] + gm)

    z_stage(
        lambda z, t, span: near[z + 3, 8 * t + 3 : 8 * t + 11, span], layers, rows, lanes, finish
    )


def vmem_call(kernel, outs, args, scratch=(), cycles=0, limit=8):
    specs = []
    for arg in args:
        space = pltpu.SMEM if arg.dtype == jnp.int32 else pltpu.VMEM
        specs.append(pl.BlockSpec(memory_space=space))
    return pl.pallas_call(
        kernel,
        out_shape=tuple(jax.ShapeDtypeStruct(shape, jnp.float32) for shape in outs),
        in_specs=specs,
        out_specs=tuple(pl.BlockSpec(memory_space=pltpu.VMEM) for _ in outs),
        scratch_shapes=[pltpu.VMEM(shape, jnp.float32) for shape in scratch],
        compiler_params=pltpu.CompilerParams(vmem_limit_bytes=limit << 20),
        cost_estimate=pl.CostEstimate(flops=cycles * 4096, bytes_accessed=1 << 20, transcendentals=0),
    )(*args)


def place_flags():
    wide, narrow = lax.axis_index("wide"), lax.axis_index("narrow")
    flags = [
        1 - wide % 2, wide == 0, wide == lax.axis_size("wide") - 1,
        1 - narrow % 2, narrow == 0, narrow == lax.axis_size("narrow") - 1,
    ]
    return jnp.stack([jnp.asarray(f).astype(jnp.int32) for f in flags])


def y_inside(place_ref, base, first_row, shape, rows):
    row = lax.broadcasted_iota(jnp.int32, shape, 0) + (first_row - base)
    inside = (row >= 0) | (place_ref[4] == 0)
    return inside & ((row < rows) | (place_ref[5] == 0))


def extend_kernel(
    place_ref, tile_ref, ra_ref, rb_ref, pa_ref, pb_ref, pc_ref, po_ref, ls_ref, sp_ref, sm_ref,
    speed_ref, speed6_ref, phi_ref, ma_ref, mb_ref, one, two, keep, pull,
):
    depth, rows, lanes = tile_ref.shape
    layers = depth - 2 * HALO
    tall = ls_ref.shape[1]
    margin = 8
    base = margin + YE
    peak = jnp.maximum(jnp.maximum(pa_ref[...], pb_ref[...]), jnp.maximum(pc_ref[...], po_ref[...]))
    scale = 1.0 / (peak[0:1, 0:1] + 1e-06)

    def assemble(z, carry):
        one[z, base : base + rows, :] = tile_ref[z]
        return carry

    lax.fori_loop(0, depth, assemble, 0)

    def below(ref):
        for z in range(depth):
            one[z, base - 8 : base, :] = ref[z]
            one[z, base - 10 : base - 8, :] = ref[depth + z // 4, 2 * (z % 4) : 2 * (z % 4) + 2, :]

    def above(ref):
        for z in range(depth):
            one[z, base + rows : base + rows + 8, :] = ref[z]
            one[z, base + rows + 8 : base + rows + 10, :] = ref[depth + z // 4, 2 * (z % 4) : 2 * (z % 4) + 2, :]

    @pl.when(place_ref[3] == 1)
    def _():
        above(ra_ref)
        below(rb_ref)

    @pl.when(place_ref[3] == 0)
    def _():
        below(ra_ref)
        above(rb_ref)

    def normalise(z, carry):
        outside = ((z < HALO) & (place_ref[1] == 1)) | ((z >= depth - HALO) & (place_ref[2] == 1))
        for t in range(tall // 8):
            at = slice(margin + 8 * t, margin + 8 * t + 8)
            ok = y_inside(place_ref, YE, 8 * t, (8, lanes), rows) & jnp.logical_not(outside)
            velocity = jnp.where(ok, one[z, at, :] * scale - 0.5, 0.0)
            one[z, at, :] = velocity

            @pl.when((z >= 1) & (z < depth - 1))
            def _():
                ls = ls_ref[z - 1, 8 * t : 8 * t + 8, :]
                weight = 1.0 / (1.0 + 4.0 * ls * ls)
                keep[z, 8 * t : 8 * t + 8, :] = weight * velocity
                pull[z, 8 * t : 8 * t + 8, :] = jnp.where(ok, (1.0 - weight) * (1.0 / 6.0), 0.0)

        return carry

    lax.fori_loop(0, depth, normalise, 0)
    for step in range(EXT_PASSES):
        source, target = (one, two) if step % 2 == 0 else (two, one)

        def extend(z, carry):
            count = tall // 8
            tiles = [source[z, 8 * t : 8 * t + 8, :] for t in range(count + 2)]
            row = lax.broadcasted_iota(jnp.int32, tiles[0].shape, 0)
            lane = lax.broadcasted_iota(jnp.int32, tiles[0].shape, 1)
            down = [pltpu.roll(v, 1, 0) for v in tiles[:-1]]
            up = [pltpu.roll(v, 7, 0) for v in tiles[1:]]
            for t in range(count):
                at = margin + 8 * t
                centre = tiles[t + 1]
                total = source[z - 1, at : at + 8, :] + source[z + 1, at : at + 8, :]
                total = total + jnp.where(row == 0, down[t], down[t + 1])
                total = total + jnp.where(row == 7, up[t + 1], up[t])
                total = total + jnp.where(lane == 0, 0.0, pltpu.roll(centre, 1, 1))
                total = total + jnp.where(lane == lanes - 1, 0.0, pltpu.roll(centre, lanes - 1, 1))
                span = slice(8 * t, 8 * t + 8)
                target[z, at : at + 8, :] = keep[z, span, :] + pull[z, span, :] * total
            return carry

        lax.fori_loop(step + 1, depth - 1 - step, extend, 0)

    final = one if EXT_PASSES % 2 == 0 else two

    def march(z, carry):
        speed_ref[z] = final[z + HALO, base : base + rows, :]
        shift = YE - Y1
        for t in range(speed6_ref.shape[1] // 8):
            span = slice(8 * t, 8 * t + 8)
            speed = final[z + HALO, margin + shift + 8 * t : margin + shift + 8 * t + 8, :]
            speed6_ref[z, span, :] = speed
            change = jnp.maximum(speed, 0.0) * sp_ref[z, span, :] + jnp.minimum(speed, 0.0) * sm_ref[z, span, :]
            phi = ls_ref[z + 3, shift + 8 * t : shift + 8 * t + 8, :] - change
            phi_ref[z, span, :] = jnp.where(y_inside(place_ref, Y1, 8 * t, phi.shape, rows), phi, 1.0)
        return carry

    lax.fori_loop(0, layers, march, 0)
    send_edges(place_ref, phi_ref, Y1 - Y2, ma_ref, mb_ref)


def send_edges(place_ref, phi_ref, offset, ma_ref, mb_ref):
    layers = phi_ref.shape[0]
    count = ma_ref.shape[1]
    upper = place_ref[0] * (layers - 3)
    lower = (1 - place_ref[0]) * (layers - 3)
    for k in range(3):
        ma_ref[k] = phi_ref[upper + k, offset : offset + count, :]
        mb_ref[k] = phi_ref[lower + k, offset : offset + count, :]


def take_edges(place_ref, ra_ref, rb_ref, edges):
    upper = 3 * place_ref[0]
    lower = 3 - upper
    for k in range(3):
        edges[upper + k] = ra_ref[k]
        edges[lower + k] = rb_ref[k]

    @pl.when(place_ref[1] == 1)
    def _():
        edges[0:3] = jnp.ones((3,) + tuple(edges.shape[1:]), jnp.float32)

    @pl.when(place_ref[2] == 1)
    def _():
        edges[3:6] = jnp.ones((3,) + tuple(edges.shape[1:]), jnp.float32)


def plane_kernel(exact, phi_ref, gp_ref, gm_ref):
    xy_stage(phi_ref, 0, gp_ref.shape[0], gp_ref, gm_ref, exact)


def finish_kernel(
    rows, place_ref, phi_ref, ra_ref, rb_ref, gp_ref, gm_ref, speed_ref, *rest
):
    out_ref, edges = rest[0], rest[-1]
    layers, count, lanes = out_ref.shape
    base = Y2 if count > rows else 0
    speed_offset = 3 if count > rows else 0
    take_edges(place_ref, ra_ref, rb_ref, edges)

    def get_phi(z, t, span):
        if z < 0:
            return edges[z + 3, 8 * t : 8 * t + 8, span]
        if z >= layers:
            return edges[z - layers + 3, 8 * t : 8 * t + 8, span]
        return phi_ref[z, 8 * t + 3 : 8 * t + 11, span]

    def finish(z, t, span, gp, gm):
        where = pl.ds(8 * t, 8)
        speed = speed_ref[z, 8 * t + speed_offset : 8 * t + speed_offset + 8, span]
        total = jnp.where(speed > 0.0, gp_ref[z, where, span] + gp, gm_ref[z, where, span] + gm)
        phi = get_phi(z, t, span) - (TIME_STEP / 6.0) * speed * jnp.sqrt(total)
        if count > rows:
            phi = jnp.where(y_inside(place_ref, base, 8 * t, phi.shape, rows), phi, 1.0)
        out_ref[z, where, span] = phi

    z_stage(get_phi, layers, count, lanes, finish)
    if len(rest) > 2:
        send_edges(place_ref, out_ref, Y2, rest[1], rest[2])


def swaps(axis):
    count = lax.axis_size(axis)
    first, second = [], []
    for i in range(0, count, 2):
        first += [(i, i + 1), (i + 1, i)]
        if i + 2 < count:
            second += [(i + 1, i + 2), (i + 2, i + 1)]
    return first, second


def stack_kernel(place_ref, ls_ref, ra_ref, rb_ref, tall_ref, ma_ref, mb_ref, edges):
    layers, rows = ls_ref.shape[:2]
    take_edges(place_ref, ra_ref, rb_ref, edges)
    for k in range(3):
        tall_ref[k] = edges[k]
        tall_ref[layers + 3 + k] = edges[3 + k]

    def copy(z, carry):
        tall_ref[z + 3] = ls_ref[z]
        return carry

    lax.fori_loop(0, layers, copy, 0)
    depth = layers + 6

    def upper(ref):
        for z in range(depth):
            ref[z] = tall_ref[z, rows - 8 : rows, :]
            ref[depth + z // 8, z % 8 : z % 8 + 1, :] = tall_ref[z, rows - 9 : rows - 8, :]

    def lower(ref):
        for z in range(depth):
            ref[z] = tall_ref[z, 0:8, :]
            ref[depth + z // 8, z % 8 : z % 8 + 1, :] = tall_ref[z, 8:9, :]

    @pl.when(place_ref[3] == 1)
    def _():
        upper(ma_ref)
        lower(mb_ref)

    @pl.when(place_ref[3] == 0)
    def _():
        lower(ma_ref)
        upper(mb_ref)


def level_part(place, tile, ma, mb, wide_peak, level_set, ls, sp, sm):
    layers, rows, lanes = level_set.shape
    nfirst, nsecond = swaps("narrow")
    wfirst, wsecond = swaps("wide")
    count = lax.axis_size("narrow")
    across = [(i, (i + count // 2) % count) for i in range(count)]
    mirror = [(i, count - 1 - i) for i in range(count)]
    ra = lax.ppermute(ma, "narrow", nfirst)
    rb = lax.ppermute(mb, "narrow", nsecond)
    pc = lax.ppermute(wide_peak, "narrow", across)
    pb = lax.ppermute(wide_peak, "narrow", mirror)
    pa = ra[-1, :, :128]
    tall = ls.shape[1]
    rows1 = -(-(rows + 2 * Y1) // 8) * 8
    rows2 = -(-(rows + 2 * Y2) // 8) * 8
    depth = layers + 2 * HALO
    speed, speed6, phi, sa, sb = vmem_call(
        extend_kernel,
        [(layers, rows, lanes), (layers, rows1, lanes), (layers, rows1, lanes), (3, rows2, lanes), (3, rows2, lanes)],
        (place, tile, ra, rb, pa, pb, pc, wide_peak, ls, sp, sm),
        [(depth, tall + 16, lanes)] * 2 + [(depth, tall, lanes)] * 2,
        8000,
        16,
    )
    ga = lax.ppermute(sa, "wide", wfirst)
    gb = lax.ppermute(sb, "wide", wsecond)
    gp, gm = vmem_call(functools.partial(plane_kernel, False), [(layers, rows2, lanes)] * 2, (phi,), (), 12000)
    phi, sa, sb = vmem_call(
        functools.partial(finish_kernel, rows),
        [(layers, rows2, lanes), (3, rows, lanes), (3, rows, lanes)],
        (place, phi, ga, gb, gp, gm, speed6),
        [(6, rows2, lanes)],
        5000,
    )
    ga = lax.ppermute(sa, "wide", wfirst)
    gb = lax.ppermute(sb, "wide", wsecond)
    gp, gm = vmem_call(functools.partial(plane_kernel, True), [(layers, rows, lanes)] * 2, (phi,), (), 12000)
    (phi,) = vmem_call(
        functools.partial(finish_kernel, rows),
        [(layers, rows, lanes)],
        (place, phi, ga, gb, gp, gm, speed),
        [(6, rows, lanes)],
        5000,
    )
    return phi, speed


def first_gradient(place, tall, ra, rb):
    depth, rows, lanes = tall.shape
    rows1 = -(-(rows + 2 * Y1) // 8) * 8
    total = -(-(rows + 2 * YE) // 8) * 8
    return vmem_call(
        first_gradient_kernel, [(depth, total, lanes)] + [(depth - 6, rows1, lanes)] * 2, (place, tall, ra, rb),
        [(depth, total, lanes)], 35000
    )


def stack_level(place, level_set, ra, rb):
    layers, rows, lanes = level_set.shape
    depth = layers + 6
    edge = (depth + -(-depth // 8), 8, lanes)
    return vmem_call(
        stack_kernel, [(depth, rows, lanes), edge, edge], (place, level_set, ra, rb), [(6, rows, lanes)], 1500
    )


def unpack_kernel(place_ref, recv_ref, tile_ref, peak_ref, ma_ref, mb_ref):
    parts = recv_ref.shape[0]
    depth, rows, lanes = tile_ref.shape
    for j in range(depth // 4):
        block = recv_ref[:, 16 * j : 16 * j + 16, :].reshape(parts * 16, 128)
        wide = pltpu.roll(block.T, 1, 1)
        for k in range(4):
            tile_ref[4 * j + k] = wide[rows * k : rows * (k + 1), :]
    peak = recv_ref[0, 80:88, :]
    for s in range(1, parts):
        peak = jnp.maximum(peak, recv_ref[s, 80:88, :])
    peak_ref[...] = peak
    fill_edges(place_ref, tile_ref, peak, ma_ref, mb_ref)


def fill_edges(place_ref, tile_ref, peak, ma_ref, mb_ref):
    depth, rows, lanes = tile_ref.shape

    def upper(ref):
        for z in range(depth):
            ref[z] = tile_ref[z, rows - 8 : rows, :]
            ref[depth + z // 4, 2 * (z % 4) : 2 * (z % 4) + 2, :] = tile_ref[z, rows - 10 : rows - 8, :]

    def lower(ref):
        for z in range(depth):
            ref[z] = tile_ref[z, 0:8, :]
            ref[depth + z // 4, 2 * (z % 4) : 2 * (z % 4) + 2, :] = tile_ref[z, 8:10, :]

    last = ma_ref.shape[0] - 1
    ma_ref[last, :, 0:128] = peak
    mb_ref[last, :, 0:128] = peak

    @pl.when(place_ref[3] == 1)
    def _():
        upper(ma_ref)
        lower(mb_ref)

    @pl.when(place_ref[3] == 0)
    def _():
        lower(ma_ref)
        upper(mb_ref)


def unpack(place, recv, own_z, rows):
    parts = recv.shape[0]
    lanes = parts * 16
    depth = own_z + 2 * HALO
    edge = (depth + depth // 4 + 1, 8, lanes)
    return vmem_call(
        unpack_kernel, [(depth, rows, lanes), (8, 128), edge, edge], (place, recv), (), 1500
    )


def per_device(displacement, material, level_set):
    wide = lax.axis_size("wide")
    loads, comps, own_x, rows, size_z = displacement.shape
    own_z, _, size_x = level_set.shape
    place = place_flags()
    backward = [(i, (i - 1) % wide) for i in range(wide)]
    wfirst, wsecond = swaps("wide")
    nfirst, nsecond = swaps("narrow")

    low = lax.ppermute(displacement[:, :, :, -1], "narrow", ring("narrow", 1))
    high = lax.ppermute(
        jnp.stack([displacement[:, :, :, 0], displacement[:, :, :, 1]], axis=2), "narrow", ring("narrow", -1)
    )
    yh = jnp.concatenate([low[:, :, None], high], axis=2)
    bounds = level_set[:3], level_set[own_z - 3 :]
    even = place[0] == 1
    la = lax.ppermute(jnp.where(even, bounds[1], bounds[0]), "wide", wfirst)
    lb = lax.ppermute(jnp.where(even, bounds[0], bounds[1]), "wide", wsecond)

    stiff = 0.2 + 0.8 * jnp.repeat(material[0].astype(jnp.float32), BZ, axis=1)
    layers, yh, la, lb = lax.optimization_barrier((displacement[:, :, :3], yh, la, lb))
    flat = [layers.reshape(-1, size_z), stiff, yh[:, :, :, :3].reshape(-1, size_z)]
    flat.append(jnp.zeros((-sum(f.shape[0] for f in flat) % 8, size_z), jnp.float32))
    beyond = lax.ppermute(jnp.concatenate(flat, axis=0), "wide", backward)
    inner, tail = inner_strain(displacement, yh)
    la, lb, inner = lax.optimization_barrier((la, lb, inner))
    tall, ya, yb = stack_level(place, level_set, la, lb)
    ya = lax.ppermute(ya, "narrow", nfirst)
    yb = lax.ppermute(yb, "narrow", nsecond)
    beyond, ya, yb = lax.optimization_barrier((beyond, ya, yb))
    message = strain_message(place, tail, beyond, inner, material, wide)
    message, tall = lax.optimization_barrier((message, tall))
    recv = lax.all_to_all(message.reshape(wide, 88, 128), "wide", split_axis=0, concat_axis=0, tiled=True)
    ls, sp, sm = first_gradient(place, tall, ya, yb)
    recv, sp = lax.optimization_barrier((recv, sp))
    tile, wide_peak, ma, mb = unpack(place, recv, own_z, rows)
    return level_part(place, tile, ma, mb, wide_peak, level_set, ls, sp, sm)


def solution(mesh):
    return jax.shard_map(
        per_device,
        mesh=mesh,
        in_specs=(
            P(None, None, "wide", "narrow", None),
            P("wide", "narrow", None),
            P("wide", "narrow", None),
        ),
        out_specs=(P("wide", "narrow", None), P("wide", "narrow", None)),
        check_vma=False,
    )
```

```python
import functools
import jax
import jax.numpy as jnp
from jax import lax
from jax.experimental import pallas as pl
from jax.experimental.pallas import tpu as pltpu
from jax.sharding import PartitionSpec as P

BZ = 16
EXT_PASSES = 4
HJ_STEPS = 3
SHEAR = 0.384615
LAME = 0.576923
WENO_EPS = 1e-06
TIME_STEP = 0.3
HALO = EXT_PASSES
GRAD_SCALE = 1.0 / (8.0 * 48.0 * 48.0)
YE = 9
Y1 = 6
Y2 = 3


def lane_shifts(value):
    blocks = [value[:, 128 * b : 128 * (b + 1)] for b in range(value.shape[1] // 128)]
    lane = lax.broadcasted_iota(jnp.int32, blocks[0].shape, 1)
    zero = jnp.zeros_like(blocks[0])
    outs = []
    for step in (-1, 1, 2):
        turned = [pltpu.roll(b, (-step) % 128, 1) for b in blocks]
        if step < 0:
            mask = lane < 1
            parts = [jnp.where(mask, turned[i - 1] if i > 0 else zero, turned[i]) for i in range(len(blocks))]
        else:
            mask = lane >= 128 - step
            parts = [
                jnp.where(mask, turned[i + 1] if i + 1 < len(blocks) else zero, turned[i])
                for i in range(len(blocks))
            ]
        outs.append(jnp.concatenate(parts, axis=1))
    return outs


def val4(a, b, c, d):
    return (a + d) + 23.0 * (b + c)


def der4(a, b, c, d):
    return (d - a) + 5.0 * (c - b)


def filter_plane(filt, comp, layer, get_rows, tiles, low, high0, high1):
    tile_rows = [get_rows(t) for t in range(tiles)]
    row = lax.broadcasted_iota(jnp.int32, tile_rows[0].shape, 0)
    down = [pltpu.roll(v, 1, 0) for v in tile_rows]
    up = [pltpu.roll(v, 7, 0) for v in tile_rows]
    up2 = [pltpu.roll(v, 6, 0) for v in tile_rows]
    for t in range(tiles):
        b = tile_rows[t]
        a = jnp.where(row == 0, down[t - 1] if t else low, down[t])
        if t + 1 < tiles:
            c = jnp.where(row == 7, up[t + 1], up[t])
            d = jnp.where(row >= 6, up2[t + 1], up2[t])
        else:
            c = jnp.where(row == 7, high0, up[t])
            d = jnp.where(row == 6, high0, jnp.where(row == 7, high1, up2[t]))
        val_y = val4(a, b, c, d)
        der_y = der4(a, b, c, d)
        before, after, after2 = lane_shifts(val_y)
        span = pl.ds(8 * t, 8)
        filt[comp, 0, layer, span, :] = val4(before, val_y, after, after2)
        filt[comp, 2, layer, span, :] = der4(before, val_y, after, after2)
        before, after, after2 = lane_shifts(der_y)
        filt[comp, 1, layer, span, :] = val4(before, der_y, after, after2)


def densities(field, rows, finish):
    for tile in range(rows // 8):
        span = pl.ds(8 * tile, 8)
        gx = [der4(*field(comp, 0, span)) for comp in range(3)]
        gy = [val4(*field(comp, 1, span)) for comp in range(3)]
        gz = [val4(*field(comp, 2, span)) for comp in range(3)]
        sxy = gy[0] + gx[1]
        sxz = gz[0] + gx[2]
        syz = gz[1] + gy[2]
        trace = gx[0] + gy[1] + gz[2]
        square = gx[0] * gx[0] + gy[1] * gy[1] + gz[2] * gz[2]
        shear = sxy * sxy + sxz * sxz + syz * syz
        scale = GRAD_SCALE * GRAD_SCALE
        finish(span, (SHEAR * scale) * (square + 0.5 * shear) + (0.5 * LAME * scale) * (trace * trace))


def accumulate(ref, slot):
    load = pl.program_id(0)

    def finish(span, density):
        @pl.when(load == 0)
        def _():
            ref[slot, span, :] = density

        @pl.when(load > 0)
        def _():
            ref[slot, span, :] += density

    return finish


def inner_kernel(u_ref, yh_ref, energy_ref, tail_ref, filt):
    own_x, rows = u_ref.shape[2:4]

    def own_layer(layer, carry):
        for comp in range(3):
            edge = [yh_ref[0, comp, k, pl.ds(layer, 1), :] for k in range(3)]
            get_rows = lambda t: u_ref[0, comp, layer, 8 * t : 8 * t + 8, :]
            filter_plane(filt, comp, layer, get_rows, rows // 8, *edge)
        return carry

    lax.fori_loop(0, own_x, own_layer, 0)

    def slot_step(slot, carry):
        field = lambda comp, which, span: [filt[comp, which, slot + k, span, :] for k in range(4)]
        densities(field, rows, accumulate(energy_ref, slot))
        return carry

    lax.fori_loop(0, own_x - 3, slot_step, 0)
    for comp in range(3):
        for which in range(3):
            for k in range(3):
                tail_ref[0, comp, which, k] = filt[comp, which, own_x - 3 + k]


def outer_kernel(place_ref, tail_ref, next_ref, inner_ref, solid_ref, msg_ref, filt, energy, turned):
    load = pl.program_id(0)
    own_x, rows, blocks = solid_ref.shape
    size_z = next_ref.shape[1]
    loads = 3
    inner = own_x - 3
    tiles = rows // 8
    keep = jnp.where(place_ref[2] == 1, 0.0, 1.0)
    for comp in range(3):
        for k in range(3):
            layer = (load * 3 + comp) * 3 + k
            corner = loads * 9 * rows + rows
            edge = [next_ref[pl.ds(corner + (load * 3 + comp) * 9 + 3 * which + k, 1), :] for which in range(3)]
            get_rows = lambda t: next_ref[pl.ds(pl.multiple_of(layer * rows + 8 * t, 8), 8), :]
            filter_plane(filt, comp, k, get_rows, tiles, *edge)

    def density_at(slot, masked):
        def field(comp, which, span):
            out = []
            for k in range(4):
                at = slot + k
                value = tail_ref[0, comp, which, at, span, :] if at < 3 else filt[comp, which, at - 3, span, :]
                out.append(value * keep if masked[k] else value)
            return out

        densities(field, rows, accumulate(energy, slot))

    density_at(0, (False, False, False, True))
    density_at(1, (False, False, True, True))
    density_at(2, (True, False, False, False))

    @pl.when(load == pl.num_programs(0) - 1)
    def _():
        peak = jnp.zeros((8, 128), jnp.float32)
        groups = own_x // 4
        block_of = lax.broadcasted_iota(jnp.int32, (blocks, size_z), 1) // (size_z // blocks)
        spread = jnp.where(block_of == lax.broadcasted_iota(jnp.int32, (blocks, size_z), 0), 1.0, 0.0)
        for g in range(groups):
            stack = []
            for q in range(4):
                x = 4 * g + q
                if x < own_x - 1:
                    solid = jnp.dot(solid_ref[x + 1].astype(jnp.float32), spread, preferred_element_type=jnp.float32)
                    stiff = 0.2 + 0.8 * solid
                else:
                    stiff = next_ref[loads * 9 * rows : loads * 9 * rows + rows, :]
                value = (inner_ref[x] if x < inner else energy[x - inner]) * stiff
                stack.append(value)
                for tile in range(tiles):
                    for b in range(size_z // 128):
                        peak = jnp.maximum(peak, value[8 * tile : 8 * tile + 8, 128 * b : 128 * b + 128])
            turned[g, 0:8, :] = jnp.zeros((8, 128), jnp.float32)
            turned[g, size_z : size_z + 16, :] = jnp.zeros((16, 128), jnp.float32)
            turned[g, HALO : HALO + size_z, :] = jnp.concatenate(stack, axis=0).T
        peak = jnp.broadcast_to(jnp.max(peak, axis=0, keepdims=True), (8, 128))
        peak = jnp.broadcast_to(jnp.max(peak, axis=1, keepdims=True), (8, 128))
        parts = msg_ref.shape[0] // 88
        own_z = size_z // parts
        quads = (own_z + 2 * HALO) // 4
        lane = lax.broadcasted_iota(jnp.int32, (parts, 128), 1) // rows
        for g in range(groups):
            for j in range(quads):
                picked = [turned[g, pl.ds(4 * j + k, parts, stride=own_z), :] for k in range(4)]
                for q in range(4):
                    out = None
                    for k in range(4):
                        shift = (rows * (k - q)) % 128
                        part = pltpu.roll(picked[k], shift, 1) if shift else picked[k]
                        out = part if out is None else jnp.where(lane == k, part, out)
                    msg_ref[pl.ds(16 * j + 4 * g + q, parts, stride=88), :] = out
        for t in range(parts):
            msg_ref[pl.ds(88 * t + 80, 8), :] = peak


def load_block(*shape):
    return pl.BlockSpec((1,) + shape, lambda l: (l,) + (0,) * len(shape))


def fixed_block(*shape):
    return pl.BlockSpec(shape, lambda l: (0,) * len(shape))


def inner_strain(disp, yh):
    loads, comps, own_x, rows, size_z = disp.shape
    return pl.pallas_call(
        inner_kernel,
        grid=(loads,),
        out_shape=(
            jax.ShapeDtypeStruct((own_x - 3, rows, size_z), jnp.float32),
            jax.ShapeDtypeStruct((loads, comps, 3, 3, rows, size_z), jnp.float32),
        ),
        in_specs=[load_block(comps, own_x, rows, size_z), load_block(comps, 3, own_x, size_z)],
        out_specs=(fixed_block(own_x - 3, rows, size_z), load_block(comps, 3, 3, rows, size_z)),
        scratch_shapes=[
            pltpu.VMEM((3, 3, own_x, rows, size_z), jnp.float32),
        ],
        compiler_params=pltpu.CompilerParams(vmem_limit_bytes=48 << 20),
        cost_estimate=pl.CostEstimate(flops=40000 * 4096, bytes_accessed=1 << 20, transcendentals=0),
    )(disp, yh)


def strain_message(place, tail, beyond, inner, solid, parts):
    loads, comps = tail.shape[:2]
    own_x, rows, blocks = solid.shape
    size_z = beyond.shape[1]
    return pl.pallas_call(
        outer_kernel,
        grid=(loads,),
        out_shape=jax.ShapeDtypeStruct((parts * 88, 128), jnp.float32),
        in_specs=[
            pl.BlockSpec(memory_space=pltpu.SMEM),
            load_block(comps, 3, 3, rows, size_z),
            fixed_block(*beyond.shape),
            fixed_block(own_x - 3, rows, size_z),
            fixed_block(own_x, rows, blocks),
        ],
        out_specs=fixed_block(parts * 88, 128),
        scratch_shapes=[
            pltpu.VMEM((3, 3, 3, rows, size_z), jnp.float32),
            pltpu.VMEM((3, rows, size_z), jnp.float32),
            pltpu.VMEM((own_x // 4, size_z + 16, 128), jnp.float32),
        ],
        compiler_params=pltpu.CompilerParams(vmem_limit_bytes=48 << 20),
        cost_estimate=pl.CostEstimate(flops=10000 * 4096, bytes_accessed=1 << 20, transcendentals=0),
    )(place, tail, beyond, inner, solid)


def ring(axis, step):
    count = lax.axis_size(axis)
    return [(i, i + step) for i in range(count) if 0 <= i + step < count]


def newton_reciprocal(x):
    r = pl.reciprocal(x, approx=True)
    return r * (2.0 - x * r)


def weno_cell(d, e0, e1, e2, e3):
    f0 = e1 - e0
    f1 = e2 - e1
    f2 = e3 - e2
    g0 = f1 - f0
    g1 = f2 - f1
    twice1 = e1 + e1
    twice2 = e2 + e2
    third = 13.0 / 3.0
    eps = 4.0 * WENO_EPS
    pa = twice1 + f0
    pb = twice1 + f1
    pc = twice2 - f2
    a = (f0 * f0 * third + eps) + pa * pa
    b = (f1 * f1 * third + eps) + pb * pb
    c = (f2 * f2 * third + eps) + pc * pc
    a = a * a
    b = b * b * (1.0 / 6.0)
    c = c * c
    ac = a * c
    ab = a * b
    cb = c * b
    u = cb * g0
    v = ab * g1
    both = u + v
    both = both + both
    s = e1 + e2
    d6 = 6.0 * d
    minus = d6 + (s + e2) - (both + v) * newton_reciprocal(ac + cb + 3.0 * ab)
    plus = (s + e1) - d6 - (both + u) * newton_reciprocal(ac + ab + 3.0 * cb)
    return minus, plus


def godunov(minus, plus):
    high = jnp.maximum(jnp.maximum(minus, plus), 0.0)
    low = jnp.minimum(jnp.minimum(minus, plus), 0.0)
    return high * high, low * low


def x_terms(phi):
    rows, size = phi.shape
    wide = size + 128
    phi = jnp.concatenate([phi, jnp.ones((rows, 128), jnp.float32)], axis=1)
    d = pltpu.roll(phi, wide - 1, 1) - phi
    e = pltpu.roll(d, wide - 1, 1) - d
    minus, plus = weno_cell(
        d, pltpu.roll(e, 2, 1), pltpu.roll(e, 1, 1), e, pltpu.roll(e, wide - 1, 1)
    )
    return godunov(pltpu.roll(minus, 1, 1)[:, :size], plus[:, :size])


def next_rows(tiles, step, count):
    row = lax.broadcasted_iota(jnp.int32, tiles[0].shape, 0)
    turned = [pltpu.roll(v, 8 - step, 0) for v in tiles]
    last = len(tiles) - 1
    return [jnp.where(row < 8 - step, turned[t], turned[min(t + 1, last)]) for t in range(count)]


def y_stage(phi_ref, layer, span, gp_ref, gm_ref, mid_ref, z, exact):
    tiles = gp_ref.shape[1] // 8
    cells = tiles + 1 if exact else tiles
    count = min(cells + 1, phi_ref.shape[1] // 8)
    phi = [phi_ref[layer, 8 * t : 8 * t + 8, span] for t in range(count)]
    d = [n - p for n, p in zip(next_rows(phi, 1, count), phi)]
    e = [n - p for n, p in zip(next_rows(d, 1, count), d)]
    d2 = next_rows(d, 2, cells)
    e1, e2, e3 = (next_rows(e, k, cells) for k in (1, 2, 3))
    sides = [weno_cell(d2[t], e[t], e1[t], e2[t], e3[t]) for t in range(cells)]
    plus = next_rows([p for _, p in sides], 1, tiles)
    mid = next_rows(phi, 3, tiles)
    for t in range(tiles):
        rows = slice(8 * t, 8 * t + 8)
        gp_ref[z, rows, span], gm_ref[z, rows, span] = godunov(sides[t][0], plus[t])
        mid_ref[z, rows, span] = mid[t]


def xy_stage(phi_ref, layer0, layers, gp_ref, gm_ref, mid_ref, exact=False):
    _, rows, lanes = gp_ref.shape

    def layer_step(z, carry):
        for block in range(lanes // 128):
            y_stage(phi_ref, z + layer0, slice(128 * block, 128 * block + 128), gp_ref, gm_ref, mid_ref, z, exact)
        for t in range(rows // 8):
            xp, xm = x_terms(mid_ref[z, 8 * t : 8 * t + 8, :])
            gp_ref[z, 8 * t : 8 * t + 8, :] += xp
            gm_ref[z, 8 * t : 8 * t + 8, :] += xm
        return carry

    lax.fori_loop(0, layers, layer_step, 0)


def z_stage(get_phi, layers, rows, lanes, finish):
    def lane_step(block, carry):
        span = pl.ds(pl.multiple_of(128 * block, 128), 128)
        for t in range(rows // 8):
            p = [get_phi(z, t, span) for z in range(-3, layers + 3)]
            d = [p[k + 1] - p[k] for k in range(len(p) - 1)]
            e = [d[k + 1] - d[k] for k in range(len(d) - 1)]
            before = None
            for cell in range(layers + 1):
                minus, plus = weno_cell(d[cell + 2], e[cell], e[cell + 1], e[cell + 2], e[cell + 3])
                if before is not None:
                    finish(cell - 1, t, span, p[cell + 2], *godunov(before, plus))
                before = minus
        return carry

    lax.fori_loop(0, lanes // 128, lane_step, 0)


def layer_rows(mid_ref, edges, z, t, span):
    layers = mid_ref.shape[0]
    if z < 0:
        return edges[z + 3, 8 * t : 8 * t + 8, span]
    if z >= layers:
        return edges[z - layers + 3, 8 * t : 8 * t + 8, span]
    return mid_ref[z, 8 * t : 8 * t + 8, span]


def first_gradient_kernel(place_ref, tall_ref, ra_ref, rb_ref, ls_ref, sp_ref, sm_ref, mid_ref, edges):
    layers, rows, lanes = sp_ref.shape
    depth, own, _ = tall_ref.shape
    ones = jnp.ones((8, lanes), jnp.float32)

    def copy(z, carry):
        for t in range(ls_ref.shape[1] // 8):
            ls_ref[z, 8 * t : 8 * t + 8, :] = ones
        ls_ref[z, YE : YE + own, :] = tall_ref[z]
        return carry

    lax.fori_loop(0, depth, copy, 0)

    def below(ref):
        @pl.when(place_ref[4] == 0)
        def _():
            for z in range(depth):
                ls_ref[z, YE - 8 : YE, :] = ref[z]
                ls_ref[z, YE - 9 : YE - 8, :] = ref[depth + z // 8, z % 8 : z % 8 + 1, :]

    def above(ref):
        @pl.when(place_ref[5] == 0)
        def _():
            for z in range(depth):
                ls_ref[z, YE + own : YE + own + 8, :] = ref[z]
                ls_ref[z, YE + own + 8 : YE + own + 9, :] = ref[depth + z // 8, z % 8 : z % 8 + 1, :]

    @pl.when(place_ref[3] == 1)
    def _():
        above(ra_ref)
        below(rb_ref)

    @pl.when(place_ref[3] == 0)
    def _():
        below(ra_ref)
        above(rb_ref)

    for k in range(6):
        layer = k if k < 3 else depth - 6 + k
        tiles = [ls_ref[layer, 8 * t : 8 * t + 8, :] for t in range(rows // 8 + 1)]
        for t, value in enumerate(next_rows(tiles, 3, rows // 8)):
            edges[k, 8 * t : 8 * t + 8, :] = value
    xy_stage(ls_ref, 3, layers, sp_ref, sm_ref, mid_ref)

    def finish(z, t, span, phi, gp, gm):
        where = pl.ds(8 * t, 8)
        scale = TIME_STEP / 6.0
        sp_ref[z, where, span] = scale * jnp.sqrt(sp_ref[z, where, span] + gp)
        sm_ref[z, where, span] = scale * jnp.sqrt(sm_ref[z, where, span] + gm)

    z_stage(
        lambda z, t, span: layer_rows(mid_ref, edges, z, t, span), layers, rows, lanes, finish
    )


def vmem_call(kernel, outs, args, scratch=(), cycles=0, limit=8):
    specs = []
    for arg in args:
        space = pltpu.SMEM if arg.dtype == jnp.int32 else pltpu.VMEM
        specs.append(pl.BlockSpec(memory_space=space))
    return pl.pallas_call(
        kernel,
        out_shape=tuple(jax.ShapeDtypeStruct(shape, jnp.float32) for shape in outs),
        in_specs=specs,
        out_specs=tuple(pl.BlockSpec(memory_space=pltpu.VMEM) for _ in outs),
        scratch_shapes=[pltpu.VMEM(shape, jnp.float32) for shape in scratch],
        compiler_params=pltpu.CompilerParams(vmem_limit_bytes=limit << 20),
        cost_estimate=pl.CostEstimate(flops=cycles * 4096, bytes_accessed=1 << 20, transcendentals=0),
    )(*args)


def place_flags():
    wide, narrow = lax.axis_index("wide"), lax.axis_index("narrow")
    flags = [
        1 - wide % 2, wide == 0, wide == lax.axis_size("wide") - 1,
        1 - narrow % 2, narrow == 0, narrow == lax.axis_size("narrow") - 1,
    ]
    return jnp.stack([jnp.asarray(f).astype(jnp.int32) for f in flags])


def y_inside(place_ref, base, first_row, shape, rows):
    row = lax.broadcasted_iota(jnp.int32, shape, 0) + (first_row - base)
    inside = (row >= 0) | (place_ref[4] == 0)
    return inside & ((row < rows) | (place_ref[5] == 0))


def extend_kernel(
    place_ref, tile_ref, ra_ref, rb_ref, pa_ref, pb_ref, pc_ref, po_ref, ls_ref, sp_ref, sm_ref, mid_ref,
    speed_ref, speed3_ref, phi_ref, ma_ref, mb_ref, one, two, keep, pull,
):
    depth, rows, lanes = tile_ref.shape
    layers = depth - 2 * HALO
    tall = ls_ref.shape[1]
    margin = 8
    base = margin + YE
    peak = jnp.maximum(jnp.maximum(pa_ref[...], pb_ref[...]), jnp.maximum(pc_ref[...], po_ref[...]))
    scale = 1.0 / (peak[0:1, 0:1] + 1e-06)

    def assemble(z, carry):
        one[z, base : base + rows, :] = tile_ref[z]
        return carry

    lax.fori_loop(0, depth, assemble, 0)

    def below(ref):
        for z in range(depth):
            one[z, base - 8 : base, :] = ref[z]
            one[z, base - 10 : base - 8, :] = ref[depth + z // 4, 2 * (z % 4) : 2 * (z % 4) + 2, :]

    def above(ref):
        for z in range(depth):
            one[z, base + rows : base + rows + 8, :] = ref[z]
            one[z, base + rows + 8 : base + rows + 10, :] = ref[depth + z // 4, 2 * (z % 4) : 2 * (z % 4) + 2, :]

    @pl.when(place_ref[3] == 1)
    def _():
        above(ra_ref)
        below(rb_ref)

    @pl.when(place_ref[3] == 0)
    def _():
        below(ra_ref)
        above(rb_ref)

    def inside(z, first_row):
        outside = ((z < HALO) & (place_ref[1] == 1)) | ((z >= depth - HALO) & (place_ref[2] == 1))
        return y_inside(place_ref, YE, first_row, (8, lanes), rows) & jnp.logical_not(outside)

    def normalise(z, carry):
        for t in range(-1, tall // 8):
            at = slice(margin + 8 * t, margin + 8 * t + 8)
            one[z, at, :] = jnp.where(inside(z, 8 * t), one[z, at, :] * scale - 0.5, 0.0)
        return carry

    def weigh(z, carry):
        for t in range(tall // 8):
            span = slice(8 * t, 8 * t + 8)
            ls = ls_ref[z - 1, span, :]
            weight = newton_reciprocal(1.0 + 4.0 * ls * ls)
            keep[z, span, :] = weight * one[z, margin + 8 * t : margin + 8 * t + 8, :]
            pull[z, span, :] = jnp.where(inside(z, 8 * t), (1.0 - weight) * (1.0 / 6.0), 0.0)
        return carry

    lax.fori_loop(0, depth, normalise, 0)
    lax.fori_loop(1, depth - 1, weigh, 0)
    for step in range(EXT_PASSES):
        source, target = (one, two) if step % 2 == 0 else (two, one)

        def extend(z, carry):
            count = tall // 8
            tiles = [source[z, 8 * t : 8 * t + 8, :] for t in range(count + 2)]
            row = lax.broadcasted_iota(jnp.int32, tiles[0].shape, 0)
            lane = lax.broadcasted_iota(jnp.int32, tiles[0].shape, 1)
            down = [pltpu.roll(v, 1, 0) for v in tiles[:-1]]
            up = [pltpu.roll(v, 7, 0) for v in tiles[1:]]
            for t in range(count):
                at = margin + 8 * t
                centre = tiles[t + 1]
                total = source[z - 1, at : at + 8, :] + source[z + 1, at : at + 8, :]
                total = total + jnp.where(row == 0, down[t], down[t + 1])
                total = total + jnp.where(row == 7, up[t + 1], up[t])
                total = total + jnp.where(lane == 0, 0.0, pltpu.roll(centre, 1, 1))
                total = total + jnp.where(lane == lanes - 1, 0.0, pltpu.roll(centre, lanes - 1, 1))
                span = slice(8 * t, 8 * t + 8)
                target[z, at : at + 8, :] = keep[z, span, :] + pull[z, span, :] * total
            return carry

        lax.fori_loop(step + 1, depth - 1 - step, extend, 0)

    final = one if EXT_PASSES % 2 == 0 else two

    def march(z, carry):
        count = tall // 8
        tiles = [final[z + HALO, margin + 8 * t : margin + 8 * t + 8, :] for t in range(count)]
        moved = next_rows(tiles, YE - Y1, count - 1)
        for t in range(count - 1):
            span = slice(8 * t, 8 * t + 8)
            speed = moved[t]
            change = jnp.maximum(speed, 0.0) * sp_ref[z, span, :] + jnp.minimum(speed, 0.0) * sm_ref[z, span, :]
            phi = mid_ref[z, span, :] - change
            phi_ref[z, span, :] = jnp.where(y_inside(place_ref, Y1, 8 * t, phi.shape, rows), phi, 1.0)
        for t, value in enumerate(next_rows(tiles, YE - Y2, speed3_ref.shape[1] // 8)):
            speed3_ref[z, 8 * t : 8 * t + 8, :] = value
        for t, value in enumerate(next_rows(tiles[1:], YE - 8, rows // 8)):
            speed_ref[z, 8 * t : 8 * t + 8, :] = value
        return carry

    lax.fori_loop(0, layers, march, 0)
    send_edges(place_ref, phi_ref, Y1 - Y2, ma_ref, mb_ref)


def send_edges(place_ref, phi_ref, offset, ma_ref, mb_ref):
    layers = phi_ref.shape[0]
    count = ma_ref.shape[1]
    upper = place_ref[0] * (layers - 3)
    lower = (1 - place_ref[0]) * (layers - 3)
    for k in range(3):
        ma_ref[k] = phi_ref[upper + k, offset : offset + count, :]
        mb_ref[k] = phi_ref[lower + k, offset : offset + count, :]


def take_edges(place_ref, ra_ref, rb_ref, edges):
    upper = 3 * place_ref[0]
    lower = 3 - upper
    for k in range(3):
        edges[upper + k] = ra_ref[k]
        edges[lower + k] = rb_ref[k]

    @pl.when(place_ref[1] == 1)
    def _():
        edges[0:3] = jnp.ones((3,) + tuple(edges.shape[1:]), jnp.float32)

    @pl.when(place_ref[2] == 1)
    def _():
        edges[3:6] = jnp.ones((3,) + tuple(edges.shape[1:]), jnp.float32)


def plane_kernel(exact, phi_ref, gp_ref, gm_ref, mid_ref):
    xy_stage(phi_ref, 0, gp_ref.shape[0], gp_ref, gm_ref, mid_ref, exact)


def finish_kernel(
    rows, place_ref, phi_ref, ra_ref, rb_ref, gp_ref, gm_ref, speed_ref, *rest
):
    out_ref, edges = rest[0], rest[-1]
    layers, count, lanes = out_ref.shape
    base = Y2 if count > rows else 0
    take_edges(place_ref, ra_ref, rb_ref, edges)
    get_phi = functools.partial(layer_rows, phi_ref, edges)

    def finish(z, t, span, phi, gp, gm):
        where = pl.ds(8 * t, 8)
        speed = speed_ref[z, where, span]
        total = jnp.where(speed > 0.0, gp_ref[z, where, span] + gp, gm_ref[z, where, span] + gm)
        phi = phi - (TIME_STEP / 6.0) * speed * jnp.sqrt(total)
        if count > rows:
            phi = jnp.where(y_inside(place_ref, base, 8 * t, phi.shape, rows), phi, 1.0)
        out_ref[z, where, span] = phi

    z_stage(get_phi, layers, count, lanes, finish)
    if len(rest) > 2:
        send_edges(place_ref, out_ref, Y2, rest[1], rest[2])


def swaps(axis):
    count = lax.axis_size(axis)
    first, second = [], []
    for i in range(0, count, 2):
        first += [(i, i + 1), (i + 1, i)]
        if i + 2 < count:
            second += [(i + 1, i + 2), (i + 2, i + 1)]
    return first, second


def stack_kernel(place_ref, ls_ref, ra_ref, rb_ref, tall_ref, ma_ref, mb_ref, edges):
    layers, rows = ls_ref.shape[:2]
    take_edges(place_ref, ra_ref, rb_ref, edges)
    for k in range(3):
        tall_ref[k] = edges[k]
        tall_ref[layers + 3 + k] = edges[3 + k]

    def copy(z, carry):
        tall_ref[z + 3] = ls_ref[z]
        return carry

    lax.fori_loop(0, layers, copy, 0)
    depth = layers + 6

    def upper(ref):
        for z in range(depth):
            ref[z] = tall_ref[z, rows - 8 : rows, :]
            ref[depth + z // 8, z % 8 : z % 8 + 1, :] = tall_ref[z, rows - 9 : rows - 8, :]

    def lower(ref):
        for z in range(depth):
            ref[z] = tall_ref[z, 0:8, :]
            ref[depth + z // 8, z % 8 : z % 8 + 1, :] = tall_ref[z, 8:9, :]

    @pl.when(place_ref[3] == 1)
    def _():
        upper(ma_ref)
        lower(mb_ref)

    @pl.when(place_ref[3] == 0)
    def _():
        lower(ma_ref)
        upper(mb_ref)


def level_part(place, tile, ma, mb, wide_peak, level_set, ls, sp, sm, mid):
    layers, rows, lanes = level_set.shape
    nfirst, nsecond = swaps("narrow")
    wfirst, wsecond = swaps("wide")
    count = lax.axis_size("narrow")
    across = [(i, (i + count // 2) % count) for i in range(count)]
    mirror = [(i, count - 1 - i) for i in range(count)]
    ra = lax.ppermute(ma, "narrow", nfirst)
    rb = lax.ppermute(mb, "narrow", nsecond)
    pc = lax.ppermute(wide_peak, "narrow", across)
    pb = lax.ppermute(wide_peak, "narrow", mirror)
    pa = ra[-1, :, :128]
    tall = ls.shape[1]
    rows1 = -(-(rows + 2 * Y1) // 8) * 8
    rows2 = -(-(rows + 2 * Y2) // 8) * 8
    depth = layers + 2 * HALO
    speed, speed3, phi, sa, sb = vmem_call(
        extend_kernel,
        [(layers, rows, lanes), (layers, rows2, lanes), (layers, rows1, lanes), (3, rows2, lanes), (3, rows2, lanes)],
        (place, tile, ra, rb, pa, pb, pc, wide_peak, ls, sp, sm, mid),
        [(depth, tall + 16, lanes)] * 2 + [(depth, tall, lanes)] * 2,
        8000,
        16,
    )
    ga = lax.ppermute(sa, "wide", wfirst)
    gb = lax.ppermute(sb, "wide", wsecond)
    gp, gm, mid = vmem_call(functools.partial(plane_kernel, False), [(layers, rows2, lanes)] * 3, (phi,), (), 12000)
    phi, sa, sb = vmem_call(
        functools.partial(finish_kernel, rows),
        [(layers, rows2, lanes), (3, rows, lanes), (3, rows, lanes)],
        (place, mid, ga, gb, gp, gm, speed3),
        [(6, rows2, lanes)],
        5000,
    )
    ga = lax.ppermute(sa, "wide", wfirst)
    gb = lax.ppermute(sb, "wide", wsecond)
    gp, gm, mid = vmem_call(functools.partial(plane_kernel, True), [(layers, rows, lanes)] * 3, (phi,), (), 12000)
    (phi,) = vmem_call(
        functools.partial(finish_kernel, rows),
        [(layers, rows, lanes)],
        (place, mid, ga, gb, gp, gm, speed),
        [(6, rows, lanes)],
        5000,
    )
    return phi, speed


def first_gradient(place, tall, ra, rb):
    depth, rows, lanes = tall.shape
    rows1 = -(-(rows + 2 * Y1) // 8) * 8
    total = -(-(rows + 2 * YE) // 8) * 8
    return vmem_call(
        first_gradient_kernel, [(depth, total, lanes)] + [(depth - 6, rows1, lanes)] * 3, (place, tall, ra, rb),
        [(6, rows1, lanes)], 35000
    )


def stack_level(place, level_set, ra, rb):
    layers, rows, lanes = level_set.shape
    depth = layers + 6
    edge = (depth + -(-depth // 8), 8, lanes)
    return vmem_call(
        stack_kernel, [(depth, rows, lanes), edge, edge], (place, level_set, ra, rb), [(6, rows, lanes)], 1500
    )


def unpack_kernel(place_ref, recv_ref, tile_ref, peak_ref, ma_ref, mb_ref):
    parts = recv_ref.shape[0]
    depth, rows, lanes = tile_ref.shape
    for j in range(depth // 4):
        block = recv_ref[:, 16 * j : 16 * j + 16, :].reshape(parts * 16, 128)
        wide = pltpu.roll(block.T, 1, 1)
        for k in range(4):
            tile_ref[4 * j + k] = wide[rows * k : rows * (k + 1), :]
    peak = recv_ref[0, 80:88, :]
    for s in range(1, parts):
        peak = jnp.maximum(peak, recv_ref[s, 80:88, :])
    peak_ref[...] = peak
    fill_edges(place_ref, tile_ref, peak, ma_ref, mb_ref)


def fill_edges(place_ref, tile_ref, peak, ma_ref, mb_ref):
    depth, rows, lanes = tile_ref.shape

    def upper(ref):
        for z in range(depth):
            ref[z] = tile_ref[z, rows - 8 : rows, :]
            ref[depth + z // 4, 2 * (z % 4) : 2 * (z % 4) + 2, :] = tile_ref[z, rows - 10 : rows - 8, :]

    def lower(ref):
        for z in range(depth):
            ref[z] = tile_ref[z, 0:8, :]
            ref[depth + z // 4, 2 * (z % 4) : 2 * (z % 4) + 2, :] = tile_ref[z, 8:10, :]

    last = ma_ref.shape[0] - 1
    ma_ref[last, :, 0:128] = peak
    mb_ref[last, :, 0:128] = peak

    @pl.when(place_ref[3] == 1)
    def _():
        upper(ma_ref)
        lower(mb_ref)

    @pl.when(place_ref[3] == 0)
    def _():
        lower(ma_ref)
        upper(mb_ref)


def unpack(place, recv, own_z, rows):
    parts = recv.shape[0]
    lanes = parts * 16
    depth = own_z + 2 * HALO
    edge = (depth + depth // 4 + 1, 8, lanes)
    return vmem_call(
        unpack_kernel, [(depth, rows, lanes), (8, 128), edge, edge], (place, recv), (), 1500
    )


def per_device(displacement, material, level_set):
    wide = lax.axis_size("wide")
    loads, comps, own_x, rows, size_z = displacement.shape
    own_z, _, size_x = level_set.shape
    place = place_flags()
    backward = [(i, (i - 1) % wide) for i in range(wide)]
    wfirst, wsecond = swaps("wide")
    nfirst, nsecond = swaps("narrow")

    low = lax.ppermute(displacement[:, :, :, -1], "narrow", ring("narrow", 1))
    high = lax.ppermute(
        jnp.stack([displacement[:, :, :, 0], displacement[:, :, :, 1]], axis=2), "narrow", ring("narrow", -1)
    )
    yh = jnp.concatenate([low[:, :, None], high], axis=2)
    bounds = level_set[:3], level_set[own_z - 3 :]
    even = place[0] == 1
    la = lax.ppermute(jnp.where(even, bounds[1], bounds[0]), "wide", wfirst)
    lb = lax.ppermute(jnp.where(even, bounds[0], bounds[1]), "wide", wsecond)

    stiff = 0.2 + 0.8 * jnp.repeat(material[0].astype(jnp.float32), BZ, axis=1)
    layers, yh, la, lb = lax.optimization_barrier((displacement[:, :, :3], yh, la, lb))
    flat = [layers.reshape(-1, size_z), stiff, yh[:, :, :, :3].reshape(-1, size_z)]
    flat.append(jnp.zeros((-sum(f.shape[0] for f in flat) % 8, size_z), jnp.float32))
    beyond = lax.ppermute(jnp.concatenate(flat, axis=0), "wide", backward)
    inner, tail = inner_strain(displacement, yh)
    la, lb, inner = lax.optimization_barrier((la, lb, inner))
    tall, ya, yb = stack_level(place, level_set, la, lb)
    ya = lax.ppermute(ya, "narrow", nfirst)
    yb = lax.ppermute(yb, "narrow", nsecond)
    beyond, ya, yb = lax.optimization_barrier((beyond, ya, yb))
    message = strain_message(place, tail, beyond, inner, material, wide)
    message, tall = lax.optimization_barrier((message, tall))
    recv = lax.all_to_all(message.reshape(wide, 88, 128), "wide", split_axis=0, concat_axis=0, tiled=True)
    ls, sp, sm, mid = first_gradient(place, tall, ya, yb)
    recv, sp = lax.optimization_barrier((recv, sp))
    tile, wide_peak, ma, mb = unpack(place, recv, own_z, rows)
    return level_part(place, tile, ma, mb, wide_peak, level_set, ls, sp, sm, mid)


def solution(mesh):
    return jax.shard_map(
        per_device,
        mesh=mesh,
        in_specs=(
            P(None, None, "wide", "narrow", None),
            P("wide", "narrow", None),
            P("wide", "narrow", None),
        ),
        out_specs=(P("wide", "narrow", None), P("wide", "narrow", None)),
        check_vma=False,
    )
```

```python
import functools
import jax
import jax.numpy as jnp
from jax import lax
from jax.experimental import pallas as pl
from jax.experimental.pallas import tpu as pltpu
from jax.sharding import PartitionSpec as P

BZ = 16
EXT_PASSES = 4
HJ_STEPS = 3
SHEAR = 0.384615
LAME = 0.576923
WENO_EPS = 1e-06
TIME_STEP = 0.3
HALO = EXT_PASSES
GRAD_SCALE = 1.0 / (8.0 * 48.0 * 48.0)
YE = 9
Y1 = 6
Y2 = 3


def lane_shifts(value):
    blocks = [value[:, 128 * b : 128 * (b + 1)] for b in range(value.shape[1] // 128)]
    lane = lax.broadcasted_iota(jnp.int32, blocks[0].shape, 1)
    zero = jnp.zeros_like(blocks[0])
    outs = []
    for step in (-1, 1, 2):
        turned = [pltpu.roll(b, (-step) % 128, 1) for b in blocks]
        if step < 0:
            mask = lane < 1
            parts = [jnp.where(mask, turned[i - 1] if i > 0 else zero, turned[i]) for i in range(len(blocks))]
        else:
            mask = lane >= 128 - step
            parts = [
                jnp.where(mask, turned[i + 1] if i + 1 < len(blocks) else zero, turned[i])
                for i in range(len(blocks))
            ]
        outs.append(jnp.concatenate(parts, axis=1))
    return outs


def val4(a, b, c, d):
    return (a + d) + 23.0 * (b + c)


def der4(a, b, c, d):
    return (d - a) + 5.0 * (c - b)


def filter_plane(filt, comp, layer, get_rows, tiles, low, high0, high1):
    tile_rows = [get_rows(t) for t in range(tiles)]
    row = lax.broadcasted_iota(jnp.int32, tile_rows[0].shape, 0)
    down = [pltpu.roll(v, 1, 0) for v in tile_rows]
    up = [pltpu.roll(v, 7, 0) for v in tile_rows]
    up2 = [pltpu.roll(v, 6, 0) for v in tile_rows]
    for t in range(tiles):
        b = tile_rows[t]
        a = jnp.where(row == 0, down[t - 1] if t else low, down[t])
        if t + 1 < tiles:
            c = jnp.where(row == 7, up[t + 1], up[t])
            d = jnp.where(row >= 6, up2[t + 1], up2[t])
        else:
            c = jnp.where(row == 7, high0, up[t])
            d = jnp.where(row == 6, high0, jnp.where(row == 7, high1, up2[t]))
        val_y = val4(a, b, c, d)
        der_y = der4(a, b, c, d)
        before, after, after2 = lane_shifts(val_y)
        span = pl.ds(8 * t, 8)
        filt[comp, 0, layer, span, :] = val4(before, val_y, after, after2)
        filt[comp, 2, layer, span, :] = der4(before, val_y, after, after2)
        before, after, after2 = lane_shifts(der_y)
        filt[comp, 1, layer, span, :] = val4(before, der_y, after, after2)


def densities(field, rows, finish):
    for tile in range(rows // 8):
        span = pl.ds(8 * tile, 8)
        gx = [der4(*field(comp, 0, span)) for comp in range(3)]
        gy = [val4(*field(comp, 1, span)) for comp in range(3)]
        gz = [val4(*field(comp, 2, span)) for comp in range(3)]
        sxy = gy[0] + gx[1]
        sxz = gz[0] + gx[2]
        syz = gz[1] + gy[2]
        trace = gx[0] + gy[1] + gz[2]
        square = gx[0] * gx[0] + gy[1] * gy[1] + gz[2] * gz[2]
        shear = sxy * sxy + sxz * sxz + syz * syz
        scale = GRAD_SCALE * GRAD_SCALE
        finish(span, (SHEAR * scale) * (square + 0.5 * shear) + (0.5 * LAME * scale) * (trace * trace))


def accumulate(ref, slot):
    load = pl.program_id(0)

    def finish(span, density):
        @pl.when(load == 0)
        def _():
            ref[slot, span, :] = density

        @pl.when(load > 0)
        def _():
            ref[slot, span, :] += density

    return finish


def inner_kernel(u_ref, yh_ref, energy_ref, tail_ref, filt):
    own_x, rows = u_ref.shape[2:4]

    def own_layer(layer, carry):
        for comp in range(3):
            edge = [yh_ref[0, comp, k, pl.ds(layer, 1), :] for k in range(3)]
            get_rows = lambda t: u_ref[0, comp, layer, 8 * t : 8 * t + 8, :]
            filter_plane(filt, comp, layer, get_rows, rows // 8, *edge)
        return carry

    lax.fori_loop(0, own_x, own_layer, 0)

    def slot_step(slot, carry):
        field = lambda comp, which, span: [filt[comp, which, slot + k, span, :] for k in range(4)]
        densities(field, rows, accumulate(energy_ref, slot))
        return carry

    lax.fori_loop(0, own_x - 3, slot_step, 0)
    for comp in range(3):
        for which in range(3):
            for k in range(3):
                tail_ref[0, comp, which, k] = filt[comp, which, own_x - 3 + k]


def outer_kernel(place_ref, tail_ref, next_ref, inner_ref, solid_ref, msg_ref, filt, energy, turned):
    load = pl.program_id(0)
    own_x, rows, blocks = solid_ref.shape
    size_z = next_ref.shape[1]
    loads = 3
    inner = own_x - 3
    tiles = rows // 8
    keep = jnp.where(place_ref[2] == 1, 0.0, 1.0)
    for comp in range(3):
        for k in range(3):
            layer = (load * 3 + comp) * 3 + k
            corner = loads * 9 * rows + rows
            edge = [next_ref[pl.ds(corner + (load * 3 + comp) * 9 + 3 * which + k, 1), :] for which in range(3)]
            get_rows = lambda t: next_ref[pl.ds(pl.multiple_of(layer * rows + 8 * t, 8), 8), :]
            filter_plane(filt, comp, k, get_rows, tiles, *edge)

    def density_at(slot, masked):
        def field(comp, which, span):
            out = []
            for k in range(4):
                at = slot + k
                value = tail_ref[0, comp, which, at, span, :] if at < 3 else filt[comp, which, at - 3, span, :]
                out.append(value * keep if masked[k] else value)
            return out

        densities(field, rows, accumulate(energy, slot))

    density_at(0, (False, False, False, True))
    density_at(1, (False, False, True, True))
    density_at(2, (True, False, False, False))

    @pl.when(load == pl.num_programs(0) - 1)
    def _():
        peak = jnp.zeros((8, 128), jnp.float32)
        groups = own_x // 4
        block_of = lax.broadcasted_iota(jnp.int32, (blocks, size_z), 1) // (size_z // blocks)
        spread = jnp.where(block_of == lax.broadcasted_iota(jnp.int32, (blocks, size_z), 0), 1.0, 0.0)
        for g in range(groups):
            stack = []
            for q in range(4):
                x = 4 * g + q
                if x < own_x - 1:
                    solid = jnp.dot(solid_ref[x + 1].astype(jnp.float32), spread, preferred_element_type=jnp.float32)
                    stiff = 0.2 + 0.8 * solid
                else:
                    stiff = next_ref[loads * 9 * rows : loads * 9 * rows + rows, :]
                value = (inner_ref[x] if x < inner else energy[x - inner]) * stiff
                stack.append(value)
                for tile in range(tiles):
                    for b in range(size_z // 128):
                        peak = jnp.maximum(peak, value[8 * tile : 8 * tile + 8, 128 * b : 128 * b + 128])
            turned[g, 0:8, :] = jnp.zeros((8, 128), jnp.float32)
            turned[g, size_z : size_z + 16, :] = jnp.zeros((16, 128), jnp.float32)
            turned[g, HALO : HALO + size_z, :] = jnp.concatenate(stack, axis=0).T
        peak = jnp.broadcast_to(jnp.max(peak, axis=0, keepdims=True), (8, 128))
        peak = jnp.broadcast_to(jnp.max(peak, axis=1, keepdims=True), (8, 128))
        parts = msg_ref.shape[0] // 88
        own_z = size_z // parts
        quads = (own_z + 2 * HALO) // 4
        lane = lax.broadcasted_iota(jnp.int32, (parts, 128), 1) // rows
        for g in range(groups):
            for j in range(quads):
                picked = [turned[g, pl.ds(4 * j + k, parts, stride=own_z), :] for k in range(4)]
                for q in range(4):
                    out = None
                    for k in range(4):
                        shift = (rows * (k - q)) % 128
                        part = pltpu.roll(picked[k], shift, 1) if shift else picked[k]
                        out = part if out is None else jnp.where(lane == k, part, out)
                    msg_ref[pl.ds(16 * j + 4 * g + q, parts, stride=88), :] = out
        for t in range(parts):
            msg_ref[pl.ds(88 * t + 80, 8), :] = peak


def load_block(*shape):
    return pl.BlockSpec((1,) + shape, lambda l: (l,) + (0,) * len(shape))


def fixed_block(*shape):
    return pl.BlockSpec(shape, lambda l: (0,) * len(shape))


def inner_strain(disp, yh):
    loads, comps, own_x, rows, size_z = disp.shape
    return pl.pallas_call(
        inner_kernel,
        grid=(loads,),
        out_shape=(
            jax.ShapeDtypeStruct((own_x - 3, rows, size_z), jnp.float32),
            jax.ShapeDtypeStruct((loads, comps, 3, 3, rows, size_z), jnp.float32),
        ),
        in_specs=[load_block(comps, own_x, rows, size_z), load_block(comps, 3, own_x, size_z)],
        out_specs=(fixed_block(own_x - 3, rows, size_z), load_block(comps, 3, 3, rows, size_z)),
        scratch_shapes=[
            pltpu.VMEM((3, 3, own_x, rows, size_z), jnp.float32),
        ],
        compiler_params=pltpu.CompilerParams(vmem_limit_bytes=48 << 20),
        cost_estimate=pl.CostEstimate(flops=40000 * 4096, bytes_accessed=1 << 20, transcendentals=0),
    )(disp, yh)


def strain_message(place, tail, beyond, inner, solid, parts):
    loads, comps = tail.shape[:2]
    own_x, rows, blocks = solid.shape
    size_z = beyond.shape[1]
    return pl.pallas_call(
        outer_kernel,
        grid=(loads,),
        out_shape=jax.ShapeDtypeStruct((parts * 88, 128), jnp.float32),
        in_specs=[
            pl.BlockSpec(memory_space=pltpu.SMEM),
            load_block(comps, 3, 3, rows, size_z),
            fixed_block(*beyond.shape),
            fixed_block(own_x - 3, rows, size_z),
            fixed_block(own_x, rows, blocks),
        ],
        out_specs=fixed_block(parts * 88, 128),
        scratch_shapes=[
            pltpu.VMEM((3, 3, 3, rows, size_z), jnp.float32),
            pltpu.VMEM((3, rows, size_z), jnp.float32),
            pltpu.VMEM((own_x // 4, size_z + 16, 128), jnp.float32),
        ],
        compiler_params=pltpu.CompilerParams(vmem_limit_bytes=48 << 20),
        cost_estimate=pl.CostEstimate(flops=10000 * 4096, bytes_accessed=1 << 20, transcendentals=0),
    )(place, tail, beyond, inner, solid)


def ring(axis, step):
    count = lax.axis_size(axis)
    return [(i, i + step) for i in range(count) if 0 <= i + step < count]


def newton_reciprocal(x):
    r = pl.reciprocal(x, approx=True)
    return r * (2.0 - x * r)


def weno_cell(d, e0, e1, e2, e3):
    f0 = e1 - e0
    f1 = e2 - e1
    f2 = e3 - e2
    g0 = f1 - f0
    g1 = f2 - f1
    twice1 = e1 + e1
    twice2 = e2 + e2
    third = 13.0 / 3.0
    eps = 4.0 * WENO_EPS
    pa = twice1 + f0
    pb = twice1 + f1
    pc = twice2 - f2
    a = (f0 * f0 * third + eps) + pa * pa
    b = (f1 * f1 * third + eps) + pb * pb
    c = (f2 * f2 * third + eps) + pc * pc
    a = a * a
    b = b * b * (1.0 / 6.0)
    c = c * c
    ac = a * c
    ab = a * b
    cb = c * b
    u = cb * g0
    v = ab * g1
    both = u + v
    both = both + both
    s = e1 + e2
    d6 = 6.0 * d
    minus = d6 + (s + e2) - (both + v) * newton_reciprocal(ac + cb + 3.0 * ab)
    plus = (s + e1) - d6 - (both + u) * newton_reciprocal(ac + ab + 3.0 * cb)
    return minus, plus


def godunov(minus, plus):
    high = jnp.maximum(jnp.maximum(minus, plus), 0.0)
    low = jnp.minimum(jnp.minimum(minus, plus), 0.0)
    return high * high, low * low


def x_terms(phi):
    rows, size = phi.shape
    wide = size + 128
    phi = jnp.concatenate([phi, jnp.ones((rows, 128), jnp.float32)], axis=1)
    d = pltpu.roll(phi, wide - 1, 1) - phi
    e = pltpu.roll(d, wide - 1, 1) - d
    minus, plus = weno_cell(
        d, pltpu.roll(e, 2, 1), pltpu.roll(e, 1, 1), e, pltpu.roll(e, wide - 1, 1)
    )
    return godunov(pltpu.roll(minus, 1, 1)[:, :size], plus[:, :size])


def next_rows(tiles, step, count):
    row = lax.broadcasted_iota(jnp.int32, tiles[0].shape, 0)
    turned = [pltpu.roll(v, 8 - step, 0) for v in tiles]
    last = len(tiles) - 1
    return [jnp.where(row < 8 - step, turned[t], turned[min(t + 1, last)]) for t in range(count)]


def y_stage(phi_ref, layer, span, gp_ref, gm_ref, mid_ref, z, exact):
    tiles = gp_ref.shape[1] // 8
    cells = tiles + 1 if exact else tiles
    count = min(cells + 1, phi_ref.shape[1] // 8)
    phi = [phi_ref[layer, 8 * t : 8 * t + 8, span] for t in range(count)]
    d = [n - p for n, p in zip(next_rows(phi, 1, count), phi)]
    e = [n - p for n, p in zip(next_rows(d, 1, count), d)]
    d2 = next_rows(d, 2, cells)
    e1, e2, e3 = (next_rows(e, k, cells) for k in (1, 2, 3))
    sides = [weno_cell(d2[t], e[t], e1[t], e2[t], e3[t]) for t in range(cells)]
    plus = next_rows([p for _, p in sides], 1, tiles)
    mid = next_rows(phi, 3, tiles)
    for t in range(tiles):
        rows = slice(8 * t, 8 * t + 8)
        gp_ref[z, rows, span], gm_ref[z, rows, span] = godunov(sides[t][0], plus[t])
        mid_ref[z, rows, span] = mid[t]


def xy_stage(phi_ref, layer0, layers, gp_ref, gm_ref, mid_ref, exact=False):
    _, rows, lanes = gp_ref.shape

    def layer_step(z, carry):
        for block in range(lanes // 128):
            y_stage(phi_ref, z + layer0, slice(128 * block, 128 * block + 128), gp_ref, gm_ref, mid_ref, z, exact)
        for t in range(rows // 8):
            xp, xm = x_terms(mid_ref[z, 8 * t : 8 * t + 8, :])
            gp_ref[z, 8 * t : 8 * t + 8, :] += xp
            gm_ref[z, 8 * t : 8 * t + 8, :] += xm
        return carry

    lax.fori_loop(0, layers, layer_step, 0)


def z_stage(get_phi, layers, rows, lanes, finish):
    def lane_step(block, carry):
        span = pl.ds(pl.multiple_of(128 * block, 128), 128)
        for t in range(rows // 8):
            p = [get_phi(z, t, span) for z in range(-3, layers + 3)]
            d = [p[k + 1] - p[k] for k in range(len(p) - 1)]
            e = [d[k + 1] - d[k] for k in range(len(d) - 1)]
            before = None
            for cell in range(layers + 1):
                minus, plus = weno_cell(d[cell + 2], e[cell], e[cell + 1], e[cell + 2], e[cell + 3])
                if before is not None:
                    finish(cell - 1, t, span, p[cell + 2], *godunov(before, plus))
                before = minus
        return carry

    lax.fori_loop(0, lanes // 128, lane_step, 0)


def layer_rows(mid_ref, edges, z, t, span):
    layers = mid_ref.shape[0]
    if z < 0:
        return edges[z + 3, 8 * t : 8 * t + 8, span]
    if z >= layers:
        return edges[z - layers + 3, 8 * t : 8 * t + 8, span]
    return mid_ref[z, 8 * t : 8 * t + 8, span]


def first_gradient_kernel(place_ref, tall_ref, ra_ref, rb_ref, ls_ref, step_ref, edges):
    layers = step_ref.shape[0] // 3
    sp_ref, sm_ref, mid_ref = (step_ref.at[pl.ds(k * layers, layers)] for k in range(3))
    _, rows, lanes = step_ref.shape
    depth, own, _ = tall_ref.shape
    ones = jnp.ones((8, lanes), jnp.float32)

    def copy(z, carry):
        for t in range(ls_ref.shape[1] // 8):
            ls_ref[z, 8 * t : 8 * t + 8, :] = ones
        ls_ref[z, YE : YE + own, :] = tall_ref[z]
        return carry

    lax.fori_loop(0, depth, copy, 0)

    def below(ref):
        @pl.when(place_ref[4] == 0)
        def _():
            for z in range(depth):
                ls_ref[z, YE - 8 : YE, :] = ref[z]
                ls_ref[z, YE - 9 : YE - 8, :] = ref[depth + z // 8, z % 8 : z % 8 + 1, :]

    def above(ref):
        @pl.when(place_ref[5] == 0)
        def _():
            for z in range(depth):
                ls_ref[z, YE + own : YE + own + 8, :] = ref[z]
                ls_ref[z, YE + own + 8 : YE + own + 9, :] = ref[depth + z // 8, z % 8 : z % 8 + 1, :]

    @pl.when(place_ref[3] == 1)
    def _():
        above(ra_ref)
        below(rb_ref)

    @pl.when(place_ref[3] == 0)
    def _():
        below(ra_ref)
        above(rb_ref)

    for k in range(6):
        layer = k if k < 3 else depth - 6 + k
        tiles = [ls_ref[layer, 8 * t : 8 * t + 8, :] for t in range(rows // 8 + 1)]
        for t, value in enumerate(next_rows(tiles, 3, rows // 8)):
            edges[k, 8 * t : 8 * t + 8, :] = value
    xy_stage(ls_ref, 3, layers, sp_ref, sm_ref, mid_ref)

    def finish(z, t, span, phi, gp, gm):
        where = pl.ds(8 * t, 8)
        scale = TIME_STEP / 6.0
        sp_ref[z, where, span] = scale * jnp.sqrt(sp_ref[z, where, span] + gp)
        sm_ref[z, where, span] = scale * jnp.sqrt(sm_ref[z, where, span] + gm)

    z_stage(
        lambda z, t, span: layer_rows(mid_ref, edges, z, t, span), layers, rows, lanes, finish
    )


def vmem_call(kernel, outs, args, scratch=(), cycles=0, limit=8):
    specs = []
    for arg in args:
        space = pltpu.SMEM if arg.dtype == jnp.int32 else pltpu.VMEM
        specs.append(pl.BlockSpec(memory_space=space))
    return pl.pallas_call(
        kernel,
        out_shape=tuple(jax.ShapeDtypeStruct(shape, jnp.float32) for shape in outs),
        in_specs=specs,
        out_specs=tuple(pl.BlockSpec(memory_space=pltpu.VMEM) for _ in outs),
        scratch_shapes=[pltpu.VMEM(shape, jnp.float32) for shape in scratch],
        compiler_params=pltpu.CompilerParams(vmem_limit_bytes=limit << 20),
        cost_estimate=pl.CostEstimate(flops=cycles * 4096, bytes_accessed=1 << 20, transcendentals=0),
    )(*args)


def place_flags():
    wide, narrow = lax.axis_index("wide"), lax.axis_index("narrow")
    flags = [
        1 - wide % 2, wide == 0, wide == lax.axis_size("wide") - 1,
        1 - narrow % 2, narrow == 0, narrow == lax.axis_size("narrow") - 1,
    ]
    return jnp.stack([jnp.asarray(f).astype(jnp.int32) for f in flags])


def y_inside(place_ref, base, first_row, shape, rows):
    row = lax.broadcasted_iota(jnp.int32, shape, 0) + (first_row - base)
    inside = (row >= 0) | (place_ref[4] == 0)
    return inside & ((row < rows) | (place_ref[5] == 0))


def extend_kernel(
    place_ref, tile_ref, ra_ref, rb_ref, pa_ref, pb_ref, pc_ref, po_ref, ls_ref, step_ref,
    speed_ref, speed3_ref, phi_ref, ma_ref, mb_ref, one, two, keep, pull,
):
    depth, rows, lanes = tile_ref.shape
    layers = depth - 2 * HALO
    sp_ref, sm_ref, mid_ref = (step_ref.at[pl.ds(k * layers, layers)] for k in range(3))
    tall = ls_ref.shape[1]
    margin = 8
    base = margin + YE
    peak = jnp.maximum(jnp.maximum(pa_ref[...], pb_ref[...]), jnp.maximum(pc_ref[...], po_ref[...]))
    scale = 1.0 / (peak[0:1, 0:1] + 1e-06)

    def assemble(z, carry):
        one[z, base : base + rows, :] = tile_ref[z]
        return carry

    lax.fori_loop(0, depth, assemble, 0)

    def below(ref):
        for z in range(depth):
            one[z, base - 8 : base, :] = ref[z]
            one[z, base - 10 : base - 8, :] = ref[depth + z // 4, 2 * (z % 4) : 2 * (z % 4) + 2, :]

    def above(ref):
        for z in range(depth):
            one[z, base + rows : base + rows + 8, :] = ref[z]
            one[z, base + rows + 8 : base + rows + 10, :] = ref[depth + z // 4, 2 * (z % 4) : 2 * (z % 4) + 2, :]

    @pl.when(place_ref[3] == 1)
    def _():
        above(ra_ref)
        below(rb_ref)

    @pl.when(place_ref[3] == 0)
    def _():
        below(ra_ref)
        above(rb_ref)

    def inside(z, first_row):
        outside = ((z < HALO) & (place_ref[1] == 1)) | ((z >= depth - HALO) & (place_ref[2] == 1))
        return y_inside(place_ref, YE, first_row, (8, lanes), rows) & jnp.logical_not(outside)

    def normalise(z, carry):
        for t in range(-1, tall // 8):
            at = slice(margin + 8 * t, margin + 8 * t + 8)
            one[z, at, :] = jnp.where(inside(z, 8 * t), one[z, at, :] * scale - 0.5, 0.0)
        return carry

    def weigh(z, carry):
        for t in range(tall // 8):
            span = slice(8 * t, 8 * t + 8)
            ls = ls_ref[z - 1, span, :]
            weight = newton_reciprocal(1.0 + 4.0 * ls * ls)
            keep[z, span, :] = weight * one[z, margin + 8 * t : margin + 8 * t + 8, :]
            pull[z, span, :] = jnp.where(inside(z, 8 * t), (1.0 - weight) * (1.0 / 6.0), 0.0)
        return carry

    lax.fori_loop(0, depth, normalise, 0)
    lax.fori_loop(1, depth - 1, weigh, 0)
    rows_of = [-(-(YE + rows + YE - k) // 8) * 8 for k in range(EXT_PASSES)]
    for step in range(EXT_PASSES):
        source, target = (one, two) if step % 2 == 0 else (two, one)

        def extend(z, carry):
            count = rows_of[step] // 8
            tiles = [source[z, 8 * t : 8 * t + 8, :] for t in range(count + 2)]
            row = lax.broadcasted_iota(jnp.int32, tiles[0].shape, 0)
            lane = lax.broadcasted_iota(jnp.int32, tiles[0].shape, 1)
            down = [pltpu.roll(v, 1, 0) for v in tiles[:-1]]
            up = [pltpu.roll(v, 7, 0) for v in tiles[1:]]
            for t in range(count):
                at = margin + 8 * t
                centre = tiles[t + 1]
                total = source[z - 1, at : at + 8, :] + source[z + 1, at : at + 8, :]
                total = total + jnp.where(row == 0, down[t], down[t + 1])
                total = total + jnp.where(row == 7, up[t + 1], up[t])
                total = total + jnp.where(lane == 0, 0.0, pltpu.roll(centre, 1, 1))
                total = total + jnp.where(lane == lanes - 1, 0.0, pltpu.roll(centre, lanes - 1, 1))
                span = slice(8 * t, 8 * t + 8)
                target[z, at : at + 8, :] = keep[z, span, :] + pull[z, span, :] * total
            return carry

        lax.fori_loop(step + 1, depth - 1 - step, extend, 0)

    final = one if EXT_PASSES % 2 == 0 else two

    def march(z, carry):
        count = tall // 8
        tiles = [final[z + HALO, margin + 8 * t : margin + 8 * t + 8, :] for t in range(count)]
        moved = next_rows(tiles, YE - Y1, count - 1)
        for t in range(count - 1):
            span = slice(8 * t, 8 * t + 8)
            speed = moved[t]
            change = jnp.maximum(speed, 0.0) * sp_ref[z, span, :] + jnp.minimum(speed, 0.0) * sm_ref[z, span, :]
            phi = mid_ref[z, span, :] - change
            phi_ref[z, span, :] = jnp.where(y_inside(place_ref, Y1, 8 * t, phi.shape, rows), phi, 1.0)
        for t, value in enumerate(next_rows(tiles, YE - Y2, speed3_ref.shape[1] // 8)):
            speed3_ref[z, 8 * t : 8 * t + 8, :] = value
        for t, value in enumerate(next_rows(tiles[1:], YE - 8, rows // 8)):
            speed_ref[z, 8 * t : 8 * t + 8, :] = value
        return carry

    lax.fori_loop(0, layers, march, 0)
    send_edges(place_ref, phi_ref, Y1 - Y2, ma_ref, mb_ref)


def send_edges(place_ref, phi_ref, offset, ma_ref, mb_ref):
    layers = phi_ref.shape[0]
    count = ma_ref.shape[1]
    upper = place_ref[0] * (layers - 3)
    lower = (1 - place_ref[0]) * (layers - 3)
    for k in range(3):
        ma_ref[k] = phi_ref[upper + k, offset : offset + count, :]
        mb_ref[k] = phi_ref[lower + k, offset : offset + count, :]


def take_edges(place_ref, ra_ref, rb_ref, edges):
    upper = 3 * place_ref[0]
    lower = 3 - upper
    for k in range(3):
        edges[upper + k] = ra_ref[k]
        edges[lower + k] = rb_ref[k]

    @pl.when(place_ref[1] == 1)
    def _():
        edges[0:3] = jnp.ones((3,) + tuple(edges.shape[1:]), jnp.float32)

    @pl.when(place_ref[2] == 1)
    def _():
        edges[3:6] = jnp.ones((3,) + tuple(edges.shape[1:]), jnp.float32)


def plane_kernel(exact, phi_ref, gp_ref, gm_ref, mid_ref):
    xy_stage(phi_ref, 0, gp_ref.shape[0], gp_ref, gm_ref, mid_ref, exact)


def finish_kernel(
    rows, place_ref, phi_ref, ra_ref, rb_ref, gp_ref, gm_ref, speed_ref, *rest
):
    out_ref, edges = rest[0], rest[-1]
    layers, count, lanes = out_ref.shape
    base = Y2 if count > rows else 0
    take_edges(place_ref, ra_ref, rb_ref, edges)
    get_phi = functools.partial(layer_rows, phi_ref, edges)

    def finish(z, t, span, phi, gp, gm):
        where = pl.ds(8 * t, 8)
        speed = speed_ref[z, where, span]
        total = jnp.where(speed > 0.0, gp_ref[z, where, span] + gp, gm_ref[z, where, span] + gm)
        phi = phi - (TIME_STEP / 6.0) * speed * jnp.sqrt(total)
        if count > rows:
            phi = jnp.where(y_inside(place_ref, base, 8 * t, phi.shape, rows), phi, 1.0)
        out_ref[z, where, span] = phi

    z_stage(get_phi, layers, count, lanes, finish)
    if len(rest) > 2:
        send_edges(place_ref, out_ref, Y2, rest[1], rest[2])


def swaps(axis):
    count = lax.axis_size(axis)
    first, second = [], []
    for i in range(0, count, 2):
        first += [(i, i + 1), (i + 1, i)]
        if i + 2 < count:
            second += [(i + 1, i + 2), (i + 2, i + 1)]
    return first, second


def stack_kernel(place_ref, ls_ref, ra_ref, rb_ref, tall_ref, ma_ref, mb_ref, edges):
    layers, rows = ls_ref.shape[:2]
    take_edges(place_ref, ra_ref, rb_ref, edges)
    for k in range(3):
        tall_ref[k] = edges[k]
        tall_ref[layers + 3 + k] = edges[3 + k]

    def copy(z, carry):
        tall_ref[z + 3] = ls_ref[z]
        return carry

    lax.fori_loop(0, layers, copy, 0)
    depth = layers + 6

    def upper(ref):
        for z in range(depth):
            ref[z] = tall_ref[z, rows - 8 : rows, :]
            ref[depth + z // 8, z % 8 : z % 8 + 1, :] = tall_ref[z, rows - 9 : rows - 8, :]

    def lower(ref):
        for z in range(depth):
            ref[z] = tall_ref[z, 0:8, :]
            ref[depth + z // 8, z % 8 : z % 8 + 1, :] = tall_ref[z, 8:9, :]

    @pl.when(place_ref[3] == 1)
    def _():
        upper(ma_ref)
        lower(mb_ref)

    @pl.when(place_ref[3] == 0)
    def _():
        lower(ma_ref)
        upper(mb_ref)


def level_part(place, tile, ma, mb, wide_peak, level_set, ls, step):
    layers, rows, lanes = level_set.shape
    nfirst, nsecond = swaps("narrow")
    wfirst, wsecond = swaps("wide")
    count = lax.axis_size("narrow")
    across = [(i, (i + count // 2) % count) for i in range(count)]
    mirror = [(i, count - 1 - i) for i in range(count)]
    ra = lax.ppermute(ma, "narrow", nfirst)
    rb = lax.ppermute(mb, "narrow", nsecond)
    pc = lax.ppermute(wide_peak, "narrow", across)
    pb = lax.ppermute(wide_peak, "narrow", mirror)
    pa = ra[-1, :, :128]
    tall = ls.shape[1]
    rows1 = -(-(rows + 2 * Y1) // 8) * 8
    rows2 = -(-(rows + 2 * Y2) // 8) * 8
    depth = layers + 2 * HALO
    speed, speed3, phi, sa, sb = vmem_call(
        extend_kernel,
        [(layers, rows, lanes), (layers, rows2, lanes), (layers, rows1, lanes), (3, rows2, lanes), (3, rows2, lanes)],
        (place, tile, ra, rb, pa, pb, pc, wide_peak, ls, step),
        [(depth, tall + 16, lanes)] * 2 + [(depth, tall, lanes)] * 2,
        8000,
        16,
    )
    ga = lax.ppermute(sa, "wide", wfirst)
    gb = lax.ppermute(sb, "wide", wsecond)
    gp, gm, mid = vmem_call(functools.partial(plane_kernel, False), [(layers, rows2, lanes)] * 3, (phi,), (), 12000)
    phi, sa, sb = vmem_call(
        functools.partial(finish_kernel, rows),
        [(layers, rows2, lanes), (3, rows, lanes), (3, rows, lanes)],
        (place, mid, ga, gb, gp, gm, speed3),
        [(6, rows2, lanes)],
        5000,
    )
    ga = lax.ppermute(sa, "wide", wfirst)
    gb = lax.ppermute(sb, "wide", wsecond)
    gp, gm, mid = vmem_call(functools.partial(plane_kernel, True), [(layers, rows, lanes)] * 3, (phi,), (), 12000)
    (phi,) = vmem_call(
        functools.partial(finish_kernel, rows),
        [(layers, rows, lanes)],
        (place, mid, ga, gb, gp, gm, speed),
        [(6, rows, lanes)],
        5000,
    )
    return phi, speed


def first_gradient(place, tall, ra, rb):
    depth, rows, lanes = tall.shape
    rows1 = -(-(rows + 2 * Y1) // 8) * 8
    total = -(-(rows + 2 * YE) // 8) * 8
    return vmem_call(
        first_gradient_kernel, [(depth, total, lanes), (3 * (depth - 6), rows1, lanes)], (place, tall, ra, rb),
        [(6, rows1, lanes)], 35000
    )


def stack_level(place, level_set, ra, rb):
    layers, rows, lanes = level_set.shape
    depth = layers + 6
    edge = (depth + -(-depth // 8), 8, lanes)
    return vmem_call(
        stack_kernel, [(depth, rows, lanes), edge, edge], (place, level_set, ra, rb), [(6, rows, lanes)], 1500
    )


def unpack_kernel(place_ref, recv_ref, tile_ref, peak_ref, ma_ref, mb_ref):
    parts = recv_ref.shape[0]
    depth, rows, lanes = tile_ref.shape
    for j in range(depth // 4):
        block = recv_ref[:, 16 * j : 16 * j + 16, :].reshape(parts * 16, 128)
        wide = pltpu.roll(block.T, 1, 1)
        for k in range(4):
            tile_ref[4 * j + k] = wide[rows * k : rows * (k + 1), :]
    peak = recv_ref[0, 80:88, :]
    for s in range(1, parts):
        peak = jnp.maximum(peak, recv_ref[s, 80:88, :])
    peak_ref[...] = peak
    fill_edges(place_ref, tile_ref, peak, ma_ref, mb_ref)


def fill_edges(place_ref, tile_ref, peak, ma_ref, mb_ref):
    depth, rows, lanes = tile_ref.shape

    def upper(ref):
        for z in range(depth):
            ref[z] = tile_ref[z, rows - 8 : rows, :]
            ref[depth + z // 4, 2 * (z % 4) : 2 * (z % 4) + 2, :] = tile_ref[z, rows - 10 : rows - 8, :]

    def lower(ref):
        for z in range(depth):
            ref[z] = tile_ref[z, 0:8, :]
            ref[depth + z // 4, 2 * (z % 4) : 2 * (z % 4) + 2, :] = tile_ref[z, 8:10, :]

    last = ma_ref.shape[0] - 1
    ma_ref[last, :, 0:128] = peak
    mb_ref[last, :, 0:128] = peak

    @pl.when(place_ref[3] == 1)
    def _():
        upper(ma_ref)
        lower(mb_ref)

    @pl.when(place_ref[3] == 0)
    def _():
        lower(ma_ref)
        upper(mb_ref)


def unpack(place, recv, own_z, rows):
    parts = recv.shape[0]
    lanes = parts * 16
    depth = own_z + 2 * HALO
    edge = (depth + depth // 4 + 1, 8, lanes)
    return vmem_call(
        unpack_kernel, [(depth, rows, lanes), (8, 128), edge, edge], (place, recv), (), 1500
    )


def per_device(displacement, material, level_set):
    wide = lax.axis_size("wide")
    loads, comps, own_x, rows, size_z = displacement.shape
    own_z, _, size_x = level_set.shape
    place = place_flags()
    backward = [(i, (i - 1) % wide) for i in range(wide)]
    wfirst, wsecond = swaps("wide")
    nfirst, nsecond = swaps("narrow")

    low = lax.ppermute(displacement[:, :, :, -1], "narrow", ring("narrow", 1))
    high = lax.ppermute(
        jnp.stack([displacement[:, :, :, 0], displacement[:, :, :, 1]], axis=2), "narrow", ring("narrow", -1)
    )
    yh = jnp.concatenate([low[:, :, None], high], axis=2)
    bounds = level_set[:3], level_set[own_z - 3 :]
    even = place[0] == 1
    la = lax.ppermute(jnp.where(even, bounds[1], bounds[0]), "wide", wfirst)
    lb = lax.ppermute(jnp.where(even, bounds[0], bounds[1]), "wide", wsecond)

    stiff = 0.2 + 0.8 * jnp.repeat(material[0].astype(jnp.float32), BZ, axis=1)
    layers, yh, la, lb = lax.optimization_barrier((displacement[:, :, :3], yh, la, lb))
    flat = [layers.reshape(-1, size_z), stiff, yh[:, :, :, :3].reshape(-1, size_z)]
    flat.append(jnp.zeros((-sum(f.shape[0] for f in flat) % 8, size_z), jnp.float32))
    beyond = lax.ppermute(jnp.concatenate(flat, axis=0), "wide", backward)
    inner, tail = inner_strain(displacement, yh)
    la, lb, inner = lax.optimization_barrier((la, lb, inner))
    tall, ya, yb = stack_level(place, level_set, la, lb)
    ya = lax.ppermute(ya, "narrow", nfirst)
    yb = lax.ppermute(yb, "narrow", nsecond)
    beyond, ya, yb = lax.optimization_barrier((beyond, ya, yb))
    message = strain_message(place, tail, beyond, inner, material, wide)
    message, tall = lax.optimization_barrier((message, tall))
    recv = lax.all_to_all(message.reshape(wide, 88, 128), "wide", split_axis=0, concat_axis=0, tiled=True)
    ls, step = first_gradient(place, tall, ya, yb)
    recv, step = lax.optimization_barrier((recv, step))
    tile, wide_peak, ma, mb = unpack(place, recv, own_z, rows)
    return level_part(place, tile, ma, mb, wide_peak, level_set, ls, step)


def solution(mesh):
    return jax.shard_map(
        per_device,
        mesh=mesh,
        in_specs=(
            P(None, None, "wide", "narrow", None),
            P("wide", "narrow", None),
            P("wide", "narrow", None),
        ),
        out_specs=(P("wide", "narrow", None), P("wide", "narrow", None)),
        check_vma=False,
    )
```

```python
import functools
import jax
import jax.numpy as jnp
from jax import lax
from jax.experimental import pallas as pl
from jax.experimental.pallas import tpu as pltpu
from jax.sharding import PartitionSpec as P

BZ = 16
EXT_PASSES = 4
HJ_STEPS = 3
SHEAR = 0.384615
LAME = 0.576923
WENO_EPS = 1e-06
TIME_STEP = 0.3
HALO = EXT_PASSES
GRAD_SCALE = 1.0 / (8.0 * 48.0 * 48.0)
YE = 9
Y1 = 6
Y2 = 3


def lane_shifts(value):
    blocks = [value[:, 128 * b : 128 * (b + 1)] for b in range(value.shape[1] // 128)]
    lane = lax.broadcasted_iota(jnp.int32, blocks[0].shape, 1)
    zero = jnp.zeros_like(blocks[0])
    outs = []
    for step in (-1, 1, 2):
        turned = [pltpu.roll(b, (-step) % 128, 1) for b in blocks]
        if step < 0:
            mask = lane < 1
            parts = [jnp.where(mask, turned[i - 1] if i > 0 else zero, turned[i]) for i in range(len(blocks))]
        else:
            mask = lane >= 128 - step
            parts = [
                jnp.where(mask, turned[i + 1] if i + 1 < len(blocks) else zero, turned[i])
                for i in range(len(blocks))
            ]
        outs.append(jnp.concatenate(parts, axis=1))
    return outs


def val4(a, b, c, d):
    return (a + d) + 23.0 * (b + c)


def der4(a, b, c, d):
    return (d - a) + 5.0 * (c - b)


def filter_plane(filt, comp, layer, get_rows, tiles, low, high0, high1):
    tile_rows = [get_rows(t) for t in range(tiles)]
    row = lax.broadcasted_iota(jnp.int32, tile_rows[0].shape, 0)
    down = [pltpu.roll(v, 1, 0) for v in tile_rows]
    up = [pltpu.roll(v, 7, 0) for v in tile_rows]
    up2 = [pltpu.roll(v, 6, 0) for v in tile_rows]
    for t in range(tiles):
        b = tile_rows[t]
        a = jnp.where(row == 0, down[t - 1] if t else low, down[t])
        if t + 1 < tiles:
            c = jnp.where(row == 7, up[t + 1], up[t])
            d = jnp.where(row >= 6, up2[t + 1], up2[t])
        else:
            c = jnp.where(row == 7, high0, up[t])
            d = jnp.where(row == 6, high0, jnp.where(row == 7, high1, up2[t]))
        val_y = val4(a, b, c, d)
        der_y = der4(a, b, c, d)
        before, after, after2 = lane_shifts(val_y)
        span = pl.ds(8 * t, 8)
        filt[comp, 0, layer, span, :] = val4(before, val_y, after, after2)
        filt[comp, 2, layer, span, :] = der4(before, val_y, after, after2)
        before, after, after2 = lane_shifts(der_y)
        filt[comp, 1, layer, span, :] = val4(before, der_y, after, after2)


def densities(field, rows, finish):
    for tile in range(rows // 8):
        span = pl.ds(8 * tile, 8)
        gx = [der4(*field(comp, 0, span)) for comp in range(3)]
        gy = [val4(*field(comp, 1, span)) for comp in range(3)]
        gz = [val4(*field(comp, 2, span)) for comp in range(3)]
        sxy = gy[0] + gx[1]
        sxz = gz[0] + gx[2]
        syz = gz[1] + gy[2]
        trace = gx[0] + gy[1] + gz[2]
        square = gx[0] * gx[0] + gy[1] * gy[1] + gz[2] * gz[2]
        shear = sxy * sxy + sxz * sxz + syz * syz
        scale = GRAD_SCALE * GRAD_SCALE
        finish(span, (SHEAR * scale) * (square + 0.5 * shear) + (0.5 * LAME * scale) * (trace * trace))


def accumulate(ref, slot):
    load = pl.program_id(0)

    def finish(span, density):
        @pl.when(load == 0)
        def _():
            ref[slot, span, :] = density

        @pl.when(load > 0)
        def _():
            ref[slot, span, :] += density

    return finish


def inner_kernel(u_ref, yh_ref, energy_ref, tail_ref, filt):
    own_x, rows = u_ref.shape[2:4]

    def own_layer(layer, carry):
        for comp in range(3):
            edge = [yh_ref[0, comp, k, pl.ds(layer, 1), :] for k in range(3)]
            get_rows = lambda t: u_ref[0, comp, layer, 8 * t : 8 * t + 8, :]
            filter_plane(filt, comp, layer, get_rows, rows // 8, *edge)
        return carry

    lax.fori_loop(0, own_x, own_layer, 0)

    def slot_step(slot, carry):
        field = lambda comp, which, span: [filt[comp, which, slot + k, span, :] for k in range(4)]
        densities(field, rows, accumulate(energy_ref, slot))
        return carry

    lax.fori_loop(0, own_x - 3, slot_step, 0)
    for comp in range(3):
        for which in range(3):
            for k in range(3):
                tail_ref[0, comp, which, k] = filt[comp, which, own_x - 3 + k]


def outer_kernel(place_ref, tail_ref, part_ref, rest_ref, inner_ref, solid_ref, msg_ref, filt, energy, turned, next_ref):
    load = pl.program_id(0)
    own_x, rows, blocks = solid_ref.shape
    size_z = rest_ref.shape[1]
    loads = 3

    @pl.when(load == 0)
    def _():
        next_ref[0 : part_ref.shape[0], :] = part_ref[...]
        next_ref[part_ref.shape[0] :, :] = rest_ref[...]

    inner = own_x - 3
    tiles = rows // 8
    keep = jnp.where(place_ref[2] == 1, 0.0, 1.0)
    for comp in range(3):
        for k in range(3):
            layer = (load * 3 + comp) * 3 + k
            corner = loads * 9 * rows + rows
            edge = [next_ref[pl.ds(corner + (load * 3 + comp) * 9 + 3 * which + k, 1), :] for which in range(3)]
            get_rows = lambda t: next_ref[pl.ds(pl.multiple_of(layer * rows + 8 * t, 8), 8), :]
            filter_plane(filt, comp, k, get_rows, tiles, *edge)

    def density_at(slot, masked):
        def field(comp, which, span):
            out = []
            for k in range(4):
                at = slot + k
                value = tail_ref[0, comp, which, at, span, :] if at < 3 else filt[comp, which, at - 3, span, :]
                out.append(value * keep if masked[k] else value)
            return out

        densities(field, rows, accumulate(energy, slot))

    density_at(0, (False, False, False, True))
    density_at(1, (False, False, True, True))
    density_at(2, (True, False, False, False))

    @pl.when(load == pl.num_programs(0) - 1)
    def _():
        peak = jnp.zeros((8, 128), jnp.float32)
        groups = own_x // 4
        block_of = lax.broadcasted_iota(jnp.int32, (blocks, size_z), 1) // (size_z // blocks)
        spread = jnp.where(block_of == lax.broadcasted_iota(jnp.int32, (blocks, size_z), 0), 1.0, 0.0)
        for g in range(groups):
            stack = []
            for q in range(4):
                x = 4 * g + q
                if x < own_x - 1:
                    solid = jnp.dot(solid_ref[x + 1].astype(jnp.float32), spread, preferred_element_type=jnp.float32)
                    stiff = 0.2 + 0.8 * solid
                else:
                    stiff = next_ref[loads * 9 * rows : loads * 9 * rows + rows, :]
                value = (inner_ref[x] if x < inner else energy[x - inner]) * stiff
                stack.append(value)
                for tile in range(tiles):
                    for b in range(size_z // 128):
                        peak = jnp.maximum(peak, value[8 * tile : 8 * tile + 8, 128 * b : 128 * b + 128])
            turned[g, 0:8, :] = jnp.zeros((8, 128), jnp.float32)
            turned[g, size_z : size_z + 16, :] = jnp.zeros((16, 128), jnp.float32)
            turned[g, HALO : HALO + size_z, :] = jnp.concatenate(stack, axis=0).T
        peak = jnp.broadcast_to(jnp.max(peak, axis=0, keepdims=True), (8, 128))
        peak = jnp.broadcast_to(jnp.max(peak, axis=1, keepdims=True), (8, 128))
        parts = msg_ref.shape[0] // 88
        own_z = size_z // parts
        quads = (own_z + 2 * HALO) // 4
        lane = lax.broadcasted_iota(jnp.int32, (parts, 128), 1) // rows
        for g in range(groups):
            for j in range(quads):
                picked = [turned[g, pl.ds(4 * j + k, parts, stride=own_z), :] for k in range(4)]
                for q in range(4):
                    out = None
                    for k in range(4):
                        shift = (rows * (k - q)) % 128
                        part = pltpu.roll(picked[k], shift, 1) if shift else picked[k]
                        out = part if out is None else jnp.where(lane == k, part, out)
                    msg_ref[pl.ds(16 * j + 4 * g + q, parts, stride=88), :] = out
        for t in range(parts):
            msg_ref[pl.ds(88 * t + 80, 8), :] = peak


def load_block(*shape):
    return pl.BlockSpec((1,) + shape, lambda l: (l,) + (0,) * len(shape))


def fixed_block(*shape):
    return pl.BlockSpec(shape, lambda l: (0,) * len(shape))


def inner_strain(disp, yh):
    loads, comps, own_x, rows, size_z = disp.shape
    return pl.pallas_call(
        inner_kernel,
        grid=(loads,),
        out_shape=(
            jax.ShapeDtypeStruct((own_x - 3, rows, size_z), jnp.float32),
            jax.ShapeDtypeStruct((loads, comps, 3, 3, rows, size_z), jnp.float32),
        ),
        in_specs=[load_block(comps, own_x, rows, size_z), load_block(comps, 3, own_x, size_z)],
        out_specs=(fixed_block(own_x - 3, rows, size_z), load_block(comps, 3, 3, rows, size_z)),
        scratch_shapes=[
            pltpu.VMEM((3, 3, own_x, rows, size_z), jnp.float32),
        ],
        compiler_params=pltpu.CompilerParams(vmem_limit_bytes=48 << 20),
        cost_estimate=pl.CostEstimate(flops=40000 * 4096, bytes_accessed=1 << 20, transcendentals=0),
    )(disp, yh)


def strain_message(place, tail, part, beyond, inner, solid, parts):
    loads, comps = tail.shape[:2]
    own_x, rows, blocks = solid.shape
    size_z = beyond.shape[1]
    return pl.pallas_call(
        outer_kernel,
        grid=(loads,),
        out_shape=jax.ShapeDtypeStruct((parts * 88, 128), jnp.float32),
        in_specs=[
            pl.BlockSpec(memory_space=pltpu.SMEM),
            load_block(comps, 3, 3, rows, size_z),
            fixed_block(*part.shape),
            fixed_block(*beyond.shape),
            fixed_block(own_x - 3, rows, size_z),
            fixed_block(own_x, rows, blocks),
        ],
        out_specs=fixed_block(parts * 88, 128),
        scratch_shapes=[
            pltpu.VMEM((3, 3, 3, rows, size_z), jnp.float32),
            pltpu.VMEM((3, rows, size_z), jnp.float32),
            pltpu.VMEM((own_x // 4, size_z + 16, 128), jnp.float32),
            pltpu.VMEM((part.shape[0] + beyond.shape[0], size_z), jnp.float32),
        ],
        compiler_params=pltpu.CompilerParams(vmem_limit_bytes=48 << 20),
        cost_estimate=pl.CostEstimate(flops=10000 * 4096, bytes_accessed=1 << 20, transcendentals=0),
    )(place, tail, part, beyond, inner, solid)


def ring(axis, step):
    count = lax.axis_size(axis)
    return [(i, i + step) for i in range(count) if 0 <= i + step < count]


def newton_reciprocal(x):
    r = pl.reciprocal(x, approx=True)
    return r * (2.0 - x * r)


def weno_cell(d, e0, e1, e2, e3):
    f0 = e1 - e0
    f1 = e2 - e1
    f2 = e3 - e2
    g0 = f1 - f0
    g1 = f2 - f1
    twice1 = e1 + e1
    twice2 = e2 + e2
    third = 13.0 / 3.0
    eps = 4.0 * WENO_EPS
    pa = twice1 + f0
    pb = twice1 + f1
    pc = twice2 - f2
    a = (f0 * f0 * third + eps) + pa * pa
    b = (f1 * f1 * third + eps) + pb * pb
    c = (f2 * f2 * third + eps) + pc * pc
    a = a * a
    b = b * b * (1.0 / 6.0)
    c = c * c
    ac = a * c
    ab = a * b
    cb = c * b
    u = cb * g0
    v = ab * g1
    both = u + v
    both = both + both
    s = e1 + e2
    d6 = 6.0 * d
    minus = d6 + (s + e2) - (both + v) * newton_reciprocal(ac + cb + 3.0 * ab)
    plus = (s + e1) - d6 - (both + u) * newton_reciprocal(ac + ab + 3.0 * cb)
    return minus, plus


def godunov(minus, plus):
    high = jnp.maximum(jnp.maximum(minus, plus), 0.0)
    low = jnp.minimum(jnp.minimum(minus, plus), 0.0)
    return high * high, low * low


def x_terms(phi):
    rows, size = phi.shape
    wide = size + 128
    phi = jnp.concatenate([phi, jnp.ones((rows, 128), jnp.float32)], axis=1)
    d = pltpu.roll(phi, wide - 1, 1) - phi
    e = pltpu.roll(d, wide - 1, 1) - d
    minus, plus = weno_cell(
        d, pltpu.roll(e, 2, 1), pltpu.roll(e, 1, 1), e, pltpu.roll(e, wide - 1, 1)
    )
    return godunov(pltpu.roll(minus, 1, 1)[:, :size], plus[:, :size])


def next_rows(tiles, step, count):
    row = lax.broadcasted_iota(jnp.int32, tiles[0].shape, 0)
    turned = [pltpu.roll(v, 8 - step, 0) for v in tiles]
    last = len(tiles) - 1
    return [jnp.where(row < 8 - step, turned[t], turned[min(t + 1, last)]) for t in range(count)]


def y_stage(phi_ref, layer, span, gp_ref, gm_ref, mid_ref, z, exact):
    tiles = gp_ref.shape[1] // 8
    cells = tiles + 1 if exact else tiles
    count = min(cells + 1, phi_ref.shape[1] // 8)
    phi = [phi_ref[layer, 8 * t : 8 * t + 8, span] for t in range(count)]
    d = [n - p for n, p in zip(next_rows(phi, 1, count), phi)]
    e = [n - p for n, p in zip(next_rows(d, 1, count), d)]
    d2 = next_rows(d, 2, cells)
    e1, e2, e3 = (next_rows(e, k, cells) for k in (1, 2, 3))
    sides = [weno_cell(d2[t], e[t], e1[t], e2[t], e3[t]) for t in range(cells)]
    plus = next_rows([p for _, p in sides], 1, tiles)
    mid = next_rows(phi, 3, tiles)
    for t in range(tiles):
        rows = slice(8 * t, 8 * t + 8)
        gp_ref[z, rows, span], gm_ref[z, rows, span] = godunov(sides[t][0], plus[t])
        mid_ref[z, rows, span] = mid[t]


def xy_stage(phi_ref, layer0, layers, gp_ref, gm_ref, mid_ref, exact=False):
    _, rows, lanes = gp_ref.shape

    def layer_step(z, carry):
        for block in range(lanes // 128):
            y_stage(phi_ref, z + layer0, slice(128 * block, 128 * block + 128), gp_ref, gm_ref, mid_ref, z, exact)
        for t in range(rows // 8):
            xp, xm = x_terms(mid_ref[z, 8 * t : 8 * t + 8, :])
            gp_ref[z, 8 * t : 8 * t + 8, :] += xp
            gm_ref[z, 8 * t : 8 * t + 8, :] += xm
        return carry

    lax.fori_loop(0, layers, layer_step, 0)


def z_stage(get_phi, layers, rows, lanes, finish):
    def lane_step(block, carry):
        span = pl.ds(pl.multiple_of(128 * block, 128), 128)
        for t in range(rows // 8):
            p = [get_phi(z, t, span) for z in range(-3, layers + 3)]
            d = [p[k + 1] - p[k] for k in range(len(p) - 1)]
            e = [d[k + 1] - d[k] for k in range(len(d) - 1)]
            before = None
            for cell in range(layers + 1):
                minus, plus = weno_cell(d[cell + 2], e[cell], e[cell + 1], e[cell + 2], e[cell + 3])
                if before is not None:
                    finish(cell - 1, t, span, p[cell + 2], *godunov(before, plus))
                before = minus
        return carry

    lax.fori_loop(0, lanes // 128, lane_step, 0)


def layer_rows(mid_ref, edges, z, t, span):
    layers = mid_ref.shape[0]
    if z < 0:
        return edges[z + 3, 8 * t : 8 * t + 8, span]
    if z >= layers:
        return edges[z - layers + 3, 8 * t : 8 * t + 8, span]
    return mid_ref[z, 8 * t : 8 * t + 8, span]


def first_gradient_kernel(place_ref, tall_ref, ra_ref, rb_ref, ls_ref, step_ref, edges):
    layers = step_ref.shape[0] // 3
    sp_ref, sm_ref, mid_ref = (step_ref.at[pl.ds(k * layers, layers)] for k in range(3))
    _, rows, lanes = step_ref.shape
    depth, own, _ = tall_ref.shape
    ones = jnp.ones((8, lanes), jnp.float32)

    def copy(z, carry):
        for t in range(ls_ref.shape[1] // 8):
            ls_ref[z, 8 * t : 8 * t + 8, :] = ones
        ls_ref[z, YE : YE + own, :] = tall_ref[z]
        return carry

    lax.fori_loop(0, depth, copy, 0)

    def below(ref):
        @pl.when(place_ref[4] == 0)
        def _():
            for z in range(depth):
                ls_ref[z, YE - 8 : YE, :] = ref[z]
                ls_ref[z, YE - 9 : YE - 8, :] = ref[depth + z // 8, z % 8 : z % 8 + 1, :]

    def above(ref):
        @pl.when(place_ref[5] == 0)
        def _():
            for z in range(depth):
                ls_ref[z, YE + own : YE + own + 8, :] = ref[z]
                ls_ref[z, YE + own + 8 : YE + own + 9, :] = ref[depth + z // 8, z % 8 : z % 8 + 1, :]

    @pl.when(place_ref[3] == 1)
    def _():
        above(ra_ref)
        below(rb_ref)

    @pl.when(place_ref[3] == 0)
    def _():
        below(ra_ref)
        above(rb_ref)

    for k in range(6):
        layer = k if k < 3 else depth - 6 + k
        tiles = [ls_ref[layer, 8 * t : 8 * t + 8, :] for t in range(rows // 8 + 1)]
        for t, value in enumerate(next_rows(tiles, 3, rows // 8)):
            edges[k, 8 * t : 8 * t + 8, :] = value
    xy_stage(ls_ref, 3, layers, sp_ref, sm_ref, mid_ref)

    def finish(z, t, span, phi, gp, gm):
        where = pl.ds(8 * t, 8)
        scale = TIME_STEP / 6.0
        sp_ref[z, where, span] = scale * jnp.sqrt(sp_ref[z, where, span] + gp)
        sm_ref[z, where, span] = scale * jnp.sqrt(sm_ref[z, where, span] + gm)

    z_stage(
        lambda z, t, span: layer_rows(mid_ref, edges, z, t, span), layers, rows, lanes, finish
    )


def vmem_call(kernel, outs, args, scratch=(), cycles=0, limit=8, fetched=()):
    specs = []
    for k, arg in enumerate(args):
        space = pltpu.SMEM if arg.dtype == jnp.int32 else pltpu.HBM if k in fetched else pltpu.VMEM
        specs.append(pl.BlockSpec(memory_space=space))
    return pl.pallas_call(
        kernel,
        out_shape=tuple(jax.ShapeDtypeStruct(shape, jnp.float32) for shape in outs),
        in_specs=specs,
        out_specs=tuple(pl.BlockSpec(memory_space=pltpu.VMEM) for _ in outs),
        scratch_shapes=[pltpu.VMEM(shape, jnp.float32) for shape in scratch] + [pltpu.SemaphoreType.DMA] * len(fetched),
        compiler_params=pltpu.CompilerParams(vmem_limit_bytes=limit << 20),
        cost_estimate=pl.CostEstimate(flops=cycles * 4096, bytes_accessed=1 << 20, transcendentals=0),
    )(*args)


def place_flags():
    wide, narrow = lax.axis_index("wide"), lax.axis_index("narrow")
    flags = [
        1 - wide % 2, wide == 0, wide == lax.axis_size("wide") - 1,
        1 - narrow % 2, narrow == 0, narrow == lax.axis_size("narrow") - 1,
    ]
    return jnp.stack([jnp.asarray(f).astype(jnp.int32) for f in flags])


def y_inside(place_ref, base, first_row, shape, rows):
    row = lax.broadcasted_iota(jnp.int32, shape, 0) + (first_row - base)
    inside = (row >= 0) | (place_ref[4] == 0)
    return inside & ((row < rows) | (place_ref[5] == 0))


def extend_kernel(
    place_ref, tile_ref, ra_ref, rb_ref, pa_ref, pb_ref, pc_ref, po_ref, ls_ref, step_ref,
    speed_ref, speed3_ref, phi_ref, ma_ref, mb_ref, one, two, keep, pull, step_buf, sem,
):
    depth, rows, lanes = tile_ref.shape
    layers = depth - 2 * HALO
    fetch = pltpu.make_async_copy(step_ref, step_buf, sem)
    fetch.start()
    sp_ref, sm_ref, mid_ref = (step_buf.at[pl.ds(k * layers, layers)] for k in range(3))
    tall = ls_ref.shape[1]
    margin = 8
    base = margin + YE
    peak = jnp.maximum(jnp.maximum(pa_ref[...], pb_ref[...]), jnp.maximum(pc_ref[...], po_ref[...]))
    scale = 1.0 / (peak[0:1, 0:1] + 1e-06)

    def assemble(z, carry):
        one[z, base : base + rows, :] = tile_ref[z]
        return carry

    lax.fori_loop(0, depth, assemble, 0)

    def below(ref):
        for z in range(depth):
            one[z, base - 8 : base, :] = ref[z]
            one[z, base - 10 : base - 8, :] = ref[depth + z // 4, 2 * (z % 4) : 2 * (z % 4) + 2, :]

    def above(ref):
        for z in range(depth):
            one[z, base + rows : base + rows + 8, :] = ref[z]
            one[z, base + rows + 8 : base + rows + 10, :] = ref[depth + z // 4, 2 * (z % 4) : 2 * (z % 4) + 2, :]

    @pl.when(place_ref[3] == 1)
    def _():
        above(ra_ref)
        below(rb_ref)

    @pl.when(place_ref[3] == 0)
    def _():
        below(ra_ref)
        above(rb_ref)

    def inside(z, first_row):
        outside = ((z < HALO) & (place_ref[1] == 1)) | ((z >= depth - HALO) & (place_ref[2] == 1))
        return y_inside(place_ref, YE, first_row, (8, lanes), rows) & jnp.logical_not(outside)

    def normalise(z, carry):
        for t in range(-1, tall // 8):
            at = slice(margin + 8 * t, margin + 8 * t + 8)
            one[z, at, :] = jnp.where(inside(z, 8 * t), one[z, at, :] * scale - 0.5, 0.0)
        return carry

    def weigh(z, carry):
        for t in range(tall // 8):
            span = slice(8 * t, 8 * t + 8)
            ls = ls_ref[z - 1, span, :]
            weight = newton_reciprocal(1.0 + 4.0 * ls * ls)
            keep[z, span, :] = weight * one[z, margin + 8 * t : margin + 8 * t + 8, :]
            pull[z, span, :] = jnp.where(inside(z, 8 * t), (1.0 - weight) * (1.0 / 6.0), 0.0)
        return carry

    lax.fori_loop(0, depth, normalise, 0)
    lax.fori_loop(1, depth - 1, weigh, 0)
    rows_of = [-(-(YE + rows + YE - k) // 8) * 8 for k in range(EXT_PASSES)]
    for step in range(EXT_PASSES):
        source, target = (one, two) if step % 2 == 0 else (two, one)

        def extend(z, carry):
            count = rows_of[step] // 8
            tiles = [source[z, 8 * t : 8 * t + 8, :] for t in range(count + 2)]
            row = lax.broadcasted_iota(jnp.int32, tiles[0].shape, 0)
            lane = lax.broadcasted_iota(jnp.int32, tiles[0].shape, 1)
            down = [pltpu.roll(v, 1, 0) for v in tiles[:-1]]
            up = [pltpu.roll(v, 7, 0) for v in tiles[1:]]
            for t in range(count):
                at = margin + 8 * t
                centre = tiles[t + 1]
                total = source[z - 1, at : at + 8, :] + source[z + 1, at : at + 8, :]
                total = total + jnp.where(row == 0, down[t], down[t + 1])
                total = total + jnp.where(row == 7, up[t + 1], up[t])
                total = total + jnp.where(lane == 0, 0.0, pltpu.roll(centre, 1, 1))
                total = total + jnp.where(lane == lanes - 1, 0.0, pltpu.roll(centre, lanes - 1, 1))
                span = slice(8 * t, 8 * t + 8)
                target[z, at : at + 8, :] = keep[z, span, :] + pull[z, span, :] * total
            return carry

        lax.fori_loop(step + 1, depth - 1 - step, extend, 0)

    final = one if EXT_PASSES % 2 == 0 else two
    fetch.wait()

    def march(z, carry):
        count = tall // 8
        tiles = [final[z + HALO, margin + 8 * t : margin + 8 * t + 8, :] for t in range(count)]
        moved = next_rows(tiles, YE - Y1, count - 1)
        for t in range(count - 1):
            span = slice(8 * t, 8 * t + 8)
            speed = moved[t]
            change = jnp.maximum(speed, 0.0) * sp_ref[z, span, :] + jnp.minimum(speed, 0.0) * sm_ref[z, span, :]
            phi = mid_ref[z, span, :] - change
            phi_ref[z, span, :] = jnp.where(y_inside(place_ref, Y1, 8 * t, phi.shape, rows), phi, 1.0)
        for t, value in enumerate(next_rows(tiles, YE - Y2, speed3_ref.shape[1] // 8)):
            speed3_ref[z, 8 * t : 8 * t + 8, :] = value
        for t, value in enumerate(next_rows(tiles[1:], YE - 8, rows // 8)):
            speed_ref[z, 8 * t : 8 * t + 8, :] = value
        return carry

    lax.fori_loop(0, layers, march, 0)
    send_edges(place_ref, phi_ref, Y1 - Y2, ma_ref, mb_ref)


def send_edges(place_ref, phi_ref, offset, ma_ref, mb_ref):
    layers = phi_ref.shape[0]
    count = ma_ref.shape[1]
    upper = place_ref[0] * (layers - 3)
    lower = (1 - place_ref[0]) * (layers - 3)
    for k in range(3):
        ma_ref[k] = phi_ref[upper + k, offset : offset + count, :]
        mb_ref[k] = phi_ref[lower + k, offset : offset + count, :]


def take_edges(place_ref, ra_ref, rb_ref, edges):
    upper = 3 * place_ref[0]
    lower = 3 - upper
    for k in range(3):
        edges[upper + k] = ra_ref[k]
        edges[lower + k] = rb_ref[k]

    @pl.when(place_ref[1] == 1)
    def _():
        edges[0:3] = jnp.ones((3,) + tuple(edges.shape[1:]), jnp.float32)

    @pl.when(place_ref[2] == 1)
    def _():
        edges[3:6] = jnp.ones((3,) + tuple(edges.shape[1:]), jnp.float32)


def plane_kernel(exact, phi_ref, gp_ref, gm_ref, mid_ref):
    xy_stage(phi_ref, 0, gp_ref.shape[0], gp_ref, gm_ref, mid_ref, exact)


def finish_kernel(
    rows, place_ref, phi_ref, ra_ref, rb_ref, gp_ref, gm_ref, speed_ref, *rest
):
    out_ref, edges = rest[0], rest[-1]
    layers, count, lanes = out_ref.shape
    base = Y2 if count > rows else 0
    take_edges(place_ref, ra_ref, rb_ref, edges)
    get_phi = functools.partial(layer_rows, phi_ref, edges)

    def finish(z, t, span, phi, gp, gm):
        where = pl.ds(8 * t, 8)
        speed = speed_ref[z, where, span]
        total = jnp.where(speed > 0.0, gp_ref[z, where, span] + gp, gm_ref[z, where, span] + gm)
        phi = phi - (TIME_STEP / 6.0) * speed * jnp.sqrt(total)
        if count > rows:
            phi = jnp.where(y_inside(place_ref, base, 8 * t, phi.shape, rows), phi, 1.0)
        out_ref[z, where, span] = phi

    z_stage(get_phi, layers, count, lanes, finish)
    if len(rest) > 2:
        send_edges(place_ref, out_ref, Y2, rest[1], rest[2])


def swaps(axis):
    count = lax.axis_size(axis)
    first, second = [], []
    for i in range(0, count, 2):
        first += [(i, i + 1), (i + 1, i)]
        if i + 2 < count:
            second += [(i + 1, i + 2), (i + 2, i + 1)]
    return first, second


def stack_kernel(place_ref, ls_ref, ra_ref, rb_ref, tall_ref, ma_ref, mb_ref, edges):
    layers, rows = ls_ref.shape[:2]
    take_edges(place_ref, ra_ref, rb_ref, edges)
    for k in range(3):
        tall_ref[k] = edges[k]
        tall_ref[layers + 3 + k] = edges[3 + k]

    def copy(z, carry):
        tall_ref[z + 3] = ls_ref[z]
        return carry

    lax.fori_loop(0, layers, copy, 0)
    depth = layers + 6

    def upper(ref):
        for z in range(depth):
            ref[z] = tall_ref[z, rows - 8 : rows, :]
            ref[depth + z // 8, z % 8 : z % 8 + 1, :] = tall_ref[z, rows - 9 : rows - 8, :]

    def lower(ref):
        for z in range(depth):
            ref[z] = tall_ref[z, 0:8, :]
            ref[depth + z // 8, z % 8 : z % 8 + 1, :] = tall_ref[z, 8:9, :]

    @pl.when(place_ref[3] == 1)
    def _():
        upper(ma_ref)
        lower(mb_ref)

    @pl.when(place_ref[3] == 0)
    def _():
        lower(ma_ref)
        upper(mb_ref)


def level_part(place, tile, ma, mb, wide_peak, level_set, ls, step):
    layers, rows, lanes = level_set.shape
    nfirst, nsecond = swaps("narrow")
    wfirst, wsecond = swaps("wide")
    count = lax.axis_size("narrow")
    across = [(i, (i + count // 2) % count) for i in range(count)]
    mirror = [(i, count - 1 - i) for i in range(count)]
    ra = lax.ppermute(ma, "narrow", nfirst)
    rb = lax.ppermute(mb, "narrow", nsecond)
    pc = lax.ppermute(wide_peak, "narrow", across)
    pb = lax.ppermute(wide_peak, "narrow", mirror)
    pa = ra[-1, :, :128]
    tall = ls.shape[1]
    rows1 = -(-(rows + 2 * Y1) // 8) * 8
    rows2 = -(-(rows + 2 * Y2) // 8) * 8
    depth = layers + 2 * HALO
    speed, speed3, phi, sa, sb = vmem_call(
        extend_kernel,
        [(layers, rows, lanes), (layers, rows2, lanes), (layers, rows1, lanes), (3, rows2, lanes), (3, rows2, lanes)],
        (place, tile, ra, rb, pa, pb, pc, wide_peak, ls, step),
        [(depth, tall + 16, lanes)] * 2 + [(depth, tall, lanes)] * 2 + [step.shape],
        8000,
        20,
        (9,),
    )
    ga = lax.ppermute(sa, "wide", wfirst)
    gb = lax.ppermute(sb, "wide", wsecond)
    gp, gm, mid = vmem_call(functools.partial(plane_kernel, False), [(layers, rows2, lanes)] * 3, (phi,), (), 12000)
    phi, sa, sb = vmem_call(
        functools.partial(finish_kernel, rows),
        [(layers, rows2, lanes), (3, rows, lanes), (3, rows, lanes)],
        (place, mid, ga, gb, gp, gm, speed3),
        [(6, rows2, lanes)],
        5000,
    )
    ga = lax.ppermute(sa, "wide", wfirst)
    gb = lax.ppermute(sb, "wide", wsecond)
    gp, gm, mid = vmem_call(functools.partial(plane_kernel, True), [(layers, rows, lanes)] * 3, (phi,), (), 12000)
    (phi,) = vmem_call(
        functools.partial(finish_kernel, rows),
        [(layers, rows, lanes)],
        (place, mid, ga, gb, gp, gm, speed),
        [(6, rows, lanes)],
        5000,
    )
    return phi, speed


def first_gradient(place, tall, ra, rb):
    depth, rows, lanes = tall.shape
    rows1 = -(-(rows + 2 * Y1) // 8) * 8
    total = -(-(rows + 2 * YE) // 8) * 8
    return vmem_call(
        first_gradient_kernel, [(depth, total, lanes), (3 * (depth - 6), rows1, lanes)], (place, tall, ra, rb),
        [(6, rows1, lanes)], 35000
    )


def stack_level(place, level_set, ra, rb):
    layers, rows, lanes = level_set.shape
    depth = layers + 6
    edge = (depth + -(-depth // 8), 8, lanes)
    return vmem_call(
        stack_kernel, [(depth, rows, lanes), edge, edge], (place, level_set, ra, rb), [(6, rows, lanes)], 1500
    )


def unpack_kernel(place_ref, recv_ref, tile_ref, peak_ref, ma_ref, mb_ref):
    parts = recv_ref.shape[0]
    depth, rows, lanes = tile_ref.shape
    for j in range(depth // 4):
        block = recv_ref[:, 16 * j : 16 * j + 16, :].reshape(parts * 16, 128)
        wide = pltpu.roll(block.T, 1, 1)
        for k in range(4):
            tile_ref[4 * j + k] = wide[rows * k : rows * (k + 1), :]
    peak = recv_ref[0, 80:88, :]
    for s in range(1, parts):
        peak = jnp.maximum(peak, recv_ref[s, 80:88, :])
    peak_ref[...] = peak
    fill_edges(place_ref, tile_ref, peak, ma_ref, mb_ref)


def fill_edges(place_ref, tile_ref, peak, ma_ref, mb_ref):
    depth, rows, lanes = tile_ref.shape

    def upper(ref):
        for z in range(depth):
            ref[z] = tile_ref[z, rows - 8 : rows, :]
            ref[depth + z // 4, 2 * (z % 4) : 2 * (z % 4) + 2, :] = tile_ref[z, rows - 10 : rows - 8, :]

    def lower(ref):
        for z in range(depth):
            ref[z] = tile_ref[z, 0:8, :]
            ref[depth + z // 4, 2 * (z % 4) : 2 * (z % 4) + 2, :] = tile_ref[z, 8:10, :]

    last = ma_ref.shape[0] - 1
    ma_ref[last, :, 0:128] = peak
    mb_ref[last, :, 0:128] = peak

    @pl.when(place_ref[3] == 1)
    def _():
        upper(ma_ref)
        lower(mb_ref)

    @pl.when(place_ref[3] == 0)
    def _():
        lower(ma_ref)
        upper(mb_ref)


def unpack(place, recv, own_z, rows):
    parts = recv.shape[0]
    lanes = parts * 16
    depth = own_z + 2 * HALO
    edge = (depth + depth // 4 + 1, 8, lanes)
    return vmem_call(
        unpack_kernel, [(depth, rows, lanes), (8, 128), edge, edge], (place, recv), (), 1500
    )


def per_device(displacement, material, level_set):
    wide = lax.axis_size("wide")
    loads, comps, own_x, rows, size_z = displacement.shape
    own_z, _, size_x = level_set.shape
    place = place_flags()
    backward = [(i, (i - 1) % wide) for i in range(wide)]
    wfirst, wsecond = swaps("wide")
    nfirst, nsecond = swaps("narrow")

    part = lax.ppermute(displacement[0, :, :3].reshape(-1, size_z), "wide", backward)
    low = lax.ppermute(displacement[:, :, :, -1], "narrow", ring("narrow", 1))
    high = lax.ppermute(
        jnp.stack([displacement[:, :, :, 0], displacement[:, :, :, 1]], axis=2), "narrow", ring("narrow", -1)
    )
    yh = jnp.concatenate([low[:, :, None], high], axis=2)
    bounds = level_set[:3], level_set[own_z - 3 :]
    even = place[0] == 1
    la = lax.ppermute(jnp.where(even, bounds[1], bounds[0]), "wide", wfirst)
    lb = lax.ppermute(jnp.where(even, bounds[0], bounds[1]), "wide", wsecond)

    stiff = 0.2 + 0.8 * jnp.repeat(material[0].astype(jnp.float32), BZ, axis=1)
    layers, yh, la, lb, part = lax.optimization_barrier((displacement[1:, :, :3], yh, la, lb, part))
    flat = [layers.reshape(-1, size_z), stiff, yh[:, :, :, :3].reshape(-1, size_z)]
    flat.append(jnp.zeros((-sum(f.shape[0] for f in flat) % 8, size_z), jnp.float32))
    beyond = lax.ppermute(jnp.concatenate(flat, axis=0), "wide", backward)
    inner, tail = inner_strain(displacement, yh)
    la, lb, inner = lax.optimization_barrier((la, lb, inner))
    tall, ya, yb = stack_level(place, level_set, la, lb)
    ya = lax.ppermute(ya, "narrow", nfirst)
    yb = lax.ppermute(yb, "narrow", nsecond)
    beyond, ya, yb = lax.optimization_barrier((beyond, ya, yb))
    message = strain_message(place, tail, part, beyond, inner, material, wide)
    message, tall = lax.optimization_barrier((message, tall))
    recv = lax.all_to_all(message.reshape(wide, 88, 128), "wide", split_axis=0, concat_axis=0, tiled=True)
    ls, step = first_gradient(place, tall, ya, yb)
    recv, step = lax.optimization_barrier((recv, step))
    tile, wide_peak, ma, mb = unpack(place, recv, own_z, rows)
    return level_part(place, tile, ma, mb, wide_peak, level_set, ls, step)


def solution(mesh):
    return jax.shard_map(
        per_device,
        mesh=mesh,
        in_specs=(
            P(None, None, "wide", "narrow", None),
            P("wide", "narrow", None),
            P("wide", "narrow", None),
        ),
        out_specs=(P("wide", "narrow", None), P("wide", "narrow", None)),
        check_vma=False,
    )
```

```python
import functools
import jax
import jax.numpy as jnp
from jax import lax
from jax.experimental import pallas as pl
from jax.experimental.pallas import tpu as pltpu
from jax.sharding import PartitionSpec as P

BZ = 16
EXT_PASSES = 4
HJ_STEPS = 3
SHEAR = 0.384615
LAME = 0.576923
WENO_EPS = 1e-06
TIME_STEP = 0.3
HALO = EXT_PASSES
GRAD_SCALE = 1.0 / (8.0 * 48.0 * 48.0)
YE = 9
Y1 = 6
Y2 = 3


def lane_shifts(value):
    blocks = [value[:, 128 * b : 128 * (b + 1)] for b in range(value.shape[1] // 128)]
    lane = lax.broadcasted_iota(jnp.int32, blocks[0].shape, 1)
    zero = jnp.zeros_like(blocks[0])
    outs = []
    for step in (-1, 1, 2):
        turned = [pltpu.roll(b, (-step) % 128, 1) for b in blocks]
        if step < 0:
            mask = lane < 1
            parts = [jnp.where(mask, turned[i - 1] if i > 0 else zero, turned[i]) for i in range(len(blocks))]
        else:
            mask = lane >= 128 - step
            parts = [
                jnp.where(mask, turned[i + 1] if i + 1 < len(blocks) else zero, turned[i])
                for i in range(len(blocks))
            ]
        outs.append(jnp.concatenate(parts, axis=1))
    return outs


def val4(a, b, c, d):
    return (a + d) + 23.0 * (b + c)


def der4(a, b, c, d):
    return (d - a) + 5.0 * (c - b)


def filter_plane(filt, comp, layer, get_rows, tiles, low, high0, high1):
    tile_rows = [get_rows(t) for t in range(tiles)]
    row = lax.broadcasted_iota(jnp.int32, tile_rows[0].shape, 0)
    down = [pltpu.roll(v, 1, 0) for v in tile_rows]
    up = [pltpu.roll(v, 7, 0) for v in tile_rows]
    up2 = [pltpu.roll(v, 6, 0) for v in tile_rows]
    for t in range(tiles):
        b = tile_rows[t]
        a = jnp.where(row == 0, down[t - 1] if t else low, down[t])
        if t + 1 < tiles:
            c = jnp.where(row == 7, up[t + 1], up[t])
            d = jnp.where(row >= 6, up2[t + 1], up2[t])
        else:
            c = jnp.where(row == 7, high0, up[t])
            d = jnp.where(row == 6, high0, jnp.where(row == 7, high1, up2[t]))
        val_y = val4(a, b, c, d)
        der_y = der4(a, b, c, d)
        before, after, after2 = lane_shifts(val_y)
        span = pl.ds(8 * t, 8)
        filt[comp, 0, layer, span, :] = val4(before, val_y, after, after2)
        filt[comp, 2, layer, span, :] = der4(before, val_y, after, after2)
        before, after, after2 = lane_shifts(der_y)
        filt[comp, 1, layer, span, :] = val4(before, der_y, after, after2)


def densities(field, rows, finish):
    for tile in range(rows // 8):
        span = pl.ds(8 * tile, 8)
        gx = [der4(*field(comp, 0, span)) for comp in range(3)]
        gy = [val4(*field(comp, 1, span)) for comp in range(3)]
        gz = [val4(*field(comp, 2, span)) for comp in range(3)]
        sxy = gy[0] + gx[1]
        sxz = gz[0] + gx[2]
        syz = gz[1] + gy[2]
        trace = gx[0] + gy[1] + gz[2]
        square = gx[0] * gx[0] + gy[1] * gy[1] + gz[2] * gz[2]
        shear = sxy * sxy + sxz * sxz + syz * syz
        scale = GRAD_SCALE * GRAD_SCALE
        finish(span, (SHEAR * scale) * (square + 0.5 * shear) + (0.5 * LAME * scale) * (trace * trace))


def accumulate(ref, slot):
    load = pl.program_id(0)

    def finish(span, density):
        @pl.when(load == 0)
        def _():
            ref[slot, span, :] = density

        @pl.when(load > 0)
        def _():
            ref[slot, span, :] += density

    return finish


def inner_kernel(u_ref, yh_ref, energy_ref, tail_ref, filt):
    own_x, rows = u_ref.shape[2:4]

    def own_layer(layer, carry):
        for comp in range(3):
            edge = [yh_ref[0, comp, k, pl.ds(layer, 1), :] for k in range(3)]
            get_rows = lambda t: u_ref[0, comp, layer, 8 * t : 8 * t + 8, :]
            filter_plane(filt, comp, layer, get_rows, rows // 8, *edge)
        return carry

    lax.fori_loop(0, own_x, own_layer, 0)

    def slot_step(slot, carry):
        field = lambda comp, which, span: [filt[comp, which, slot + k, span, :] for k in range(4)]
        densities(field, rows, accumulate(energy_ref, slot))
        return carry

    lax.fori_loop(0, own_x - 3, slot_step, 0)
    for comp in range(3):
        for which in range(3):
            for k in range(3):
                tail_ref[0, comp, which, k] = filt[comp, which, own_x - 3 + k]


def outer_kernel(place_ref, tail_ref, next_ref, inner_ref, solid_ref, msg_ref, filt, energy, turned):
    load = pl.program_id(0)
    own_x, rows, blocks = solid_ref.shape
    size_z = next_ref.shape[1]
    loads = 3
    inner = own_x - 3
    tiles = rows // 8
    keep = jnp.where(place_ref[2] == 1, 0.0, 1.0)
    for comp in range(3):
        for k in range(3):
            layer = (load * 3 + comp) * 3 + k
            corner = loads * 9 * rows + rows
            edge = [next_ref[pl.ds(corner + (load * 3 + comp) * 9 + 3 * which + k, 1), :] for which in range(3)]
            get_rows = lambda t: next_ref[pl.ds(pl.multiple_of(layer * rows + 8 * t, 8), 8), :]
            filter_plane(filt, comp, k, get_rows, tiles, *edge)

    def density_at(slot, masked):
        def field(comp, which, span):
            out = []
            for k in range(4):
                at = slot + k
                value = tail_ref[0, comp, which, at, span, :] if at < 3 else filt[comp, which, at - 3, span, :]
                out.append(value * keep if masked[k] else value)
            return out

        densities(field, rows, accumulate(energy, slot))

    density_at(0, (False, False, False, True))
    density_at(1, (False, False, True, True))
    density_at(2, (True, False, False, False))

    @pl.when(load == pl.num_programs(0) - 1)
    def _():
        peak = jnp.zeros((8, 128), jnp.float32)
        groups = own_x // 4
        block_of = lax.broadcasted_iota(jnp.int32, (blocks, size_z), 1) // (size_z // blocks)
        spread = jnp.where(block_of == lax.broadcasted_iota(jnp.int32, (blocks, size_z), 0), 1.0, 0.0)
        for g in range(groups):
            stack = []
            for q in range(4):
                x = 4 * g + q
                if x < own_x - 1:
                    solid = jnp.dot(solid_ref[x + 1].astype(jnp.float32), spread, preferred_element_type=jnp.float32)
                    stiff = 0.2 + 0.8 * solid
                else:
                    stiff = next_ref[loads * 9 * rows : loads * 9 * rows + rows, :]
                value = (inner_ref[x] if x < inner else energy[x - inner]) * stiff
                stack.append(value)
                for tile in range(tiles):
                    for b in range(size_z // 128):
                        peak = jnp.maximum(peak, value[8 * tile : 8 * tile + 8, 128 * b : 128 * b + 128])
            turned[g, 0:8, :] = jnp.zeros((8, 128), jnp.float32)
            turned[g, size_z : size_z + 16, :] = jnp.zeros((16, 128), jnp.float32)
            turned[g, HALO : HALO + size_z, :] = jnp.concatenate(stack, axis=0).T
        peak = jnp.broadcast_to(jnp.max(peak, axis=0, keepdims=True), (8, 128))
        peak = jnp.broadcast_to(jnp.max(peak, axis=1, keepdims=True), (8, 128))
        parts = msg_ref.shape[0] // 88
        own_z = size_z // parts
        quads = (own_z + 2 * HALO) // 4
        lane = lax.broadcasted_iota(jnp.int32, (parts, 128), 1) // rows
        for g in range(groups):
            for j in range(quads):
                picked = [turned[g, pl.ds(4 * j + k, parts, stride=own_z), :] for k in range(4)]
                for q in range(4):
                    out = None
                    for k in range(4):
                        shift = (rows * (k - q)) % 128
                        part = pltpu.roll(picked[k], shift, 1) if shift else picked[k]
                        out = part if out is None else jnp.where(lane == k, part, out)
                    msg_ref[pl.ds(16 * j + 4 * g + q, parts, stride=88), :] = out
        for t in range(parts):
            msg_ref[pl.ds(88 * t + 80, 8), :] = peak


def load_block(*shape):
    return pl.BlockSpec((1,) + shape, lambda l: (l,) + (0,) * len(shape))


def fixed_block(*shape):
    return pl.BlockSpec(shape, lambda l: (0,) * len(shape))


def inner_strain(disp, yh):
    loads, comps, own_x, rows, size_z = disp.shape
    return pl.pallas_call(
        inner_kernel,
        grid=(loads,),
        out_shape=(
            jax.ShapeDtypeStruct((own_x - 3, rows, size_z), jnp.float32),
            jax.ShapeDtypeStruct((loads, comps, 3, 3, rows, size_z), jnp.float32),
        ),
        in_specs=[load_block(comps, own_x, rows, size_z), load_block(comps, 3, own_x, size_z)],
        out_specs=(fixed_block(own_x - 3, rows, size_z), load_block(comps, 3, 3, rows, size_z)),
        scratch_shapes=[
            pltpu.VMEM((3, 3, own_x, rows, size_z), jnp.float32),
        ],
        compiler_params=pltpu.CompilerParams(vmem_limit_bytes=54 << 20),
        cost_estimate=pl.CostEstimate(flops=40000 * 4096, bytes_accessed=1 << 20, transcendentals=0),
    )(disp, yh)


def strain_message(place, tail, beyond, inner, solid, parts):
    loads, comps = tail.shape[:2]
    own_x, rows, blocks = solid.shape
    size_z = beyond.shape[1]
    return pl.pallas_call(
        outer_kernel,
        grid=(loads,),
        out_shape=jax.ShapeDtypeStruct((parts * 88, 128), jnp.float32),
        in_specs=[
            pl.BlockSpec(memory_space=pltpu.SMEM),
            load_block(comps, 3, 3, rows, size_z),
            fixed_block(*beyond.shape),
            fixed_block(own_x - 3, rows, size_z),
            fixed_block(own_x, rows, blocks),
        ],
        out_specs=fixed_block(parts * 88, 128),
        scratch_shapes=[
            pltpu.VMEM((3, 3, 3, rows, size_z), jnp.float32),
            pltpu.VMEM((3, rows, size_z), jnp.float32),
            pltpu.VMEM((own_x // 4, size_z + 16, 128), jnp.float32),
        ],
        compiler_params=pltpu.CompilerParams(vmem_limit_bytes=48 << 20),
        cost_estimate=pl.CostEstimate(flops=10000 * 4096, bytes_accessed=1 << 20, transcendentals=0),
    )(place, tail, beyond, inner, solid)


def ring(axis, step):
    count = lax.axis_size(axis)
    return [(i, i + step) for i in range(count) if 0 <= i + step < count]


def newton_reciprocal(x):
    r = pl.reciprocal(x, approx=True)
    return r * (2.0 - x * r)


def weno_cell(d, e0, e1, e2, e3):
    f0 = e1 - e0
    f1 = e2 - e1
    f2 = e3 - e2
    g0 = f1 - f0
    g1 = f2 - f1
    twice1 = e1 + e1
    twice2 = e2 + e2
    third = 13.0 / 3.0
    eps = 4.0 * WENO_EPS
    pa = twice1 + f0
    pb = twice1 + f1
    pc = twice2 - f2
    a = (f0 * f0 * third + eps) + pa * pa
    b = (f1 * f1 * third + eps) + pb * pb
    c = (f2 * f2 * third + eps) + pc * pc
    a = a * a
    b = b * b * (1.0 / 6.0)
    c = c * c
    ac = a * c
    ab = a * b
    cb = c * b
    u = cb * g0
    v = ab * g1
    both = u + v
    both = both + both
    s = e1 + e2
    d6 = 6.0 * d
    minus = d6 + (s + e2) - (both + v) * newton_reciprocal(ac + cb + 3.0 * ab)
    plus = (s + e1) - d6 - (both + u) * newton_reciprocal(ac + ab + 3.0 * cb)
    return minus, plus


def godunov(minus, plus):
    high = jnp.maximum(jnp.maximum(minus, plus), 0.0)
    low = jnp.minimum(jnp.minimum(minus, plus), 0.0)
    return high * high, low * low


def x_terms(phi):
    rows, size = phi.shape
    wide = size + 128
    phi = jnp.concatenate([phi, jnp.ones((rows, 128), jnp.float32)], axis=1)
    d = pltpu.roll(phi, wide - 1, 1) - phi
    e = pltpu.roll(d, wide - 1, 1) - d
    minus, plus = weno_cell(
        d, pltpu.roll(e, 2, 1), pltpu.roll(e, 1, 1), e, pltpu.roll(e, wide - 1, 1)
    )
    return godunov(pltpu.roll(minus, 1, 1)[:, :size], plus[:, :size])


def next_rows(tiles, step, count):
    row = lax.broadcasted_iota(jnp.int32, tiles[0].shape, 0)
    turned = [pltpu.roll(v, 8 - step, 0) for v in tiles]
    last = len(tiles) - 1
    return [jnp.where(row < 8 - step, turned[t], turned[min(t + 1, last)]) for t in range(count)]


def y_stage(phi_ref, layer, span, gp_ref, gm_ref, mid_ref, z, exact):
    tiles = gp_ref.shape[1] // 8
    cells = tiles + 1 if exact else tiles
    count = min(cells + 1, phi_ref.shape[1] // 8)
    phi = [phi_ref[layer, 8 * t : 8 * t + 8, span] for t in range(count)]
    d = [n - p for n, p in zip(next_rows(phi, 1, count), phi)]
    e = [n - p for n, p in zip(next_rows(d, 1, count), d)]
    d2 = next_rows(d, 2, cells)
    e1, e2, e3 = (next_rows(e, k, cells) for k in (1, 2, 3))
    sides = [weno_cell(d2[t], e[t], e1[t], e2[t], e3[t]) for t in range(cells)]
    plus = next_rows([p for _, p in sides], 1, tiles)
    mid = next_rows(phi, 3, tiles)
    for t in range(tiles):
        rows = slice(8 * t, 8 * t + 8)
        gp_ref[z, rows, span], gm_ref[z, rows, span] = godunov(sides[t][0], plus[t])
        mid_ref[z, rows, span] = mid[t]


def xy_stage(phi_ref, layer0, layers, gp_ref, gm_ref, mid_ref, exact=False):
    _, rows, lanes = gp_ref.shape

    def layer_step(z, carry):
        for block in range(lanes // 128):
            y_stage(phi_ref, z + layer0, slice(128 * block, 128 * block + 128), gp_ref, gm_ref, mid_ref, z, exact)
        for t in range(rows // 8):
            xp, xm = x_terms(mid_ref[z, 8 * t : 8 * t + 8, :])
            gp_ref[z, 8 * t : 8 * t + 8, :] += xp
            gm_ref[z, 8 * t : 8 * t + 8, :] += xm
        return carry

    lax.fori_loop(0, layers, layer_step, 0)


def z_stage(get_phi, layers, rows, lanes, finish):
    def lane_step(block, carry):
        span = pl.ds(pl.multiple_of(128 * block, 128), 128)
        for t in range(rows // 8):
            p = [get_phi(z, t, span) for z in range(-3, layers + 3)]
            d = [p[k + 1] - p[k] for k in range(len(p) - 1)]
            e = [d[k + 1] - d[k] for k in range(len(d) - 1)]
            before = None
            for cell in range(layers + 1):
                minus, plus = weno_cell(d[cell + 2], e[cell], e[cell + 1], e[cell + 2], e[cell + 3])
                if before is not None:
                    finish(cell - 1, t, span, p[cell + 2], *godunov(before, plus))
                before = minus
        return carry

    lax.fori_loop(0, lanes // 128, lane_step, 0)


def layer_rows(mid_ref, edges, z, t, span):
    layers = mid_ref.shape[0]
    if z < 0:
        return edges[z + 3, 8 * t : 8 * t + 8, span]
    if z >= layers:
        return edges[z - layers + 3, 8 * t : 8 * t + 8, span]
    return mid_ref[z, 8 * t : 8 * t + 8, span]


def first_gradient_kernel(place_ref, tall_ref, ra_ref, rb_ref, ls_ref, step_ref, edges):
    layers = step_ref.shape[0] // 3
    sp_ref, sm_ref, mid_ref = (step_ref.at[pl.ds(k * layers, layers)] for k in range(3))
    _, rows, lanes = step_ref.shape
    depth, own, _ = tall_ref.shape
    ones = jnp.ones((8, lanes), jnp.float32)

    def copy(z, carry):
        for t in range(ls_ref.shape[1] // 8):
            ls_ref[z, 8 * t : 8 * t + 8, :] = ones
        ls_ref[z, YE : YE + own, :] = tall_ref[z]
        return carry

    lax.fori_loop(0, depth, copy, 0)

    def below(ref):
        @pl.when(place_ref[4] == 0)
        def _():
            for z in range(depth):
                ls_ref[z, YE - 8 : YE, :] = ref[z]
                ls_ref[z, YE - 9 : YE - 8, :] = ref[depth + z // 8, z % 8 : z % 8 + 1, :]

    def above(ref):
        @pl.when(place_ref[5] == 0)
        def _():
            for z in range(depth):
                ls_ref[z, YE + own : YE + own + 8, :] = ref[z]
                ls_ref[z, YE + own + 8 : YE + own + 9, :] = ref[depth + z // 8, z % 8 : z % 8 + 1, :]

    @pl.when(place_ref[3] == 1)
    def _():
        above(ra_ref)
        below(rb_ref)

    @pl.when(place_ref[3] == 0)
    def _():
        below(ra_ref)
        above(rb_ref)

    for k in range(6):
        layer = k if k < 3 else depth - 6 + k
        tiles = [ls_ref[layer, 8 * t : 8 * t + 8, :] for t in range(rows // 8 + 1)]
        for t, value in enumerate(next_rows(tiles, 3, rows // 8)):
            edges[k, 8 * t : 8 * t + 8, :] = value
    xy_stage(ls_ref, 3, layers, sp_ref, sm_ref, mid_ref)

    def finish(z, t, span, phi, gp, gm):
        where = pl.ds(8 * t, 8)
        scale = TIME_STEP / 6.0
        sp_ref[z, where, span] = scale * jnp.sqrt(sp_ref[z, where, span] + gp)
        sm_ref[z, where, span] = scale * jnp.sqrt(sm_ref[z, where, span] + gm)

    z_stage(
        lambda z, t, span: layer_rows(mid_ref, edges, z, t, span), layers, rows, lanes, finish
    )


def vmem_call(kernel, outs, args, scratch=(), cycles=0, limit=8):
    specs = []
    for arg in args:
        space = pltpu.SMEM if arg.dtype == jnp.int32 else pltpu.VMEM
        specs.append(pl.BlockSpec(memory_space=space))
    return pl.pallas_call(
        kernel,
        out_shape=tuple(jax.ShapeDtypeStruct(shape, jnp.float32) for shape in outs),
        in_specs=specs,
        out_specs=tuple(pl.BlockSpec(memory_space=pltpu.VMEM) for _ in outs),
        scratch_shapes=[pltpu.VMEM(shape, jnp.float32) for shape in scratch],
        compiler_params=pltpu.CompilerParams(vmem_limit_bytes=limit << 20),
        cost_estimate=pl.CostEstimate(flops=cycles * 4096, bytes_accessed=1 << 20, transcendentals=0),
    )(*args)


def place_flags():
    wide, narrow = lax.axis_index("wide"), lax.axis_index("narrow")
    flags = [
        1 - wide % 2, wide == 0, wide == lax.axis_size("wide") - 1,
        1 - narrow % 2, narrow == 0, narrow == lax.axis_size("narrow") - 1,
    ]
    return jnp.stack([jnp.asarray(f).astype(jnp.int32) for f in flags])


def y_inside(place_ref, base, first_row, shape, rows):
    row = lax.broadcasted_iota(jnp.int32, shape, 0) + (first_row - base)
    inside = (row >= 0) | (place_ref[4] == 0)
    return inside & ((row < rows) | (place_ref[5] == 0))


def extend_kernel(
    place_ref, tile_ref, ra_ref, rb_ref, pa_ref, pb_ref, pc_ref, po_ref, ls_ref, step_ref,
    speed_ref, speed3_ref, phi_ref, ma_ref, mb_ref, one, two, keep, pull,
):
    depth, rows, lanes = tile_ref.shape
    layers = depth - 2 * HALO
    sp_ref, sm_ref, mid_ref = (step_ref.at[pl.ds(k * layers, layers)] for k in range(3))
    tall = ls_ref.shape[1]
    margin = 8
    base = margin + YE
    peak = jnp.maximum(jnp.maximum(pa_ref[...], pb_ref[...]), jnp.maximum(pc_ref[...], po_ref[...]))
    scale = 1.0 / (peak[0:1, 0:1] + 1e-06)

    def assemble(z, carry):
        one[z, base : base + rows, :] = tile_ref[z]
        return carry

    lax.fori_loop(0, depth, assemble, 0)

    def below(ref):
        for z in range(depth):
            one[z, base - 8 : base, :] = ref[z]
            one[z, base - 10 : base - 8, :] = ref[depth + z // 4, 2 * (z % 4) : 2 * (z % 4) + 2, :]

    def above(ref):
        for z in range(depth):
            one[z, base + rows : base + rows + 8, :] = ref[z]
            one[z, base + rows + 8 : base + rows + 10, :] = ref[depth + z // 4, 2 * (z % 4) : 2 * (z % 4) + 2, :]

    @pl.when(place_ref[3] == 1)
    def _():
        above(ra_ref)
        below(rb_ref)

    @pl.when(place_ref[3] == 0)
    def _():
        below(ra_ref)
        above(rb_ref)

    def inside(z, first_row):
        outside = ((z < HALO) & (place_ref[1] == 1)) | ((z >= depth - HALO) & (place_ref[2] == 1))
        return y_inside(place_ref, YE, first_row, (8, lanes), rows) & jnp.logical_not(outside)

    def normalise(z, carry):
        for t in range(-1, tall // 8):
            at = slice(margin + 8 * t, margin + 8 * t + 8)
            one[z, at, :] = jnp.where(inside(z, 8 * t), one[z, at, :] * scale - 0.5, 0.0)
        return carry

    def weigh(z, carry):
        for t in range(tall // 8):
            span = slice(8 * t, 8 * t + 8)
            ls = ls_ref[z - 1, span, :]
            weight = newton_reciprocal(1.0 + 4.0 * ls * ls)
            keep[z, span, :] = weight * one[z, margin + 8 * t : margin + 8 * t + 8, :]
            pull[z, span, :] = jnp.where(inside(z, 8 * t), (1.0 - weight) * (1.0 / 6.0), 0.0)
        return carry

    lax.fori_loop(0, depth, normalise, 0)
    lax.fori_loop(1, depth - 1, weigh, 0)
    rows_of = [-(-(YE + rows + YE - k) // 8) * 8 for k in range(EXT_PASSES)]
    for step in range(EXT_PASSES):
        source, target = (one, two) if step % 2 == 0 else (two, one)

        def extend(z, carry):
            count = rows_of[step] // 8
            tiles = [source[z, 8 * t : 8 * t + 8, :] for t in range(count + 2)]
            row = lax.broadcasted_iota(jnp.int32, tiles[0].shape, 0)
            lane = lax.broadcasted_iota(jnp.int32, tiles[0].shape, 1)
            down = [pltpu.roll(v, 1, 0) for v in tiles[:-1]]
            up = [pltpu.roll(v, 7, 0) for v in tiles[1:]]
            for t in range(count):
                at = margin + 8 * t
                centre = tiles[t + 1]
                total = source[z - 1, at : at + 8, :] + source[z + 1, at : at + 8, :]
                total = total + jnp.where(row == 0, down[t], down[t + 1])
                total = total + jnp.where(row == 7, up[t + 1], up[t])
                total = total + jnp.where(lane == 0, 0.0, pltpu.roll(centre, 1, 1))
                total = total + jnp.where(lane == lanes - 1, 0.0, pltpu.roll(centre, lanes - 1, 1))
                span = slice(8 * t, 8 * t + 8)
                target[z, at : at + 8, :] = keep[z, span, :] + pull[z, span, :] * total
            return carry

        lax.fori_loop(step + 1, depth - 1 - step, extend, 0)

    final = one if EXT_PASSES % 2 == 0 else two

    def march(z, carry):
        count = tall // 8
        tiles = [final[z + HALO, margin + 8 * t : margin + 8 * t + 8, :] for t in range(count)]
        moved = next_rows(tiles, YE - Y1, count - 1)
        for t in range(count - 1):
            span = slice(8 * t, 8 * t + 8)
            speed = moved[t]
            change = jnp.maximum(speed, 0.0) * sp_ref[z, span, :] + jnp.minimum(speed, 0.0) * sm_ref[z, span, :]
            phi = mid_ref[z, span, :] - change
            phi_ref[z, span, :] = jnp.where(y_inside(place_ref, Y1, 8 * t, phi.shape, rows), phi, 1.0)
        for t, value in enumerate(next_rows(tiles, YE - Y2, speed3_ref.shape[1] // 8)):
            speed3_ref[z, 8 * t : 8 * t + 8, :] = value
        for t, value in enumerate(next_rows(tiles[1:], YE - 8, rows // 8)):
            speed_ref[z, 8 * t : 8 * t + 8, :] = value
        return carry

    lax.fori_loop(0, layers, march, 0)
    send_edges(place_ref, phi_ref, Y1 - Y2, ma_ref, mb_ref)


def send_edges(place_ref, phi_ref, offset, ma_ref, mb_ref):
    layers = phi_ref.shape[0]
    count = ma_ref.shape[1]
    upper = place_ref[0] * (layers - 3)
    lower = (1 - place_ref[0]) * (layers - 3)
    for k in range(3):
        ma_ref[k] = phi_ref[upper + k, offset : offset + count, :]
        mb_ref[k] = phi_ref[lower + k, offset : offset + count, :]


def take_edges(place_ref, ra_ref, rb_ref, edges):
    upper = 3 * place_ref[0]
    lower = 3 - upper
    for k in range(3):
        edges[upper + k] = ra_ref[k]
        edges[lower + k] = rb_ref[k]

    @pl.when(place_ref[1] == 1)
    def _():
        edges[0:3] = jnp.ones((3,) + tuple(edges.shape[1:]), jnp.float32)

    @pl.when(place_ref[2] == 1)
    def _():
        edges[3:6] = jnp.ones((3,) + tuple(edges.shape[1:]), jnp.float32)


def plane_kernel(exact, phi_ref, gp_ref, gm_ref, mid_ref):
    xy_stage(phi_ref, 0, gp_ref.shape[0], gp_ref, gm_ref, mid_ref, exact)


def finish_kernel(
    rows, place_ref, phi_ref, ra_ref, rb_ref, gp_ref, gm_ref, speed_ref, *rest
):
    out_ref, edges = rest[0], rest[-1]
    layers, count, lanes = out_ref.shape
    base = Y2 if count > rows else 0
    take_edges(place_ref, ra_ref, rb_ref, edges)
    get_phi = functools.partial(layer_rows, phi_ref, edges)

    def finish(z, t, span, phi, gp, gm):
        where = pl.ds(8 * t, 8)
        speed = speed_ref[z, where, span]
        total = jnp.where(speed > 0.0, gp_ref[z, where, span] + gp, gm_ref[z, where, span] + gm)
        phi = phi - (TIME_STEP / 6.0) * speed * jnp.sqrt(total)
        if count > rows:
            phi = jnp.where(y_inside(place_ref, base, 8 * t, phi.shape, rows), phi, 1.0)
        out_ref[z, where, span] = phi

    z_stage(get_phi, layers, count, lanes, finish)
    if len(rest) > 2:
        send_edges(place_ref, out_ref, Y2, rest[1], rest[2])


def swaps(axis):
    count = lax.axis_size(axis)
    first, second = [], []
    for i in range(0, count, 2):
        first += [(i, i + 1), (i + 1, i)]
        if i + 2 < count:
            second += [(i + 1, i + 2), (i + 2, i + 1)]
    return first, second


def stack_kernel(place_ref, ls_ref, ra_ref, rb_ref, tall_ref, ma_ref, mb_ref, edges):
    layers, rows = ls_ref.shape[:2]
    take_edges(place_ref, ra_ref, rb_ref, edges)
    for k in range(3):
        tall_ref[k] = edges[k]
        tall_ref[layers + 3 + k] = edges[3 + k]

    def copy(z, carry):
        tall_ref[z + 3] = ls_ref[z]
        return carry

    lax.fori_loop(0, layers, copy, 0)
    depth = layers + 6

    def upper(ref):
        for z in range(depth):
            ref[z] = tall_ref[z, rows - 8 : rows, :]
            ref[depth + z // 8, z % 8 : z % 8 + 1, :] = tall_ref[z, rows - 9 : rows - 8, :]

    def lower(ref):
        for z in range(depth):
            ref[z] = tall_ref[z, 0:8, :]
            ref[depth + z // 8, z % 8 : z % 8 + 1, :] = tall_ref[z, 8:9, :]

    @pl.when(place_ref[3] == 1)
    def _():
        upper(ma_ref)
        lower(mb_ref)

    @pl.when(place_ref[3] == 0)
    def _():
        lower(ma_ref)
        upper(mb_ref)


def level_part(place, tile, ma, mb, wide_peak, level_set, ls, step):
    layers, rows, lanes = level_set.shape
    nfirst, nsecond = swaps("narrow")
    wfirst, wsecond = swaps("wide")
    count = lax.axis_size("narrow")
    across = [(i, (i + count // 2) % count) for i in range(count)]
    mirror = [(i, count - 1 - i) for i in range(count)]
    ra = lax.ppermute(ma, "narrow", nfirst)
    rb = lax.ppermute(mb, "narrow", nsecond)
    pc = lax.ppermute(wide_peak, "narrow", across)
    pb = lax.ppermute(wide_peak, "narrow", mirror)
    pa = ra[-1, :, :128]
    tall = ls.shape[1]
    rows1 = -(-(rows + 2 * Y1) // 8) * 8
    rows2 = -(-(rows + 2 * Y2) // 8) * 8
    depth = layers + 2 * HALO
    speed, speed3, phi, sa, sb = vmem_call(
        extend_kernel,
        [(layers, rows, lanes), (layers, rows2, lanes), (layers, rows1, lanes), (3, rows2, lanes), (3, rows2, lanes)],
        (place, tile, ra, rb, pa, pb, pc, wide_peak, ls, step),
        [(depth, tall + 16, lanes)] * 2 + [(depth, tall, lanes)] * 2,
        8000,
        16,
    )
    ga = lax.ppermute(sa, "wide", wfirst)
    gb = lax.ppermute(sb, "wide", wsecond)
    gp, gm, mid = vmem_call(functools.partial(plane_kernel, False), [(layers, rows2, lanes)] * 3, (phi,), (), 12000)
    phi, sa, sb = vmem_call(
        functools.partial(finish_kernel, rows),
        [(layers, rows2, lanes), (3, rows, lanes), (3, rows, lanes)],
        (place, mid, ga, gb, gp, gm, speed3),
        [(6, rows2, lanes)],
        5000,
    )
    ga = lax.ppermute(sa, "wide", wfirst)
    gb = lax.ppermute(sb, "wide", wsecond)
    gp, gm, mid = vmem_call(functools.partial(plane_kernel, True), [(layers, rows, lanes)] * 3, (phi,), (), 12000)
    (phi,) = vmem_call(
        functools.partial(finish_kernel, rows),
        [(layers, rows, lanes)],
        (place, mid, ga, gb, gp, gm, speed),
        [(6, rows, lanes)],
        5000,
    )
    return phi, speed


def first_gradient(place, tall, ra, rb):
    depth, rows, lanes = tall.shape
    rows1 = -(-(rows + 2 * Y1) // 8) * 8
    total = -(-(rows + 2 * YE) // 8) * 8
    return vmem_call(
        first_gradient_kernel, [(depth, total, lanes), (3 * (depth - 6), rows1, lanes)], (place, tall, ra, rb),
        [(6, rows1, lanes)], 35000
    )


def stack_level(place, level_set, ra, rb):
    layers, rows, lanes = level_set.shape
    depth = layers + 6
    edge = (depth + -(-depth // 8), 8, lanes)
    return vmem_call(
        stack_kernel, [(depth, rows, lanes), edge, edge], (place, level_set, ra, rb), [(6, rows, lanes)], 1500
    )


def unpack_kernel(place_ref, recv_ref, tile_ref, peak_ref, ma_ref, mb_ref):
    parts = recv_ref.shape[0]
    depth, rows, lanes = tile_ref.shape
    for j in range(depth // 4):
        block = recv_ref[:, 16 * j : 16 * j + 16, :].reshape(parts * 16, 128)
        wide = pltpu.roll(block.T, 1, 1)
        for k in range(4):
            tile_ref[4 * j + k] = wide[rows * k : rows * (k + 1), :]
    peak = recv_ref[0, 80:88, :]
    for s in range(1, parts):
        peak = jnp.maximum(peak, recv_ref[s, 80:88, :])
    peak_ref[...] = peak
    fill_edges(place_ref, tile_ref, peak, ma_ref, mb_ref)


def fill_edges(place_ref, tile_ref, peak, ma_ref, mb_ref):
    depth, rows, lanes = tile_ref.shape

    def upper(ref):
        for z in range(depth):
            ref[z] = tile_ref[z, rows - 8 : rows, :]
            ref[depth + z // 4, 2 * (z % 4) : 2 * (z % 4) + 2, :] = tile_ref[z, rows - 10 : rows - 8, :]

    def lower(ref):
        for z in range(depth):
            ref[z] = tile_ref[z, 0:8, :]
            ref[depth + z // 4, 2 * (z % 4) : 2 * (z % 4) + 2, :] = tile_ref[z, 8:10, :]

    last = ma_ref.shape[0] - 1
    ma_ref[last, :, 0:128] = peak
    mb_ref[last, :, 0:128] = peak

    @pl.when(place_ref[3] == 1)
    def _():
        upper(ma_ref)
        lower(mb_ref)

    @pl.when(place_ref[3] == 0)
    def _():
        lower(ma_ref)
        upper(mb_ref)


def unpack(place, recv, own_z, rows):
    parts = recv.shape[0]
    lanes = parts * 16
    depth = own_z + 2 * HALO
    edge = (depth + depth // 4 + 1, 8, lanes)
    return vmem_call(
        unpack_kernel, [(depth, rows, lanes), (8, 128), edge, edge], (place, recv), (), 1500
    )


def per_device(displacement, material, level_set):
    wide = lax.axis_size("wide")
    loads, comps, own_x, rows, size_z = displacement.shape
    own_z, _, size_x = level_set.shape
    place = place_flags()
    backward = [(i, (i - 1) % wide) for i in range(wide)]
    wfirst, wsecond = swaps("wide")
    nfirst, nsecond = swaps("narrow")

    low = lax.ppermute(displacement[:, :, :, -1], "narrow", ring("narrow", 1))
    high = lax.ppermute(
        jnp.stack([displacement[:, :, :, 0], displacement[:, :, :, 1]], axis=2), "narrow", ring("narrow", -1)
    )
    yh = jnp.concatenate([low[:, :, None], high], axis=2)
    bounds = level_set[:3], level_set[own_z - 3 :]
    even = place[0] == 1
    la = lax.ppermute(jnp.where(even, bounds[1], bounds[0]), "wide", wfirst)
    lb = lax.ppermute(jnp.where(even, bounds[0], bounds[1]), "wide", wsecond)

    stiff = 0.2 + 0.8 * jnp.repeat(material[0].astype(jnp.float32), BZ, axis=1)
    layers, yh, la, lb = lax.optimization_barrier((displacement[:, :, :3], yh, la, lb))
    flat = [layers.reshape(-1, size_z), stiff, yh[:, :, :, :3].reshape(-1, size_z)]
    flat.append(jnp.zeros((-sum(f.shape[0] for f in flat) % 8, size_z), jnp.float32))
    beyond = lax.ppermute(jnp.concatenate(flat, axis=0), "wide", backward)
    inner, tail = inner_strain(displacement, yh)
    la, lb, inner = lax.optimization_barrier((la, lb, inner))
    tall, ya, yb = stack_level(place, level_set, la, lb)
    ya = lax.ppermute(ya, "narrow", nfirst)
    yb = lax.ppermute(yb, "narrow", nsecond)
    beyond, ya, yb = lax.optimization_barrier((beyond, ya, yb))
    message = strain_message(place, tail, beyond, inner, material, wide)
    message, tall = lax.optimization_barrier((message, tall))
    recv = lax.all_to_all(message.reshape(wide, 88, 128), "wide", split_axis=0, concat_axis=0, tiled=True)
    ls, step = first_gradient(place, tall, ya, yb)
    recv, step = lax.optimization_barrier((recv, step))
    tile, wide_peak, ma, mb = unpack(place, recv, own_z, rows)
    return level_part(place, tile, ma, mb, wide_peak, level_set, ls, step)


def solution(mesh):
    return jax.shard_map(
        per_device,
        mesh=mesh,
        in_specs=(
            P(None, None, "wide", "narrow", None),
            P("wide", "narrow", None),
            P("wide", "narrow", None),
        ),
        out_specs=(P("wide", "narrow", None), P("wide", "narrow", None)),
        check_vma=False,
    )
```

```python
import functools
import jax
import jax.numpy as jnp
from jax import lax
from jax.experimental import pallas as pl
from jax.experimental.pallas import tpu as pltpu
from jax.sharding import PartitionSpec as P

BZ = 16
EXT_PASSES = 4
HJ_STEPS = 3
SHEAR = 0.384615
LAME = 0.576923
WENO_EPS = 1e-06
TIME_STEP = 0.3
HALO = EXT_PASSES
GRAD_SCALE = 1.0 / (8.0 * 48.0 * 48.0)
YE = 9
Y1 = 6
Y2 = 3


def lane_shifts(value):
    blocks = [value[:, 128 * b : 128 * (b + 1)] for b in range(value.shape[1] // 128)]
    lane = lax.broadcasted_iota(jnp.int32, blocks[0].shape, 1)
    zero = jnp.zeros_like(blocks[0])
    outs = []
    for step in (-1, 1, 2):
        turned = [pltpu.roll(b, (-step) % 128, 1) for b in blocks]
        if step < 0:
            mask = lane < 1
            parts = [jnp.where(mask, turned[i - 1] if i > 0 else zero, turned[i]) for i in range(len(blocks))]
        else:
            mask = lane >= 128 - step
            parts = [
                jnp.where(mask, turned[i + 1] if i + 1 < len(blocks) else zero, turned[i])
                for i in range(len(blocks))
            ]
        outs.append(jnp.concatenate(parts, axis=1))
    return outs


def val4(a, b, c, d):
    return (a + d) + 23.0 * (b + c)


def der4(a, b, c, d):
    return (d - a) + 5.0 * (c - b)


def filter_plane(filt, comp, layer, get_rows, tiles, low, high0, high1):
    tile_rows = [get_rows(t) for t in range(tiles)]
    row = lax.broadcasted_iota(jnp.int32, tile_rows[0].shape, 0)
    down = [pltpu.roll(v, 1, 0) for v in tile_rows]
    up = [pltpu.roll(v, 7, 0) for v in tile_rows]
    up2 = [pltpu.roll(v, 6, 0) for v in tile_rows]
    for t in range(tiles):
        b = tile_rows[t]
        a = jnp.where(row == 0, down[t - 1] if t else low, down[t])
        if t + 1 < tiles:
            c = jnp.where(row == 7, up[t + 1], up[t])
            d = jnp.where(row >= 6, up2[t + 1], up2[t])
        else:
            c = jnp.where(row == 7, high0, up[t])
            d = jnp.where(row == 6, high0, jnp.where(row == 7, high1, up2[t]))
        val_y = val4(a, b, c, d)
        der_y = der4(a, b, c, d)
        before, after, after2 = lane_shifts(val_y)
        span = pl.ds(8 * t, 8)
        filt[comp, 0, layer, span, :] = val4(before, val_y, after, after2)
        filt[comp, 2, layer, span, :] = der4(before, val_y, after, after2)
        before, after, after2 = lane_shifts(der_y)
        filt[comp, 1, layer, span, :] = val4(before, der_y, after, after2)


def densities(field, rows, finish):
    for tile in range(rows // 8):
        span = pl.ds(8 * tile, 8)
        gx = [der4(*field(comp, 0, span)) for comp in range(3)]
        gy = [val4(*field(comp, 1, span)) for comp in range(3)]
        gz = [val4(*field(comp, 2, span)) for comp in range(3)]
        sxy = gy[0] + gx[1]
        sxz = gz[0] + gx[2]
        syz = gz[1] + gy[2]
        trace = gx[0] + gy[1] + gz[2]
        square = gx[0] * gx[0] + gy[1] * gy[1] + gz[2] * gz[2]
        shear = sxy * sxy + sxz * sxz + syz * syz
        scale = GRAD_SCALE * GRAD_SCALE
        finish(span, (SHEAR * scale) * (square + 0.5 * shear) + (0.5 * LAME * scale) * (trace * trace))


def accumulate(ref, slot):
    load = pl.program_id(0)

    def finish(span, density):
        @pl.when(load == 0)
        def _():
            ref[slot, span, :] = density

        @pl.when(load > 0)
        def _():
            ref[slot, span, :] += density

    return finish


def inner_kernel(u_ref, yh_ref, energy_ref, tail_ref, filt):
    own_x, rows = u_ref.shape[2:4]

    def own_layer(layer, carry):
        for comp in range(3):
            edge = [yh_ref[0, comp, k, pl.ds(layer, 1), :] for k in range(3)]
            get_rows = lambda t: u_ref[0, comp, layer, 8 * t : 8 * t + 8, :]
            filter_plane(filt, comp, layer, get_rows, rows // 8, *edge)
        return carry

    lax.fori_loop(0, own_x, own_layer, 0)

    def slot_step(slot, carry):
        field = lambda comp, which, span: [filt[comp, which, slot + k, span, :] for k in range(4)]
        densities(field, rows, accumulate(energy_ref, slot))
        return carry

    lax.fori_loop(0, own_x - 3, slot_step, 0)
    for comp in range(3):
        for which in range(3):
            for k in range(3):
                tail_ref[0, comp, which, k] = filt[comp, which, own_x - 3 + k]


def outer_kernel(place_ref, tail_ref, next_ref, inner_ref, solid_ref, msg_ref, filt, energy, turned):
    load = pl.program_id(0)
    own_x, rows, blocks = solid_ref.shape
    size_z = next_ref.shape[1]
    loads = 3
    inner = own_x - 3
    tiles = rows // 8
    keep = jnp.where(place_ref[2] == 1, 0.0, 1.0)
    for comp in range(3):
        for k in range(3):
            layer = (load * 3 + comp) * 3 + k
            corner = loads * 9 * rows + rows
            edge = [next_ref[pl.ds(corner + (load * 3 + comp) * 9 + 3 * which + k, 1), :] for which in range(3)]
            get_rows = lambda t: next_ref[pl.ds(pl.multiple_of(layer * rows + 8 * t, 8), 8), :]
            filter_plane(filt, comp, k, get_rows, tiles, *edge)

    def density_at(slot, masked):
        def field(comp, which, span):
            out = []
            for k in range(4):
                at = slot + k
                value = tail_ref[0, comp, which, at, span, :] if at < 3 else filt[comp, which, at - 3, span, :]
                out.append(value * keep if masked[k] else value)
            return out

        densities(field, rows, accumulate(energy, slot))

    density_at(0, (False, False, False, True))
    density_at(1, (False, False, True, True))
    density_at(2, (True, False, False, False))

    @pl.when(load == pl.num_programs(0) - 1)
    def _():
        peak = jnp.zeros((8, 128), jnp.float32)
        groups = own_x // 4
        block_of = lax.broadcasted_iota(jnp.int32, (blocks, size_z), 1) // (size_z // blocks)
        spread = jnp.where(block_of == lax.broadcasted_iota(jnp.int32, (blocks, size_z), 0), 1.0, 0.0)
        for g in range(groups):
            stack = []
            for q in range(4):
                x = 4 * g + q
                if x < own_x - 1:
                    solid = jnp.dot(solid_ref[x + 1].astype(jnp.float32), spread, preferred_element_type=jnp.float32)
                    stiff = 0.2 + 0.8 * solid
                else:
                    stiff = next_ref[loads * 9 * rows : loads * 9 * rows + rows, :]
                value = (inner_ref[x] if x < inner else energy[x - inner]) * stiff
                stack.append(value)
                for tile in range(tiles):
                    for b in range(size_z // 128):
                        peak = jnp.maximum(peak, value[8 * tile : 8 * tile + 8, 128 * b : 128 * b + 128])
            turned[g, 0:8, :] = jnp.zeros((8, 128), jnp.float32)
            turned[g, size_z : size_z + 16, :] = jnp.zeros((16, 128), jnp.float32)
            turned[g, HALO : HALO + size_z, :] = jnp.concatenate(stack, axis=0).T
        peak = jnp.broadcast_to(jnp.max(peak, axis=0, keepdims=True), (8, 128))
        peak = jnp.broadcast_to(jnp.max(peak, axis=1, keepdims=True), (8, 128))
        parts = msg_ref.shape[0] // 88
        own_z = size_z // parts
        quads = (own_z + 2 * HALO) // 4
        lane = lax.broadcasted_iota(jnp.int32, (parts, 128), 1) // rows
        for g in range(groups):
            for j in range(quads):
                picked = [turned[g, pl.ds(4 * j + k, parts, stride=own_z), :] for k in range(4)]
                for q in range(4):
                    out = None
                    for k in range(4):
                        shift = (rows * (k - q)) % 128
                        part = pltpu.roll(picked[k], shift, 1) if shift else picked[k]
                        out = part if out is None else jnp.where(lane == k, part, out)
                    msg_ref[pl.ds(16 * j + 4 * g + q, parts, stride=88), :] = out
        for t in range(parts):
            msg_ref[pl.ds(88 * t + 80, 8), :] = peak


def load_block(*shape):
    return pl.BlockSpec((1,) + shape, lambda l: (l,) + (0,) * len(shape))


def fixed_block(*shape):
    return pl.BlockSpec(shape, lambda l: (0,) * len(shape))


def inner_strain(disp, yh):
    loads, comps, own_x, rows, size_z = disp.shape
    return pl.pallas_call(
        inner_kernel,
        grid=(loads,),
        out_shape=(
            jax.ShapeDtypeStruct((own_x - 3, rows, size_z), jnp.float32),
            jax.ShapeDtypeStruct((loads, comps, 3, 3, rows, size_z), jnp.float32),
        ),
        in_specs=[load_block(comps, own_x, rows, size_z), load_block(comps, 3, own_x, size_z)],
        out_specs=(fixed_block(own_x - 3, rows, size_z), load_block(comps, 3, 3, rows, size_z)),
        scratch_shapes=[
            pltpu.VMEM((3, 3, own_x, rows, size_z), jnp.float32),
        ],
        compiler_params=pltpu.CompilerParams(vmem_limit_bytes=54 << 20),
        cost_estimate=pl.CostEstimate(flops=40000 * 4096, bytes_accessed=1 << 20, transcendentals=0),
    )(disp, yh)


def strain_message(place, tail, beyond, inner, solid, parts):
    loads, comps = tail.shape[:2]
    own_x, rows, blocks = solid.shape
    size_z = beyond.shape[1]
    return pl.pallas_call(
        outer_kernel,
        grid=(loads,),
        out_shape=jax.ShapeDtypeStruct((parts * 88, 128), jnp.float32),
        in_specs=[
            pl.BlockSpec(memory_space=pltpu.SMEM),
            load_block(comps, 3, 3, rows, size_z),
            fixed_block(*beyond.shape),
            fixed_block(own_x - 3, rows, size_z),
            fixed_block(own_x, rows, blocks),
        ],
        out_specs=fixed_block(parts * 88, 128),
        scratch_shapes=[
            pltpu.VMEM((3, 3, 3, rows, size_z), jnp.float32),
            pltpu.VMEM((3, rows, size_z), jnp.float32),
            pltpu.VMEM((own_x // 4, size_z + 16, 128), jnp.float32),
        ],
        compiler_params=pltpu.CompilerParams(vmem_limit_bytes=48 << 20),
        cost_estimate=pl.CostEstimate(flops=10000 * 4096, bytes_accessed=1 << 20, transcendentals=0),
    )(place, tail, beyond, inner, solid)


def ring(axis, step):
    count = lax.axis_size(axis)
    return [(i, i + step) for i in range(count) if 0 <= i + step < count]


def newton_reciprocal(x):
    r = pl.reciprocal(x, approx=True)
    return r * (2.0 - x * r)


def weno_cell(d, e0, e1, e2, e3):
    f0 = e1 - e0
    f1 = e2 - e1
    f2 = e3 - e2
    g0 = f1 - f0
    g1 = f2 - f1
    twice1 = e1 + e1
    twice2 = e2 + e2
    third = 13.0 / 3.0
    eps = 4.0 * WENO_EPS
    pa = twice1 + f0
    pb = twice1 + f1
    pc = twice2 - f2
    a = (f0 * f0 * third + eps) + pa * pa
    b = (f1 * f1 * third + eps) + pb * pb
    c = (f2 * f2 * third + eps) + pc * pc
    a = a * a
    b = b * b * (1.0 / 6.0)
    c = c * c
    ac = a * c
    ab = a * b
    cb = c * b
    u = cb * g0
    v = ab * g1
    both = u + v
    both = both + both
    s = e1 + e2
    d6 = 6.0 * d
    minus = d6 + (s + e2) - (both + v) * newton_reciprocal(ac + cb + 3.0 * ab)
    plus = (s + e1) - d6 - (both + u) * newton_reciprocal(ac + ab + 3.0 * cb)
    return minus, plus


def godunov(minus, plus):
    high = jnp.maximum(jnp.maximum(minus, plus), 0.0)
    low = jnp.minimum(jnp.minimum(minus, plus), 0.0)
    return high * high, low * low


def x_terms(phi):
    rows, size = phi.shape
    wide = size + 128
    phi = jnp.concatenate([phi, jnp.ones((rows, 128), jnp.float32)], axis=1)
    d = pltpu.roll(phi, wide - 1, 1) - phi
    e = pltpu.roll(d, wide - 1, 1) - d
    minus, plus = weno_cell(
        d, pltpu.roll(e, 2, 1), pltpu.roll(e, 1, 1), e, pltpu.roll(e, wide - 1, 1)
    )
    return godunov(pltpu.roll(minus, 1, 1)[:, :size], plus[:, :size])


def next_rows(tiles, step, count):
    row = lax.broadcasted_iota(jnp.int32, tiles[0].shape, 0)
    turned = [pltpu.roll(v, 8 - step, 0) for v in tiles]
    last = len(tiles) - 1
    return [jnp.where(row < 8 - step, turned[t], turned[min(t + 1, last)]) for t in range(count)]


def y_stage(phi_ref, layer, span, gp_ref, gm_ref, mid_ref, z, exact):
    tiles = gp_ref.shape[1] // 8
    cells = tiles + 1 if exact else tiles
    count = min(cells + 1, phi_ref.shape[1] // 8)
    phi = [phi_ref[layer, 8 * t : 8 * t + 8, span] for t in range(count)]
    d = [n - p for n, p in zip(next_rows(phi, 1, count), phi)]
    e = [n - p for n, p in zip(next_rows(d, 1, count), d)]
    d2 = next_rows(d, 2, cells)
    e1, e2, e3 = (next_rows(e, k, cells) for k in (1, 2, 3))
    sides = [weno_cell(d2[t], e[t], e1[t], e2[t], e3[t]) for t in range(cells)]
    plus = next_rows([p for _, p in sides], 1, tiles)
    mid = next_rows(phi, 3, tiles)
    for t in range(tiles):
        rows = slice(8 * t, 8 * t + 8)
        gp_ref[z, rows, span], gm_ref[z, rows, span] = godunov(sides[t][0], plus[t])
        mid_ref[z, rows, span] = mid[t]


def xy_stage(phi_ref, layer0, layers, gp_ref, gm_ref, mid_ref, exact=False):
    _, rows, lanes = gp_ref.shape

    def layer_step(z, carry):
        for block in range(lanes // 128):
            y_stage(phi_ref, z + layer0, slice(128 * block, 128 * block + 128), gp_ref, gm_ref, mid_ref, z, exact)
        for t in range(rows // 8):
            xp, xm = x_terms(mid_ref[z, 8 * t : 8 * t + 8, :])
            gp_ref[z, 8 * t : 8 * t + 8, :] += xp
            gm_ref[z, 8 * t : 8 * t + 8, :] += xm
        return carry

    lax.fori_loop(0, layers, layer_step, 0)


def z_stage(get_phi, layers, rows, lanes, finish):
    def lane_step(block, carry):
        span = pl.ds(pl.multiple_of(128 * block, 128), 128)
        for t in range(rows // 8):
            p = [get_phi(z, t, span) for z in range(-3, layers + 3)]
            d = [p[k + 1] - p[k] for k in range(len(p) - 1)]
            e = [d[k + 1] - d[k] for k in range(len(d) - 1)]
            before = None
            for cell in range(layers + 1):
                minus, plus = weno_cell(d[cell + 2], e[cell], e[cell + 1], e[cell + 2], e[cell + 3])
                if before is not None:
                    finish(cell - 1, t, span, p[cell + 2], *godunov(before, plus))
                before = minus
        return carry

    lax.fori_loop(0, lanes // 128, lane_step, 0)


def layer_rows(mid_ref, edges, z, t, span):
    layers = mid_ref.shape[0]
    if z < 0:
        return edges[z + 3, 8 * t : 8 * t + 8, span]
    if z >= layers:
        return edges[z - layers + 3, 8 * t : 8 * t + 8, span]
    return mid_ref[z, 8 * t : 8 * t + 8, span]


def first_gradient_kernel(place_ref, tall_ref, ra_ref, rb_ref, ls_ref, step_ref, edges):
    layers = step_ref.shape[0] // 3
    sp_ref, sm_ref, mid_ref = (step_ref.at[pl.ds(k * layers, layers)] for k in range(3))
    _, rows, lanes = step_ref.shape
    depth, own, _ = tall_ref.shape
    ones = jnp.ones((8, lanes), jnp.float32)

    def copy(z, carry):
        for t in range(ls_ref.shape[1] // 8):
            ls_ref[z, 8 * t : 8 * t + 8, :] = ones
        ls_ref[z, YE : YE + own, :] = tall_ref[z]
        return carry

    lax.fori_loop(0, depth, copy, 0)

    def below(ref):
        @pl.when(place_ref[4] == 0)
        def _():
            for z in range(depth):
                ls_ref[z, YE - 8 : YE, :] = ref[z]
                ls_ref[z, YE - 9 : YE - 8, :] = ref[depth + z // 8, z % 8 : z % 8 + 1, :]

    def above(ref):
        @pl.when(place_ref[5] == 0)
        def _():
            for z in range(depth):
                ls_ref[z, YE + own : YE + own + 8, :] = ref[z]
                ls_ref[z, YE + own + 8 : YE + own + 9, :] = ref[depth + z // 8, z % 8 : z % 8 + 1, :]

    @pl.when(place_ref[3] == 1)
    def _():
        above(ra_ref)
        below(rb_ref)

    @pl.when(place_ref[3] == 0)
    def _():
        below(ra_ref)
        above(rb_ref)

    for k in range(6):
        layer = k if k < 3 else depth - 6 + k
        tiles = [ls_ref[layer, 8 * t : 8 * t + 8, :] for t in range(rows // 8 + 1)]
        for t, value in enumerate(next_rows(tiles, 3, rows // 8)):
            edges[k, 8 * t : 8 * t + 8, :] = value
    xy_stage(ls_ref, 3, layers, sp_ref, sm_ref, mid_ref)

    def finish(z, t, span, phi, gp, gm):
        where = pl.ds(8 * t, 8)
        scale = TIME_STEP / 6.0
        sp_ref[z, where, span] = scale * jnp.sqrt(sp_ref[z, where, span] + gp)
        sm_ref[z, where, span] = scale * jnp.sqrt(sm_ref[z, where, span] + gm)

    z_stage(
        lambda z, t, span: layer_rows(mid_ref, edges, z, t, span), layers, rows, lanes, finish
    )


def vmem_call(kernel, outs, args, scratch=(), cycles=0, limit=8):
    specs = []
    for arg in args:
        space = pltpu.SMEM if arg.dtype == jnp.int32 else pltpu.VMEM
        specs.append(pl.BlockSpec(memory_space=space))
    return pl.pallas_call(
        kernel,
        out_shape=tuple(jax.ShapeDtypeStruct(shape, jnp.float32) for shape in outs),
        in_specs=specs,
        out_specs=tuple(pl.BlockSpec(memory_space=pltpu.VMEM) for _ in outs),
        scratch_shapes=[pltpu.VMEM(shape, jnp.float32) for shape in scratch],
        compiler_params=pltpu.CompilerParams(vmem_limit_bytes=limit << 20),
        cost_estimate=pl.CostEstimate(flops=cycles * 4096, bytes_accessed=1 << 20, transcendentals=0),
    )(*args)


def place_flags():
    wide, narrow = lax.axis_index("wide"), lax.axis_index("narrow")
    flags = [
        1 - wide % 2, wide == 0, wide == lax.axis_size("wide") - 1,
        1 - narrow % 2, narrow == 0, narrow == lax.axis_size("narrow") - 1,
    ]
    return jnp.stack([jnp.asarray(f).astype(jnp.int32) for f in flags])


def y_inside(place_ref, base, first_row, shape, rows):
    row = lax.broadcasted_iota(jnp.int32, shape, 0) + (first_row - base)
    inside = (row >= 0) | (place_ref[4] == 0)
    return inside & ((row < rows) | (place_ref[5] == 0))


def extend_kernel(
    place_ref, tile_ref, ra_ref, rb_ref, pa_ref, pb_ref, pc_ref, po_ref, ls_ref, step_ref,
    speed_ref, speed3_ref, phi_ref, ma_ref, mb_ref, one, two, keep, pull,
):
    depth, rows, lanes = tile_ref.shape
    layers = depth - 2 * HALO
    sp_ref, sm_ref, mid_ref = (step_ref.at[pl.ds(k * layers, layers)] for k in range(3))
    tall = ls_ref.shape[1]
    margin = 8
    base = margin + YE
    peak = jnp.maximum(jnp.maximum(pa_ref[...], pb_ref[...]), jnp.maximum(pc_ref[...], po_ref[...]))
    scale = 1.0 / (peak[0:1, 0:1] + 1e-06)

    def assemble(z, carry):
        one[z, base : base + rows, :] = tile_ref[z]
        return carry

    lax.fori_loop(0, depth, assemble, 0)

    def below(ref):
        for z in range(depth):
            one[z, base - 8 : base, :] = ref[z]
            one[z, base - 10 : base - 8, :] = ref[depth + z // 4, 2 * (z % 4) : 2 * (z % 4) + 2, :]

    def above(ref):
        for z in range(depth):
            one[z, base + rows : base + rows + 8, :] = ref[z]
            one[z, base + rows + 8 : base + rows + 10, :] = ref[depth + z // 4, 2 * (z % 4) : 2 * (z % 4) + 2, :]

    @pl.when(place_ref[3] == 1)
    def _():
        above(ra_ref)
        below(rb_ref)

    @pl.when(place_ref[3] == 0)
    def _():
        below(ra_ref)
        above(rb_ref)

    def inside(z, first_row):
        outside = ((z < HALO) & (place_ref[1] == 1)) | ((z >= depth - HALO) & (place_ref[2] == 1))
        return y_inside(place_ref, YE, first_row, (8, lanes), rows) & jnp.logical_not(outside)

    def normalise(z, carry):
        for t in range(-1, tall // 8):
            at = slice(margin + 8 * t, margin + 8 * t + 8)
            one[z, at, :] = jnp.where(inside(z, 8 * t), one[z, at, :] * scale - 0.5, 0.0)
        return carry

    def weigh(z, carry):
        for t in range(tall // 8):
            span = slice(8 * t, 8 * t + 8)
            ls = ls_ref[z - 1, span, :]
            weight = newton_reciprocal(1.0 + 4.0 * ls * ls)
            keep[z, span, :] = weight * one[z, margin + 8 * t : margin + 8 * t + 8, :]
            pull[z, span, :] = jnp.where(inside(z, 8 * t), (1.0 - weight) * (1.0 / 6.0), 0.0)
        return carry

    lax.fori_loop(0, depth, normalise, 0)
    lax.fori_loop(1, depth - 1, weigh, 0)
    rows_of = [-(-(YE + rows + YE - k) // 8) * 8 for k in range(EXT_PASSES)]
    for step in range(EXT_PASSES):
        source, target = (one, two) if step % 2 == 0 else (two, one)

        def extend(z, carry):
            count = rows_of[step] // 8
            tiles = [source[z, 8 * t : 8 * t + 8, :] for t in range(count + 2)]
            row = lax.broadcasted_iota(jnp.int32, tiles[0].shape, 0)
            lane = lax.broadcasted_iota(jnp.int32, tiles[0].shape, 1)
            down = [pltpu.roll(v, 1, 0) for v in tiles[:-1]]
            up = [pltpu.roll(v, 7, 0) for v in tiles[1:]]
            for t in range(count):
                at = margin + 8 * t
                centre = tiles[t + 1]
                total = source[z - 1, at : at + 8, :] + source[z + 1, at : at + 8, :]
                total = total + jnp.where(row == 0, down[t], down[t + 1])
                total = total + jnp.where(row == 7, up[t + 1], up[t])
                total = total + jnp.where(lane == 0, 0.0, pltpu.roll(centre, 1, 1))
                total = total + jnp.where(lane == lanes - 1, 0.0, pltpu.roll(centre, lanes - 1, 1))
                span = slice(8 * t, 8 * t + 8)
                target[z, at : at + 8, :] = keep[z, span, :] + pull[z, span, :] * total
            return carry

        lax.fori_loop(step + 1, depth - 1 - step, extend, 0)

    final = one if EXT_PASSES % 2 == 0 else two

    def march(z, carry):
        count = tall // 8
        tiles = [final[z + HALO, margin + 8 * t : margin + 8 * t + 8, :] for t in range(count)]
        moved = next_rows(tiles, YE - Y1, count - 1)
        for t in range(count - 1):
            span = slice(8 * t, 8 * t + 8)
            speed = moved[t]
            change = jnp.maximum(speed, 0.0) * sp_ref[z, span, :] + jnp.minimum(speed, 0.0) * sm_ref[z, span, :]
            phi = mid_ref[z, span, :] - change
            phi_ref[z, span, :] = jnp.where(y_inside(place_ref, Y1, 8 * t, phi.shape, rows), phi, 1.0)
        for t, value in enumerate(next_rows(tiles, YE - Y2, speed3_ref.shape[1] // 8)):
            speed3_ref[z, 8 * t : 8 * t + 8, :] = value
        for t, value in enumerate(next_rows(tiles[1:], YE - 8, rows // 8)):
            speed_ref[z, 8 * t : 8 * t + 8, :] = value
        return carry

    lax.fori_loop(0, layers, march, 0)
    send_edges(place_ref, phi_ref, Y1 - Y2, ma_ref, mb_ref)


def send_edges(place_ref, phi_ref, offset, ma_ref, mb_ref):
    layers = phi_ref.shape[0]
    count = ma_ref.shape[1]
    upper = place_ref[0] * (layers - 3)
    lower = (1 - place_ref[0]) * (layers - 3)
    for k in range(3):
        ma_ref[k] = phi_ref[upper + k, offset : offset + count, :]
        mb_ref[k] = phi_ref[lower + k, offset : offset + count, :]


def take_edges(place_ref, ra_ref, rb_ref, edges):
    upper = 3 * place_ref[0]
    lower = 3 - upper
    for k in range(3):
        edges[upper + k] = ra_ref[k]
        edges[lower + k] = rb_ref[k]

    @pl.when(place_ref[1] == 1)
    def _():
        edges[0:3] = jnp.ones((3,) + tuple(edges.shape[1:]), jnp.float32)

    @pl.when(place_ref[2] == 1)
    def _():
        edges[3:6] = jnp.ones((3,) + tuple(edges.shape[1:]), jnp.float32)


def plane_kernel(exact, phi_ref, gp_ref, gm_ref, mid_ref):
    xy_stage(phi_ref, 0, gp_ref.shape[0], gp_ref, gm_ref, mid_ref, exact)


def finish_kernel(
    rows, place_ref, phi_ref, ra_ref, rb_ref, gp_ref, gm_ref, speed_ref, *rest
):
    out_ref, edges = rest[0], rest[-1]
    layers, count, lanes = out_ref.shape
    base = Y2 if count > rows else 0
    take_edges(place_ref, ra_ref, rb_ref, edges)
    get_phi = functools.partial(layer_rows, phi_ref, edges)

    def finish(z, t, span, phi, gp, gm):
        where = pl.ds(8 * t, 8)
        speed = speed_ref[z, where, span]
        total = jnp.where(speed > 0.0, gp_ref[z, where, span] + gp, gm_ref[z, where, span] + gm)
        phi = phi - (TIME_STEP / 6.0) * speed * jnp.sqrt(total)
        if count > rows:
            phi = jnp.where(y_inside(place_ref, base, 8 * t, phi.shape, rows), phi, 1.0)
        out_ref[z, where, span] = phi

    z_stage(get_phi, layers, count, lanes, finish)
    if len(rest) > 2:
        send_edges(place_ref, out_ref, Y2, rest[1], rest[2])


def swaps(axis):
    count = lax.axis_size(axis)
    first, second = [], []
    for i in range(0, count, 2):
        first += [(i, i + 1), (i + 1, i)]
        if i + 2 < count:
            second += [(i + 1, i + 2), (i + 2, i + 1)]
    return first, second


def stack_kernel(place_ref, ls_ref, ra_ref, rb_ref, tall_ref, ma_ref, mb_ref, edges):
    layers, rows = ls_ref.shape[:2]
    take_edges(place_ref, ra_ref, rb_ref, edges)
    for k in range(3):
        tall_ref[k] = edges[k]
        tall_ref[layers + 3 + k] = edges[3 + k]

    def copy(z, carry):
        tall_ref[z + 3] = ls_ref[z]
        return carry

    lax.fori_loop(0, layers, copy, 0)
    depth = layers + 6

    def upper(ref):
        for z in range(depth):
            ref[z] = tall_ref[z, rows - 8 : rows, :]
            ref[depth + z // 8, z % 8 : z % 8 + 1, :] = tall_ref[z, rows - 9 : rows - 8, :]

    def lower(ref):
        for z in range(depth):
            ref[z] = tall_ref[z, 0:8, :]
            ref[depth + z // 8, z % 8 : z % 8 + 1, :] = tall_ref[z, 8:9, :]

    @pl.when(place_ref[3] == 1)
    def _():
        upper(ma_ref)
        lower(mb_ref)

    @pl.when(place_ref[3] == 0)
    def _():
        lower(ma_ref)
        upper(mb_ref)


def level_part(place, tile, ma, mb, wide_peak, level_set, ls, step):
    layers, rows, lanes = level_set.shape
    nfirst, nsecond = swaps("narrow")
    wfirst, wsecond = swaps("wide")
    count = lax.axis_size("narrow")
    across = [(i, (i + count // 2) % count) for i in range(count)]
    mirror = [(i, count - 1 - i) for i in range(count)]
    ra = lax.ppermute(ma, "narrow", nfirst)
    rb = lax.ppermute(mb, "narrow", nsecond)
    pc = lax.ppermute(wide_peak, "narrow", across)
    pb = lax.ppermute(wide_peak, "narrow", mirror)
    pa = ra[-1, :, :128]
    tall = ls.shape[1]
    rows1 = -(-(rows + 2 * Y1) // 8) * 8
    rows2 = -(-(rows + 2 * Y2) // 8) * 8
    depth = layers + 2 * HALO
    speed, speed3, phi, sa, sb = vmem_call(
        extend_kernel,
        [(layers, rows, lanes), (layers, rows2, lanes), (layers, rows1, lanes), (3, rows2, lanes), (3, rows2, lanes)],
        (place, tile, ra, rb, pa, pb, pc, wide_peak, ls, step),
        [(depth, tall + 16, lanes)] * 2 + [(depth, tall, lanes)] * 2,
        8000,
        16,
    )
    ga = lax.ppermute(sa, "wide", wfirst)
    gb = lax.ppermute(sb, "wide", wsecond)
    gp, gm, mid = vmem_call(functools.partial(plane_kernel, False), [(layers, rows2, lanes)] * 3, (phi,), (), 12000)
    phi, sa, sb = vmem_call(
        functools.partial(finish_kernel, rows),
        [(layers, rows2, lanes), (3, rows, lanes), (3, rows, lanes)],
        (place, mid, ga, gb, gp, gm, speed3),
        [(6, rows2, lanes)],
        5000,
    )
    ga = lax.ppermute(sa, "wide", wfirst)
    gb = lax.ppermute(sb, "wide", wsecond)
    gp, gm, mid = vmem_call(functools.partial(plane_kernel, True), [(layers, rows, lanes)] * 3, (phi,), (), 12000)
    (phi,) = vmem_call(
        functools.partial(finish_kernel, rows),
        [(layers, rows, lanes)],
        (place, mid, ga, gb, gp, gm, speed),
        [(6, rows, lanes)],
        5000,
    )
    return phi, speed


def first_gradient(place, tall, ra, rb):
    depth, rows, lanes = tall.shape
    rows1 = -(-(rows + 2 * Y1) // 8) * 8
    total = -(-(rows + 2 * YE) // 8) * 8
    return vmem_call(
        first_gradient_kernel, [(depth, total, lanes), (3 * (depth - 6), rows1, lanes)], (place, tall, ra, rb),
        [(6, rows1, lanes)], 35000, 54
    )


def stack_level(place, level_set, ra, rb):
    layers, rows, lanes = level_set.shape
    depth = layers + 6
    edge = (depth + -(-depth // 8), 8, lanes)
    return vmem_call(
        stack_kernel, [(depth, rows, lanes), edge, edge], (place, level_set, ra, rb), [(6, rows, lanes)], 1500
    )


def unpack_kernel(place_ref, recv_ref, tile_ref, peak_ref, ma_ref, mb_ref):
    parts = recv_ref.shape[0]
    depth, rows, lanes = tile_ref.shape
    for j in range(depth // 4):
        block = recv_ref[:, 16 * j : 16 * j + 16, :].reshape(parts * 16, 128)
        wide = pltpu.roll(block.T, 1, 1)
        for k in range(4):
            tile_ref[4 * j + k] = wide[rows * k : rows * (k + 1), :]
    peak = recv_ref[0, 80:88, :]
    for s in range(1, parts):
        peak = jnp.maximum(peak, recv_ref[s, 80:88, :])
    peak_ref[...] = peak
    fill_edges(place_ref, tile_ref, peak, ma_ref, mb_ref)


def fill_edges(place_ref, tile_ref, peak, ma_ref, mb_ref):
    depth, rows, lanes = tile_ref.shape

    def upper(ref):
        for z in range(depth):
            ref[z] = tile_ref[z, rows - 8 : rows, :]
            ref[depth + z // 4, 2 * (z % 4) : 2 * (z % 4) + 2, :] = tile_ref[z, rows - 10 : rows - 8, :]

    def lower(ref):
        for z in range(depth):
            ref[z] = tile_ref[z, 0:8, :]
            ref[depth + z // 4, 2 * (z % 4) : 2 * (z % 4) + 2, :] = tile_ref[z, 8:10, :]

    last = ma_ref.shape[0] - 1
    ma_ref[last, :, 0:128] = peak
    mb_ref[last, :, 0:128] = peak

    @pl.when(place_ref[3] == 1)
    def _():
        upper(ma_ref)
        lower(mb_ref)

    @pl.when(place_ref[3] == 0)
    def _():
        lower(ma_ref)
        upper(mb_ref)


def unpack(place, recv, own_z, rows):
    parts = recv.shape[0]
    lanes = parts * 16
    depth = own_z + 2 * HALO
    edge = (depth + depth // 4 + 1, 8, lanes)
    return vmem_call(
        unpack_kernel, [(depth, rows, lanes), (8, 128), edge, edge], (place, recv), (), 1500
    )


def per_device(displacement, material, level_set):
    wide = lax.axis_size("wide")
    loads, comps, own_x, rows, size_z = displacement.shape
    own_z, _, size_x = level_set.shape
    place = place_flags()
    backward = [(i, (i - 1) % wide) for i in range(wide)]
    wfirst, wsecond = swaps("wide")
    nfirst, nsecond = swaps("narrow")

    low = lax.ppermute(displacement[:, :, :, -1], "narrow", ring("narrow", 1))
    high = lax.ppermute(
        jnp.stack([displacement[:, :, :, 0], displacement[:, :, :, 1]], axis=2), "narrow", ring("narrow", -1)
    )
    yh = jnp.concatenate([low[:, :, None], high], axis=2)
    bounds = level_set[:3], level_set[own_z - 3 :]
    even = place[0] == 1
    la = lax.ppermute(jnp.where(even, bounds[1], bounds[0]), "wide", wfirst)
    lb = lax.ppermute(jnp.where(even, bounds[0], bounds[1]), "wide", wsecond)

    stiff = 0.2 + 0.8 * jnp.repeat(material[0].astype(jnp.float32), BZ, axis=1)
    layers, yh, la, lb = lax.optimization_barrier((displacement[:, :, :3], yh, la, lb))
    flat = [layers.reshape(-1, size_z), stiff, yh[:, :, :, :3].reshape(-1, size_z)]
    flat.append(jnp.zeros((-sum(f.shape[0] for f in flat) % 8, size_z), jnp.float32))
    beyond = lax.ppermute(jnp.concatenate(flat, axis=0), "wide", backward)
    inner, tail = inner_strain(displacement, yh)
    la, lb, inner = lax.optimization_barrier((la, lb, inner))
    tall, ya, yb = stack_level(place, level_set, la, lb)
    ya = lax.ppermute(ya, "narrow", nfirst)
    yb = lax.ppermute(yb, "narrow", nsecond)
    beyond, ya, yb = lax.optimization_barrier((beyond, ya, yb))
    message = strain_message(place, tail, beyond, inner, material, wide)
    message, tall = lax.optimization_barrier((message, tall))
    recv = lax.all_to_all(message.reshape(wide, 88, 128), "wide", split_axis=0, concat_axis=0, tiled=True)
    ls, step = first_gradient(place, tall, ya, yb)
    recv, step = lax.optimization_barrier((recv, step))
    tile, wide_peak, ma, mb = unpack(place, recv, own_z, rows)
    return level_part(place, tile, ma, mb, wide_peak, level_set, ls, step)


def solution(mesh):
    return jax.shard_map(
        per_device,
        mesh=mesh,
        in_specs=(
            P(None, None, "wide", "narrow", None),
            P("wide", "narrow", None),
            P("wide", "narrow", None),
        ),
        out_specs=(P("wide", "narrow", None), P("wide", "narrow", None)),
        check_vma=False,
    )
```
